32 devices in a mesh: shard: 4 (over y, x), seq: 8 (over z, core).
Axes of the slice: x: 2, y: 2, z: 4, core: 2. Of those that a mesh axis runs over, the one named last changes fastest.
Arguments:
- layer_input: bfloat16 [4096, 2048], P(('shard', 'seq')), may hold values from -6 to 6
- doc_lengths: int32 [16], replicated, may hold values from 1 to 3640, as said below
- norm_gain: bfloat16 [2048], P(('shard', 'seq')), may hold values from 0.5 to 1.5
- query_weight: bfloat16 [2048, 2048], P(('shard', 'seq')), may hold values from -0.125 to 0.125
- key_weight: bfloat16 [2048, 2048], P(('shard', 'seq')), may hold values from -0.125 to 0.125
- value_weight: bfloat16 [2048, 2048], P(('shard', 'seq')), may hold values from -0.125 to 0.125
- output_weight: bfloat16 [2048, 2048], P(('shard', 'seq')), may hold values from -6 to 6
- feed_gain: bfloat16 [2048], P(('shard', 'seq')), may hold values from 0.5 to 1.5
- gate_weight: bfloat16 [8192, 2048], P(('shard', 'seq')), may hold values from -0.125 to 0.125
- up_weight: bfloat16 [8192, 2048], P(('shard', 'seq')), may hold values from -0.125 to 0.125
- down_weight: bfloat16 [8192, 2048], P(('shard', 'seq')), may hold values from -0.0625 to 0.0625
- output_grad: bfloat16 [4096, 2048], P(('shard', 'seq')), may hold values from -6 to 6
Outputs:
- layer_output: bfloat16 [4096, 2048], P(('shard', 'seq'))
- input_grad: bfloat16 [4096, 2048], P(('shard', 'seq'))
- norm_gain_grad: float32 [2048], P(('shard', 'seq'))
- query_weight_grad: float32 [2048, 2048], P(('shard', 'seq'))
- key_weight_grad: float32 [2048, 2048], P(('shard', 'seq'))
- value_weight_grad: float32 [2048, 2048], P(('shard', 'seq'))
- output_weight_grad: float32 [2048, 2048], P(('shard', 'seq'))
- feed_gain_grad: float32 [2048], P(('shard', 'seq'))
- gate_weight_grad: float32 [8192, 2048], P(('shard', 'seq'))
- up_weight_grad: float32 [8192, 2048], P(('shard', 'seq'))
- down_weight_grad: float32 [8192, 2048], P(('shard', 'seq'))
The draws below stay inside these ranges and needn't reach their ends.
Inputs may be any that keep to these rules, and one draw needn't show every extreme that they name: `doc_lengths`: the lengths add up to 4096. One document, neither the first nor the last, has the largest length; it begins within the first 1024 positions of the stream and ends within the last 1024.
All inputs are finite; a program needn't handle non-finite values.
Results may differ from the reference program's by a relative error of at most 0.014.
Values may be sent and summed in bfloat16 or wider, within the bound.
No kernel may reach another device: no remote copies, remote signals or barrier semaphores. Data moves between devices by JAX's collectives and lax.ppermute only.
A program may use at most 704 MiB of HBM per device.

```python
import math
import jax
import jax.numpy as jnp
from jax import lax

D = 2048
HEADS = 32
HEAD_DIM = 64
FF = 8192
NDOC = 16
SPAN = 1024
STREAM = 4096


def draw_doc_lengths(key, part):
    key = jax.random.fold_in(key, 11)
    pick_key, order_key = jax.random.split(key)
    short_most = SPAN // NDOC
    short_places = jnp.arange(NDOC - 1, dtype=jnp.int32)
    shorts = jnp.where(short_places % 2 == 0, 1, short_most).astype(jnp.int32)
    shorts = jax.random.permutation(order_key, shorts)
    long_len = STREAM - NDOC // 2 - (NDOC - 1) // 2 * short_most
    long_index = jax.random.randint(pick_key, (), 1, NDOC - 1)
    places = jnp.arange(NDOC, dtype=jnp.int32)
    source = jnp.clip(jnp.where(places < long_index, places, places - 1), 0, NDOC - 2)
    picked = jnp.take(shorts, source)
    return jnp.where(places == long_index, long_len, picked).astype(jnp.int32)


def block_levels(own_key, extent, cuts, least, high):
    factor_of = 1.0
    for position, blocks in cuts:
        steps = jax.random.uniform(jax.random.fold_in(jax.random.fold_in(own_key, 6), position), (blocks,), jnp.float32, least / len(cuts), high / len(cuts))
        factor_of = factor_of * jnp.repeat(jnp.exp(steps), extent[position] // blocks).reshape((-1,) + (1,) * (len(extent) - 1 - position))
    return factor_of


def scatter_about(key, shape, scale, limit, cuts=(), kind=jnp.bfloat16):
    result = scale * jax.random.normal(key, shape, jnp.float32)
    if cuts:
        result = result * block_levels(key, shape, cuts, -0.22, 0.18)
    return jnp.clip(result, -limit, limit).astype(kind)


def setup_inputs(seed: int = 0) -> dict:
    key_of = jax.random.split(jax.random.key(seed), 13)
    layer_input = scatter_about(key_of[0], (STREAM, D), 1.0, 6.0, ((0, 32),))
    doc_lengths = draw_doc_lengths(jax.random.fold_in(key_of[12], 71), 0)
    norm_gain = jnp.clip(1.0 + 0.1 * jax.random.normal(key_of[2], (D,), jnp.float32), 0.5, 1.5).astype(jnp.bfloat16)
    query_weight = scatter_about(key_of[3], (D, D), D ** -0.5, 0.125, ((0, 32),))
    key_weight = scatter_about(key_of[4], (D, D), D ** -0.5, 0.125, ((0, 32),))
    value_weight = scatter_about(key_of[5], (D, D), D ** -0.5, 0.125, ((0, 32),))
    output_weight = scatter_about(key_of[6], (D, D), (SPAN ** 0.5 * D ** -0.5), 6.0, ((0, 32),))
    feed_gain = jnp.clip(1.0 + 0.1 * jax.random.normal(key_of[7], (D,), jnp.float32), 0.5, 1.5).astype(jnp.bfloat16)
    gate_weight = scatter_about(key_of[8], (FF, D), D ** -0.5, 0.125, ((0, 32),))
    up_weight = scatter_about(key_of[9], (FF, D), D ** -0.5, 0.125, ((0, 32),))
    down_weight = scatter_about(key_of[10], (FF, D), FF ** -0.5, 0.0625, ((0, 32),))
    output_grad = scatter_about(key_of[11], (STREAM, D), 1.0, 6.0, ((0, 32),))
    return dict(layer_input=layer_input, doc_lengths=doc_lengths, norm_gain=norm_gain, query_weight=query_weight, key_weight=key_weight, value_weight=value_weight, output_weight=output_weight, feed_gain=feed_gain, gate_weight=gate_weight, up_weight=up_weight, down_weight=down_weight, output_grad=output_grad)


@jax.custom_vjp
def low(v):
    return lax.optimization_barrier(v.astype(jnp.bfloat16)).astype(jnp.float32)

@jax.custom_vjp
def low_back(v):
    return v

def low_keep(v):
    return (low(v), None)

def low_pass(kept, grad):
    return (grad,)

def back_keep(v):
    return (v, None)

def back_low(kept, grad):
    return (low(grad),)
low.defvjp(low_keep, low_pass)
low_back.defvjp(back_keep, back_low)
NORM_EPS = 1e-05
ROPE_BASE = 130000.0
HIGHEST = lax.Precision.HIGHEST

def rope_tables(positions, width):
    half_width = width // 2
    exponent = -2.0 * jnp.arange(half_width, dtype=jnp.float32) / width
    inverse = jnp.power(jnp.float32(ROPE_BASE), exponent)
    angles = positions.astype(jnp.float32)[:, None] * inverse[None, :]
    return (jnp.cos(angles), jnp.sin(angles))

def rotate(values, cos_table, sin_table):
    half_width = values.shape[-1] // 2
    front = values[..., :half_width]
    back_half = values[..., half_width:]
    cos_wide = cos_table[:, None, :]
    sin_wide = sin_table[:, None, :]
    return jnp.concatenate([front * cos_wide - back_half * sin_wide, back_half * cos_wide + front * sin_wide], axis=-1)

def normalize(values, gain_vec):
    scale_row = lax.rsqrt(lax.optimization_barrier(jnp.mean(values * values, axis=-1, keepdims=True)) + NORM_EPS)
    return values * scale_row * gain_vec

def attention_ref(query_rot, key_rot, value_all, positions, doc_ids):
    stream_len = positions.shape[0]
    block_len = math.gcd(stream_len, 256)
    block_count = stream_len // block_len
    score_scale = HEAD_DIM ** (-0.5)

    def one_block(pieces):
        query_blk, query_pos, query_doc = pieces
        scores = low_back(jnp.einsum('qhd,khd->hqk', query_blk, key_rot, precision=HIGHEST) * score_scale)
        allowed = (positions[None, :] <= query_pos[:, None]) & (doc_ids[None, :] == query_doc[:, None])
        scores = jnp.where(allowed[None], scores, -jnp.inf)
        log_total = jax.nn.logsumexp(scores, axis=-1, keepdims=True)
        probs = low(jnp.exp(scores - log_total))
        return jnp.einsum('hqk,khd->qhd', probs, value_all, precision=HIGHEST)
    outputs = lax.map(jax.checkpoint(one_block), (query_rot.reshape(block_count, block_len, HEADS, HEAD_DIM), positions.reshape(block_count, block_len), doc_ids.reshape(block_count, block_len)))
    return outputs.reshape(stream_len, HEADS * HEAD_DIM)

def reference(layer_input, doc_lengths, norm_gain, query_weight, key_weight, value_weight, output_weight, feed_gain, gate_weight, up_weight, down_weight, output_grad):
    positions = jnp.arange(STREAM, dtype=jnp.int32)
    doc_ends = jnp.cumsum(doc_lengths).astype(jnp.int32)
    doc_ids = lax.optimization_barrier(jnp.sum((doc_ends[:, None] <= positions[None, :]).astype(jnp.int32), axis=0)).astype(jnp.int32)
    cos_table, sin_table = rope_tables(positions, HEAD_DIM)

    def forward(inputs, gain_one, query_w, key_w, value_w, out_w, gain_two, gate_w, up_w, down_w):
        normed = low(normalize(inputs, gain_one))
        query_proj = low_back(jnp.dot(normed, query_w, precision=HIGHEST))
        key_proj = low_back(jnp.dot(normed, key_w, precision=HIGHEST))
        value_low = low_back(low(jnp.dot(normed, value_w, precision=HIGHEST)))
        query_rot = low(rotate(query_proj.reshape(STREAM, HEADS, HEAD_DIM), cos_table, sin_table))
        key_rot = low(rotate(key_proj.reshape(STREAM, HEADS, HEAD_DIM), cos_table, sin_table))
        attended = attention_ref(query_rot, key_rot, value_low.reshape(STREAM, HEADS, HEAD_DIM), positions, doc_ids)
        attended = low_back(low(attended))
        middle = inputs + low_back(jnp.dot(attended, out_w, precision=HIGHEST))
        normed_two = low(normalize(middle, gain_two))
        gate_val = low_back(jnp.dot(normed_two, gate_w.T, precision=HIGHEST))
        up_val = low_back(jnp.dot(normed_two, up_w.T, precision=HIGHEST))
        hidden = low(jax.nn.silu(gate_val) * up_val)
        return middle + jnp.dot(hidden, down_w, precision=HIGHEST)
    output, pullback = jax.vjp(forward, layer_input.astype(jnp.float32), norm_gain.astype(jnp.float32), query_weight.astype(jnp.float32), key_weight.astype(jnp.float32), value_weight.astype(jnp.float32), output_weight.astype(jnp.float32), feed_gain.astype(jnp.float32), gate_weight.astype(jnp.float32), up_weight.astype(jnp.float32), down_weight.astype(jnp.float32))
    gradients = pullback(output_grad.astype(jnp.float32))
    return (output.astype(jnp.bfloat16), gradients[0].astype(jnp.bfloat16), gradients[1], gradients[2], gradients[3], gradients[4], gradients[5], gradients[6], gradients[7], gradients[8], gradients[9])
```

```python
import functools
import math

import jax
import jax.numpy as jnp
from jax import lax
from jax.experimental import pallas as pl
from jax.experimental.pallas import tpu as pltpu
from jax.sharding import PartitionSpec as P

HEAD_DIM = 64


NORM_EPS = 1e-05
ROPE_BASE = 130000.0


def rope_tables(positions, width):
    half_width = width // 2
    exponent = -2.0 * jnp.arange(half_width, dtype=jnp.float32) / width
    inverse = jnp.power(jnp.float32(ROPE_BASE), exponent)
    angles = positions.astype(jnp.float32)[:, None] * inverse[None, :]
    return (jnp.cos(angles), jnp.sin(angles))


def rotate(values, cos_table, sin_table):
    half_width = values.shape[-1] // 2
    front = values[..., :half_width]
    back_half = values[..., half_width:]
    cos_wide = cos_table[:, None, :]
    sin_wide = sin_table[:, None, :]
    return jnp.concatenate(
        [front * cos_wide - back_half * sin_wide, back_half * cos_wide + front * sin_wide], axis=-1
    )


def unrotate(values, cos_table, sin_table):
    half_width = values.shape[-1] // 2
    front = values[..., :half_width]
    back_half = values[..., half_width:]
    cos_wide = cos_table[:, None, :]
    sin_wide = sin_table[:, None, :]
    return jnp.concatenate(
        [front * cos_wide + back_half * sin_wide, back_half * cos_wide - front * sin_wide], axis=-1
    )


def doc_numbers(doc_lengths, positions):
    doc_ends = jnp.cumsum(doc_lengths)
    return jnp.sum((doc_ends[:, None] <= positions[None, :]).astype(jnp.int32), axis=0)


def normalize(values, gain_vec):
    scale_row = lax.rsqrt(jnp.mean(values * values, axis=-1, keepdims=True) + NORM_EPS)
    return (values * scale_row * gain_vec, scale_row)


def norm_back(grad_in, values, scale_row, gain_vec):
    unit_rows = values * scale_row
    gain_grad = jnp.sum(grad_in * unit_rows, axis=0)
    unit_grad = grad_in * gain_vec
    value_grad = scale_row * (
        unit_grad - unit_rows * jnp.mean(unit_grad * unit_rows, axis=-1, keepdims=True)
    )
    return (value_grad, gain_grad)


def times_trans(lhs_mat, rhs_mat):
    return lax.dot_general(
        lhs_mat, rhs_mat, (((1,), (1,)), ((), ())), preferred_element_type=jnp.float32
    )


def trans_times(lhs_mat, rhs_mat):
    return lax.dot_general(
        lhs_mat, rhs_mat, (((0,), (0,)), ((), ())), preferred_element_type=jnp.float32
    )


def per_device_any(
    layer_input,
    doc_lengths,
    norm_gain,
    query_weight,
    key_weight,
    value_weight,
    output_weight,
    feed_gain,
    gate_weight,
    up_weight,
    down_weight,
    output_grad,
):
    tok_rows = layer_input.shape[0]
    width = layer_input.shape[1]
    seq_count = lax.axis_size("seq")
    shard_count = lax.axis_size("shard")
    span_len = tok_rows * seq_count
    stream_len = span_len * shard_count
    span_start = lax.axis_index("shard") * span_len
    own_positions = (
        span_start + lax.axis_index("seq") * tok_rows + jnp.arange(tok_rows, dtype=jnp.int32)
    )
    span_positions = span_start + jnp.arange(span_len, dtype=jnp.int32)
    all_positions = jnp.arange(stream_len, dtype=jnp.int32)
    key_docs = doc_numbers(doc_lengths, all_positions)
    query_docs = lax.dynamic_slice_in_dim(key_docs, span_start, span_len)
    score_scale = HEAD_DIM ** (-0.5)
    gathered = (
        lax.all_gather(query_weight, ("shard", "seq"), axis=0, tiled=True),
        lax.all_gather(key_weight, ("shard", "seq"), axis=0, tiled=True),
        lax.all_gather(value_weight, ("shard", "seq"), axis=0, tiled=True),
        lax.all_gather(output_weight, ("shard", "seq"), axis=0, tiled=True),
        lax.all_gather(norm_gain, ("shard", "seq"), axis=0, tiled=True),
        lax.all_gather(feed_gain, ("shard", "seq"), axis=0, tiled=True),
    )
    query_full, key_full, value_full, output_full = (
        gathered[0],
        gathered[1],
        gathered[2],
        gathered[3],
    )
    gain_one = gathered[4].astype(jnp.float32)
    gain_two = gathered[5].astype(jnp.float32)
    inputs = layer_input.astype(jnp.float32)
    normed, scale_one = normalize(inputs, gain_one)
    normed_low = normed.astype(jnp.bfloat16)
    own_cos, own_sin = rope_tables(own_positions, HEAD_DIM)
    query_proj = jnp.dot(normed_low, query_full, preferred_element_type=jnp.float32)
    key_proj = jnp.dot(normed_low, key_full, preferred_element_type=jnp.float32)
    value_proj = jnp.dot(normed_low, value_full, preferred_element_type=jnp.float32)
    query_rot = rotate(query_proj.reshape(tok_rows, -1, HEAD_DIM), own_cos, own_sin).reshape(
        tok_rows, width
    )
    key_rot = rotate(key_proj.reshape(tok_rows, -1, HEAD_DIM), own_cos, own_sin).reshape(
        tok_rows, width
    )
    stacked = jnp.stack(
        [
            query_rot.astype(jnp.bfloat16),
            key_rot.astype(jnp.bfloat16),
            value_proj.astype(jnp.bfloat16),
        ]
    )
    head_triple = lax.all_to_all(stacked, "seq", split_axis=2, concat_axis=1, tiled=True)
    head_width = head_triple.shape[2]
    heads_dev = head_width // HEAD_DIM
    head_query = head_triple[0].reshape(span_len, heads_dev, HEAD_DIM)
    key_value = lax.all_gather(head_triple[1:], "shard", axis=1, tiled=True)
    key_block = math.gcd(stream_len, max(512, stream_len // 16))
    block_count = stream_len // key_block
    key_blocks = key_value[0].reshape(block_count, key_block, heads_dev, HEAD_DIM)
    value_blocks = key_value[1].reshape(block_count, key_block, heads_dev, HEAD_DIM)
    pos_blocks = all_positions.reshape(block_count, key_block)
    doc_blocks = key_docs.reshape(block_count, key_block)

    def block_scores(key_blk, key_pos, key_doc):
        scores = (
            jnp.einsum("qhd,khd->hqk", head_query, key_blk, preferred_element_type=jnp.float32)
            * score_scale
        )
        allowed = (key_pos[None, :] <= span_positions[:, None]) & (
            key_doc[None, :] == query_docs[:, None]
        )
        return jnp.where(allowed[None], scores, -jnp.inf)

    def total_step(state_pair, pieces):
        run_max, run_sum = state_pair
        scores = block_scores(pieces[0], pieces[1], pieces[2])
        new_max = jnp.maximum(run_max, jnp.max(scores, axis=-1))
        new_sum = run_sum * jnp.exp(run_max - new_max) + jnp.sum(
            jnp.exp(scores - new_max[..., None]), axis=-1
        )
        return ((new_max, new_sum), None)

    start_max = jnp.full((heads_dev, span_len), -1e30, jnp.float32)
    start_sum = jnp.zeros((heads_dev, span_len), jnp.float32)
    totals, unused = lax.scan(
        total_step, (start_max, start_sum), (key_blocks, pos_blocks, doc_blocks)
    )
    log_total = totals[0] + jnp.log(totals[1])

    def output_step(accum, pieces):
        scores = block_scores(pieces[0], pieces[2], pieces[3])
        probs = jnp.exp(scores - log_total[..., None]).astype(jnp.bfloat16)
        return (
            accum
            + jnp.einsum("hqk,khd->qhd", probs, pieces[1], preferred_element_type=jnp.float32),
            None,
        )

    start_acc = jnp.zeros((span_len, heads_dev, HEAD_DIM), jnp.float32)
    head_out32, unused = lax.scan(
        output_step, start_acc, (key_blocks, value_blocks, pos_blocks, doc_blocks)
    )
    head_out = head_out32.reshape(span_len, head_width).astype(jnp.bfloat16)
    token_out = lax.all_to_all(head_out, "seq", split_axis=0, concat_axis=1, tiled=True)
    middle = inputs + jnp.dot(token_out, output_full, preferred_element_type=jnp.float32)
    normed_two, scale_two = normalize(middle, gain_two)
    feed_low = normed_two.astype(jnp.bfloat16)
    feed_mats = (
        lax.all_gather(gate_weight, ("shard", "seq"), axis=0, tiled=True),
        lax.all_gather(up_weight, ("shard", "seq"), axis=0, tiled=True),
        lax.all_gather(down_weight, ("shard", "seq"), axis=0, tiled=True),
    )
    gate_full, up_full, down_full = (feed_mats[0], feed_mats[1], feed_mats[2])
    gate_val = times_trans(feed_low, gate_full)
    up_val = times_trans(feed_low, up_full)
    hidden = (jax.nn.silu(gate_val) * up_val).astype(jnp.bfloat16)
    down_val = jnp.dot(hidden, down_full, preferred_element_type=jnp.float32)
    layer_output = (middle + down_val).astype(jnp.bfloat16)
    hidden_grad = times_trans(output_grad, down_full)
    sigmoid_val = jax.nn.sigmoid(gate_val)
    gate_grad = (
        hidden_grad * up_val * (sigmoid_val * (1.0 + gate_val * (1.0 - sigmoid_val)))
    ).astype(jnp.bfloat16)
    up_grad = (hidden_grad * jax.nn.silu(gate_val)).astype(jnp.bfloat16)
    feed_grad = jnp.dot(gate_grad, gate_full, preferred_element_type=jnp.float32) + jnp.dot(
        up_grad, up_full, preferred_element_type=jnp.float32
    )
    feed_sums = lax.psum_scatter(
        jnp.stack(
            [
                trans_times(gate_grad, feed_low),
                trans_times(up_grad, feed_low),
                trans_times(hidden, output_grad),
            ],
            axis=1,
        ),
        ("shard", "seq"),
        scatter_dimension=0,
        tiled=True,
    )
    middle_norm_grad, gain_two_grad = norm_back(feed_grad, middle, scale_two, gain_two)
    middle_grad = output_grad.astype(jnp.float32) + middle_norm_grad
    attend_grad = middle_grad.astype(jnp.bfloat16)
    output_term = trans_times(token_out, attend_grad)
    token_out_grad = times_trans(attend_grad, output_full).astype(jnp.bfloat16)
    head_out_grad = lax.all_to_all(
        token_out_grad, "seq", split_axis=1, concat_axis=0, tiled=True
    ).reshape(span_len, heads_dev, HEAD_DIM)
    row_dots = jnp.transpose(jnp.sum(head_out_grad.astype(jnp.float32) * head_out32, axis=-1))

    def grad_step(query_acc, pieces):
        key_blk, value_blk, key_pos, key_doc = pieces
        scores = block_scores(key_blk, key_pos, key_doc)
        probs = jnp.exp(scores - log_total[..., None])
        prob_grad = jnp.einsum(
            "qhd,khd->hqk", head_out_grad, value_blk, preferred_element_type=jnp.float32
        )
        score_grad = (probs * (prob_grad - row_dots[..., None])).astype(jnp.bfloat16)
        query_next = query_acc + score_scale * jnp.einsum(
            "hqk,khd->qhd", score_grad, key_blk, preferred_element_type=jnp.float32
        )
        key_part = score_scale * jnp.einsum(
            "hqk,qhd->khd", score_grad, head_query, preferred_element_type=jnp.float32
        )
        value_part = jnp.einsum(
            "hqk,qhd->khd",
            probs.astype(jnp.bfloat16),
            head_out_grad,
            preferred_element_type=jnp.float32,
        )
        return (query_next, (key_part, value_part))

    query_grad, block_grads = lax.scan(
        grad_step, start_acc, (key_blocks, value_blocks, pos_blocks, doc_blocks)
    )
    pair_grads = jnp.stack(
        [
            block_grads[0].reshape(stream_len, head_width),
            block_grads[1].reshape(stream_len, head_width),
        ]
    )
    own_pair = lax.psum_scatter(
        pair_grads.astype(jnp.bfloat16), "shard", scatter_dimension=1, tiled=True
    ).astype(jnp.float32)
    span_cos, span_sin = rope_tables(span_positions, HEAD_DIM)
    query_back = unrotate(query_grad, span_cos, span_sin).reshape(span_len, head_width)
    key_back = unrotate(
        own_pair[0].reshape(span_len, heads_dev, HEAD_DIM), span_cos, span_sin
    ).reshape(span_len, head_width)
    back_stack = jnp.stack([query_back, key_back, own_pair[1]]).astype(jnp.bfloat16)
    token_grads = lax.all_to_all(back_stack, "seq", split_axis=1, concat_axis=2, tiled=True)
    norm_grad = (
        times_trans(token_grads[0], query_full)
        + times_trans(token_grads[1], key_full)
        + times_trans(token_grads[2], value_full)
    )
    input_norm_grad, gain_one_grad = norm_back(norm_grad, inputs, scale_one, gain_one)
    input_grad = (middle_grad + input_norm_grad).astype(jnp.bfloat16)
    query_term = trans_times(normed_low, token_grads[0])
    key_term = trans_times(normed_low, token_grads[1])
    value_term = trans_times(normed_low, token_grads[2])
    summed = (
        lax.psum_scatter(query_term, ("shard", "seq"), scatter_dimension=0, tiled=True),
        lax.psum_scatter(key_term, ("shard", "seq"), scatter_dimension=0, tiled=True),
        lax.psum_scatter(value_term, ("shard", "seq"), scatter_dimension=0, tiled=True),
        lax.psum_scatter(output_term, ("shard", "seq"), scatter_dimension=0, tiled=True),
        lax.psum_scatter(gain_one_grad, ("shard", "seq"), scatter_dimension=0, tiled=True),
        lax.psum_scatter(gain_two_grad, ("shard", "seq"), scatter_dimension=0, tiled=True),
    )
    query_wgrad, key_wgrad, value_wgrad = (summed[0], summed[1], summed[2])
    output_wgrad, gain_one_out, gain_two_out = (summed[3], summed[4], summed[5])
    return (
        layer_output,
        input_grad,
        gain_one_out,
        query_wgrad,
        key_wgrad,
        value_wgrad,
        output_wgrad,
        gain_two_out,
        feed_sums[:, 0],
        feed_sums[:, 1],
        feed_sums[:, 2],
    )


HEADS = 32
BF16 = jnp.bfloat16
F32 = jnp.float32


def dot_nn(lhs_mat, rhs_mat):
    return lax.dot_general(
        lhs_mat, rhs_mat, (((1,), (0,)), ((), ())), preferred_element_type=jnp.float32
    )


def slot_block(slot, place, half):
    z, core = place // 2, place % 2
    return ((z + slot // 2) % half) * 2 + (core + slot) % 2


def fwd_kernel(tok, place_ref, lo_ref, full_ref, start_ref, qkv_ref, out_ref, blocks_ref, lse_ref,
               k_nat, m_s, l_s, acc_s):
    i = pl.program_id(0)
    spans, rows, span = qkv_ref.shape
    slots = span // tok
    place = place_ref[0]
    scale2 = HEAD_DIM ** -0.5 * math.log2(math.e)

    @pl.when(i == 0)
    def _():
        for s in range(spans):
            k_nat[pl.ds(s * span, span), :] = qkv_ref[s, HEAD_DIM : 2 * HEAD_DIM, :].T

    q_t = qkv_ref[i, :HEAD_DIM, :]
    m_s[...] = jnp.full_like(m_s, -1e30)
    l_s[...] = jnp.zeros_like(l_s)
    acc_s[...] = jnp.zeros_like(acc_s)

    def step(j, masked):
        s_t = dot_nn(k_nat[pl.ds(pl.multiple_of(j * span, span), span), :], q_t) * scale2
        if masked:
            s_t = jnp.where(allowed_pairs(i, j, place, tok, span, start_ref), s_t, -jnp.inf)
        m_old = m_s[...]
        m_new = jnp.maximum(m_old, jnp.max(s_t, axis=0, keepdims=True))
        alpha = jnp.exp2(m_old - m_new)
        p_t = jnp.exp2(s_t - m_new)
        l_s[...] = l_s[...] * alpha + jnp.sum(p_t, axis=0, keepdims=True)
        m_s[...] = m_new
        acc_s[...] = acc_s[...] * alpha + dot_nn(
            qkv_ref[j, 2 * HEAD_DIM :, :], p_t.astype(jnp.bfloat16)
        )

    def loop_body(masked):
        def body(j, carry):
            step(j, masked)
            return carry

        return body

    lax.fori_loop(lo_ref[i], full_ref[i], loop_body(True), 0)
    lax.fori_loop(full_ref[i], i, loop_body(False), 0)
    step(i, True)
    out = acc_s[...] / l_s[...]
    out_ref[...] = out
    lse_ref[...] = m_s[...] + jnp.log2(l_s[...])
    for slot in range(slots):
        blocks_ref[slot_block(slot, place, slots // 2)] = out[
            :, slot * tok : (slot + 1) * tok
        ].astype(jnp.bfloat16)


def span_positions_of(lane, place, tok, span):
    half = span // tok // 2
    return slot_block(lane // tok, place, half) * tok + lane % tok


def allowed_pairs(i, j, place, tok, span, start_ref):
    k_lane = lax.broadcasted_iota(jnp.int32, (span, 128), 0)
    k_pos = (j * span + span_positions_of(k_lane, place, tok, span))[:, :1]
    q_lane = lax.broadcasted_iota(jnp.int32, (8, span), 1)
    q_pos = (i * span + span_positions_of(q_lane, place, tok, span))[:1]
    start = start_ref[i]
    return (k_pos <= q_pos) & (k_pos >= start)


def bwd_kernel(tok, place_ref, hi_ref, full_ref, start_ref, qkv_ref, lse_ref, out_ref, dob_ref,
               dq_ref, dk_ref, dv_ref, dk_s, dv_s, do_s, di_s):
    j = pl.program_id(0)
    spans, rows, span = qkv_ref.shape
    slots = span // tok
    place = place_ref[0]
    scale = HEAD_DIM ** -0.5
    scale2 = scale * math.log2(math.e)

    @pl.when(j == 0)
    def _():
        dq_ref[...] = jnp.zeros_like(dq_ref)
        for s in range(spans):
            for slot in range(slots):
                do_s[s, :, slot * tok : (slot + 1) * tok] = dob_ref[
                    s * slots + slot_block(slot, place, slots // 2)
                ]
            cols = slice(s * span, (s + 1) * span)
            di_s[s] = jnp.sum(do_s[s].astype(jnp.float32) * out_ref[:, cols], axis=0, keepdims=True)

    k_t = qkv_ref[j, HEAD_DIM : 2 * HEAD_DIM, :]
    k_nat = k_t.T
    v_nat = qkv_ref[j, 2 * HEAD_DIM :, :].T
    dk_s[...] = jnp.zeros_like(dk_s)
    dv_s[...] = jnp.zeros_like(dv_s)

    def step(i, masked):
        cols = pl.ds(pl.multiple_of(i * span, span), span)
        q_t = qkv_ref[i, :HEAD_DIM, :]
        p_t = jnp.exp2(dot_nn(k_nat, q_t) * scale2 - lse_ref[:, cols])
        if masked:
            p_t = jnp.where(allowed_pairs(i, j, place, tok, span, start_ref), p_t, 0.0)
        do_t = do_s[i]
        dv_s[...] += times_trans(do_t, p_t.astype(jnp.bfloat16))
        ds_t = (p_t * (dot_nn(v_nat, do_t) - di_s[i])).astype(jnp.bfloat16)
        dk_s[...] += times_trans(q_t, ds_t)
        dq_ref[:, cols] += dot_nn(k_t, ds_t)

    step(j, True)

    def body(i, carry):
        whole = full_ref[i] <= j

        @pl.when(whole)
        def _():
            step(i, False)

        @pl.when(jnp.logical_not(whole))
        def _():
            step(i, True)

        return carry

    lax.fori_loop(j + 1, hi_ref[j], body, 0)
    dk_ref[...] = dk_s[...] * scale
    dv_ref[...] = dv_s[...]

    @pl.when(j == pl.num_programs(0) - 1)
    def _():
        dq_ref[...] = dq_ref[...] * scale


def doc_bounds(doc_lengths, positions):
    spans, span = positions.shape
    ends = jnp.cumsum(doc_lengths)
    over = ends[:, None, None] <= positions[None]
    start = jnp.max(jnp.where(over, ends[:, None, None], 0), axis=0).astype(jnp.int32)
    stop = jnp.min(jnp.where(over, spans * span, ends[:, None, None]), axis=0).astype(jnp.int32)
    first = jnp.min(start, axis=1) // span
    whole = jnp.minimum(
        (jnp.max(start, axis=1) + span - 1) // span, jnp.arange(spans, dtype=jnp.int32)
    )
    last = (jnp.max(stop, axis=1) + span - 1) // span
    return start[:, None, :], first, whole, last


def attend(qkv, tok, place, bounds):
    spans, rows, span = qkv.shape
    stream = spans * span
    slots = span // tok
    start, first, whole, last = bounds
    smem = pl.BlockSpec(memory_space=pltpu.SMEM)
    vmem = pl.BlockSpec(memory_space=pltpu.VMEM)
    return pl.pallas_call(
        functools.partial(fwd_kernel, tok),
        grid=(spans,),
        in_specs=[smem, smem, smem, vmem, vmem],
        out_specs=[
            pl.BlockSpec((HEAD_DIM, span), lambda i: (0, i)),
            pl.BlockSpec((slots, HEAD_DIM, tok), lambda i: (i, 0, 0)),
            pl.BlockSpec((1, span), lambda i: (0, i)),
        ],
        out_shape=[
            jax.ShapeDtypeStruct((HEAD_DIM, stream), jnp.float32),
            jax.ShapeDtypeStruct((stream // tok, HEAD_DIM, tok), jnp.bfloat16),
            jax.ShapeDtypeStruct((1, stream), jnp.float32),
        ],
        scratch_shapes=[
            pltpu.VMEM((stream, HEAD_DIM), jnp.bfloat16),
            pltpu.VMEM((1, span), jnp.float32),
            pltpu.VMEM((1, span), jnp.float32),
            pltpu.VMEM((HEAD_DIM, span), jnp.float32),
        ],
        compiler_params=pltpu.CompilerParams(vmem_limit_bytes=40 * 2**20),
        cost_estimate=pl.CostEstimate(
            flops=stream * stream * 256 * 2, bytes_accessed=stream * 1024, transcendentals=stream * stream // 2
        ),
        name="attend",
    )(place, first, whole, start, qkv)


def attend_back(qkv, lse, out, out_grad, tok, place, bounds):
    spans, rows, span = qkv.shape
    stream = spans * span
    start, first, whole, last = bounds
    smem = pl.BlockSpec(memory_space=pltpu.SMEM)
    vmem = pl.BlockSpec(memory_space=pltpu.VMEM)
    return pl.pallas_call(
        functools.partial(bwd_kernel, tok),
        grid=(spans,),
        in_specs=[smem, smem, smem, vmem, vmem, vmem, vmem, vmem],
        out_specs=[
            pl.BlockSpec((HEAD_DIM, stream), lambda j: (0, 0)),
            pl.BlockSpec((HEAD_DIM, span), lambda j: (0, j)),
            pl.BlockSpec((HEAD_DIM, span), lambda j: (0, j)),
        ],
        out_shape=[jax.ShapeDtypeStruct((HEAD_DIM, stream), jnp.float32)] * 3,
        scratch_shapes=[
            pltpu.VMEM((HEAD_DIM, span), jnp.float32),
            pltpu.VMEM((HEAD_DIM, span), jnp.float32),
            pltpu.VMEM((spans, HEAD_DIM, span), jnp.bfloat16),
            pltpu.VMEM((spans, 1, span), jnp.float32),
        ],
        compiler_params=pltpu.CompilerParams(vmem_limit_bytes=40 * 2**20),
        cost_estimate=pl.CostEstimate(
            flops=5 * stream * stream * 256, bytes_accessed=stream * 2048, transcendentals=stream * stream // 2
        ),
        name="attend_back",
    )(place, whole_last(last), whole, start, qkv, lse, out, out_grad)


def whole_last(last):
    return last


def swap_cores(values):
    count = lax.axis_size("seq")
    return lax.ppermute(values, "seq", [(i, i ^ 1) for i in range(count)])


def from_chip(values, step):
    count = lax.axis_size("seq")
    return lax.ppermute(values, "seq", [((i + 2 * step) % count, i) for i in range(count)])


def from_shard(values, flip):
    return lax.ppermute(values, "shard", [(i, i ^ flip) for i in range(4)])


def gather_seq(values):
    half = lax.axis_size("seq") // 2
    same = [values] + [from_chip(values, step) for step in range(1, half)]
    return [block for one in same for block in (one, swap_cores(one))]


def scatter_seq(parts):
    half = lax.axis_size("seq") // 2
    total = None
    for step in range(half):
        pair = parts[2 * step].astype(F32) + swap_cores(parts[2 * step + 1].astype(BF16)).astype(F32)
        if step:
            pair = from_chip(pair.astype(BF16), -step).astype(F32)
        total = pair if total is None else total + pair
    return total


def gather_shard(block):
    rows = block.shape[0] // 2
    one, two = from_shard(block, 1), from_shard(block, 2)
    far = [from_shard(one[:rows], 2), from_shard(two[rows:], 1)]
    return [block, one, two, jnp.concatenate(far)]


def scatter_shard(parts):
    rows = parts[3].shape[0] // 2
    low = parts[3].astype(BF16)
    top, bottom = from_shard(low[:rows], 1), from_shard(low[rows:], 2)
    one = jnp.concatenate([parts[1][:rows], parts[1][rows:] + bottom.astype(F32)])
    two = jnp.concatenate([parts[2][:rows] + top.astype(F32), parts[2][rows:]])
    return (
        parts[0]
        + from_shard(one.astype(BF16), 1).astype(F32)
        + from_shard(two.astype(BF16), 2).astype(F32)
    )


def to_natural_shards(slots):
    own = lax.axis_index("shard")
    stacked = jnp.stack(slots)
    return jnp.concatenate(
        [lax.dynamic_index_in_dim(stacked, own ^ k, 0, keepdims=False) for k in range(4)]
    )


def bits_of(flat):
    seq_bits = [("seq", 1 << b) for b in range(lax.axis_size("seq").bit_length() - 1)]
    return seq_bits + [("shard", 1), ("shard", 2)]


def gather_small(row):
    rows = row
    for axis, flip in bits_of(row):
        count = lax.axis_size(axis)
        other = lax.ppermute(rows, axis, [(i, i ^ flip) for i in range(count)])
        upper = (lax.axis_index(axis) & flip) != 0
        rows = jnp.concatenate(
            [jnp.where(upper, other, rows), jnp.where(upper, rows, other)], axis=0
        )
    return rows


def scatter_small(rows):
    for axis, flip in reversed(bits_of(rows)):
        count = lax.axis_size(axis)
        upper = (lax.axis_index(axis) & flip) != 0
        half = rows.shape[0] // 2
        keep = jnp.where(upper, rows[half:], rows[:half])
        give = jnp.where(upper, rows[:half], rows[half:])
        rows = keep + lax.ppermute(give, axis, [(i, i ^ flip) for i in range(count)])
    return rows


def rotate_rows(front, back, cos_t, sin_t):
    return jnp.concatenate([front * cos_t - back * sin_t, back * cos_t + front * sin_t], axis=-2)


def per_device(
    layer_input,
    doc_lengths,
    norm_gain,
    query_weight,
    key_weight,
    value_weight,
    output_weight,
    feed_gain,
    gate_weight,
    up_weight,
    down_weight,
    output_grad,
):
    tok, width = layer_input.shape
    seqs, shards = lax.axis_size("seq"), lax.axis_size("shard")
    shard, seq = lax.axis_index("shard"), lax.axis_index("seq")
    span = tok * seqs
    half_head = HEAD_DIM // 2
    place = jnp.reshape(seq, (1,)).astype(jnp.int32)

    lanes = jnp.arange(span, dtype=jnp.int32)
    in_span = slot_block(lanes // tok, seq.astype(jnp.int32), seqs // 2) * tok + lanes % tok
    positions = jnp.arange(shards, dtype=jnp.int32)[:, None] * span + in_span[None]
    bounds = doc_bounds(doc_lengths, positions)
    exponent = -2.0 * jnp.arange(half_head, dtype=jnp.float32) / HEAD_DIM
    inverse = jnp.power(jnp.float32(ROPE_BASE), exponent)
    angles = positions.astype(F32)[:, None, :] * inverse[None, :, None]
    cos_all, sin_all = jnp.cos(angles), jnp.sin(angles)
    cos_own = lax.dynamic_index_in_dim(cos_all, shard, 0, keepdims=False)
    sin_own = lax.dynamic_index_in_dim(sin_all, shard, 0, keepdims=False)

    inputs_slots = gather_seq(layer_input)
    gain_col = norm_gain.astype(F32)[:, None]
    heads_here = HEADS // seqs
    own_rows = query_weight.shape[0]
    packed = jnp.stack(
        [
            (weight.astype(F32) * gain_col).astype(BF16).reshape(own_rows, shards, seqs, HEAD_DIM)
            for weight in (query_weight, key_weight, value_weight)
        ],
        axis=2,
    )
    packed = jnp.transpose(packed, (3, 0, 1, 2, 4)).reshape(seqs, own_rows, heads_here * 3 * HEAD_DIM)
    columns = lax.all_to_all(packed, "seq", split_axis=0, concat_axis=0, tiled=True)
    columns = to_natural_shards(
        gather_shard(columns.reshape(seqs * own_rows, heads_here * 3 * HEAD_DIM))
    )

    span_inputs = jnp.concatenate(inputs_slots).astype(F32)
    scale_span = lax.rsqrt(jnp.mean(span_inputs * span_inputs, axis=-1, keepdims=True) + NORM_EPS)
    unit_low = (span_inputs * scale_span).astype(BF16)
    qkv = lax.dot_general(
        columns, unit_low, (((0,), (1,)), ((), ())), preferred_element_type=F32
    ).reshape(shards, 3, HEAD_DIM, span)
    turned = rotate_rows(
        qkv[:, :2, :half_head], qkv[:, :2, half_head:], cos_own[None, None], sin_own[None, None]
    )
    qkv_low = jnp.concatenate([turned, qkv[:, 2:]], axis=1).astype(BF16)
    head_qkv = lax.all_to_all(
        qkv_low.reshape(shards, 3 * HEAD_DIM, span), "shard", split_axis=0, concat_axis=0, tiled=True
    )

    head_out, out_blocks, lse = attend(head_qkv, tok, place, bounds)
    token_out = lax.all_to_all(
        out_blocks, ("shard", "seq"), split_axis=0, concat_axis=0, tiled=True
    ).reshape(width, tok)

    output_full = lax.all_gather(output_weight, ("shard", "seq"), axis=0, tiled=True)
    gain_two = gather_small(feed_gain.astype(F32)[None, :]).reshape(1, width)
    grad_slots = gather_seq(output_grad)
    span_grad = jnp.concatenate(grad_slots)
    gate_here = jnp.concatenate(gather_shard(gate_weight))
    up_here = jnp.concatenate(gather_shard(up_weight))
    down_here = jnp.concatenate(gather_shard(down_weight))

    inputs = layer_input.astype(F32)
    middle = inputs + trans_times(token_out, output_full)
    normed_two, scale_two = normalize(middle, gain_two)
    feed_low = jnp.concatenate(gather_seq(normed_two.astype(BF16)))

    gate_val = times_trans(feed_low, gate_here)
    up_val = times_trans(feed_low, up_here)
    hidden_grad = times_trans(span_grad, down_here)
    sigmoid_val = jax.nn.sigmoid(gate_val)
    hidden = (gate_val * sigmoid_val * up_val).astype(BF16)
    gate_grad = (
        hidden_grad * up_val * (sigmoid_val * (1.0 + gate_val * (1.0 - sigmoid_val)))
    ).astype(BF16)
    up_grad = (hidden_grad * (gate_val * sigmoid_val)).astype(BF16)
    feed_part = dot_nn(gate_grad, gate_here) + dot_nn(up_grad, up_here)
    feed_grad = scatter_seq(feed_part.reshape(seqs, tok, width))

    middle_norm_grad, gain_two_part = norm_back(feed_grad, middle, scale_two, gain_two)
    middle_grad = output_grad.astype(F32) + middle_norm_grad
    attend_grad = middle_grad.astype(BF16)
    token_out_grad = times_trans(output_full, attend_grad).astype(BF16)
    out_grad_blocks = lax.all_to_all(
        token_out_grad.reshape(HEADS, HEAD_DIM, tok),
        ("shard", "seq"),
        split_axis=0,
        concat_axis=0,
        tiled=True,
    )
    query_grad, key_grad, value_grad = attend_back(
        head_qkv, lse, head_out, out_grad_blocks, tok, place, bounds
    )

    def by_span(grad):
        return jnp.transpose(grad.reshape(HEAD_DIM, shards, span), (1, 0, 2))

    def turn_back(grad):
        rows = by_span(grad)
        return rotate_rows(rows[:, :half_head], rows[:, half_head:], cos_all, -sin_all)

    back = jnp.concatenate(
        [turn_back(query_grad), turn_back(key_grad), by_span(value_grad)], axis=1
    ).astype(BF16)
    span_back = lax.all_to_all(back, "shard", split_axis=0, concat_axis=0, tiled=True).reshape(
        heads_here * 3 * HEAD_DIM, span
    )
    unit_part = lax.dot_general(
        span_back, columns, (((0,), (1,)), ((), ())), preferred_element_type=F32
    )
    unit_grad = scatter_seq(unit_part.reshape(seqs, tok, width))
    scale_one = lax.rsqrt(jnp.mean(inputs * inputs, axis=-1, keepdims=True) + NORM_EPS)
    unit_rows = inputs * scale_one
    input_grad = (
        middle_grad
        + scale_one * (unit_grad - unit_rows * jnp.mean(unit_grad * unit_rows, axis=-1, keepdims=True))
    ).astype(BF16)

    cols_part = lax.dot_general(
        unit_low, span_back, (((0,), (1,)), ((), ())), preferred_element_type=F32
    ).reshape(shards, seqs * own_rows, heads_here * 3 * HEAD_DIM)
    cols_sum = scatter_shard(
        [lax.dynamic_index_in_dim(cols_part, shard ^ k, 0, keepdims=False) for k in range(4)]
    )
    cols_all = lax.all_to_all(
        cols_sum.astype(BF16).reshape(seqs, own_rows, -1), "seq", split_axis=0, concat_axis=0, tiled=True
    ).reshape(seqs, own_rows, shards, 3, HEAD_DIM)
    unit_wgrads = jnp.transpose(cols_all, (3, 1, 2, 0, 4)).reshape(3, own_rows, width).astype(F32)
    query_wgrad, key_wgrad, value_wgrad = [unit_wgrads[i] * gain_col for i in range(3)]
    gain_one_out = sum(
        jnp.sum(unit_wgrads[i] * weight.astype(F32), axis=1)
        for i, weight in enumerate((query_weight, key_weight, value_weight))
    )

    out_low = by_span(head_out).astype(BF16)
    out_slots = jnp.concatenate(
        [
            from_shard(lax.dynamic_index_in_dim(out_low, shard ^ k, 0, keepdims=False), k)
            if k
            else lax.dynamic_index_in_dim(out_low, shard, 0, keepdims=False)
            for k in range(4)
        ]
    )
    span_attend_grad = jnp.concatenate(gather_seq(attend_grad))
    out_part = dot_nn(out_slots, span_attend_grad).reshape(shards, HEAD_DIM, width)
    output_wgrad = scatter_shard([out_part[k] for k in range(4)])
    gain_two_out = scatter_small(gain_two_part.reshape(shards * seqs, -1)).reshape(-1)

    down_part = dot_nn(hidden, down_here)
    layer_output = (middle + scatter_seq(down_part.reshape(seqs, tok, width))).astype(BF16)

    def feed_wgrad(lhs_mat, rhs_mat):
        part = trans_times(lhs_mat, rhs_mat).reshape(shards, -1, width)
        return scatter_shard([part[k] for k in range(4)])

    down_wgrad = feed_wgrad(hidden, span_grad)
    gate_wgrad = feed_wgrad(gate_grad, feed_low)
    up_wgrad = feed_wgrad(up_grad, feed_low)
    return (
        layer_output,
        input_grad,
        gain_one_out,
        query_wgrad,
        key_wgrad,
        value_wgrad,
        output_wgrad,
        gain_two_out,
        gate_wgrad,
        up_wgrad,
        down_wgrad,
    )


def solution(mesh):
    shards, seqs = mesh.shape["shard"], mesh.shape["seq"]
    body = per_device if shards == 4 and shards * seqs == HEADS else per_device_any
    return jax.shard_map(
        body,
        mesh=mesh,
        in_specs=(
            P(("shard", "seq"), None),
            P(),
            P(("shard", "seq")),
            P(("shard", "seq"), None),
            P(("shard", "seq"), None),
            P(("shard", "seq"), None),
            P(("shard", "seq"), None),
            P(("shard", "seq")),
            P(("shard", "seq"), None),
            P(("shard", "seq"), None),
            P(("shard", "seq"), None),
            P(("shard", "seq"), None),
        ),
        out_specs=(
            P(("shard", "seq"), None),
            P(("shard", "seq"), None),
            P(("shard", "seq")),
            P(("shard", "seq"), None),
            P(("shard", "seq"), None),
            P(("shard", "seq"), None),
            P(("shard", "seq"), None),
            P(("shard", "seq")),
            P(("shard", "seq"), None),
            P(("shard", "seq"), None),
            P(("shard", "seq"), None),
        ),
        check_vma=False,
    )
```

```python
import functools
import math

import jax
import jax.numpy as jnp
from jax import lax
from jax.experimental import pallas as pl
from jax.experimental.pallas import tpu as pltpu
from jax.sharding import PartitionSpec as P

HEAD_DIM = 64


NORM_EPS = 1e-05
ROPE_BASE = 130000.0


def rope_tables(positions, width):
    half_width = width // 2
    exponent = -2.0 * jnp.arange(half_width, dtype=jnp.float32) / width
    inverse = jnp.power(jnp.float32(ROPE_BASE), exponent)
    angles = positions.astype(jnp.float32)[:, None] * inverse[None, :]
    return (jnp.cos(angles), jnp.sin(angles))


def rotate(values, cos_table, sin_table):
    half_width = values.shape[-1] // 2
    front = values[..., :half_width]
    back_half = values[..., half_width:]
    cos_wide = cos_table[:, None, :]
    sin_wide = sin_table[:, None, :]
    return jnp.concatenate(
        [front * cos_wide - back_half * sin_wide, back_half * cos_wide + front * sin_wide], axis=-1
    )


def unrotate(values, cos_table, sin_table):
    half_width = values.shape[-1] // 2
    front = values[..., :half_width]
    back_half = values[..., half_width:]
    cos_wide = cos_table[:, None, :]
    sin_wide = sin_table[:, None, :]
    return jnp.concatenate(
        [front * cos_wide + back_half * sin_wide, back_half * cos_wide - front * sin_wide], axis=-1
    )


def doc_numbers(doc_lengths, positions):
    doc_ends = jnp.cumsum(doc_lengths)
    return jnp.sum((doc_ends[:, None] <= positions[None, :]).astype(jnp.int32), axis=0)


def normalize(values, gain_vec):
    scale_row = lax.rsqrt(jnp.mean(values * values, axis=-1, keepdims=True) + NORM_EPS)
    return (values * scale_row * gain_vec, scale_row)


def norm_back(grad_in, values, scale_row, gain_vec):
    unit_rows = values * scale_row
    gain_grad = jnp.sum(grad_in * unit_rows, axis=0)
    unit_grad = grad_in * gain_vec
    value_grad = scale_row * (
        unit_grad - unit_rows * jnp.mean(unit_grad * unit_rows, axis=-1, keepdims=True)
    )
    return (value_grad, gain_grad)


def times_trans(lhs_mat, rhs_mat):
    return lax.dot_general(
        lhs_mat, rhs_mat, (((1,), (1,)), ((), ())), preferred_element_type=jnp.float32
    )


def trans_times(lhs_mat, rhs_mat):
    return lax.dot_general(
        lhs_mat, rhs_mat, (((0,), (0,)), ((), ())), preferred_element_type=jnp.float32
    )


def per_device_any(
    layer_input,
    doc_lengths,
    norm_gain,
    query_weight,
    key_weight,
    value_weight,
    output_weight,
    feed_gain,
    gate_weight,
    up_weight,
    down_weight,
    output_grad,
):
    tok_rows = layer_input.shape[0]
    width = layer_input.shape[1]
    seq_count = lax.axis_size("seq")
    shard_count = lax.axis_size("shard")
    span_len = tok_rows * seq_count
    stream_len = span_len * shard_count
    span_start = lax.axis_index("shard") * span_len
    own_positions = (
        span_start + lax.axis_index("seq") * tok_rows + jnp.arange(tok_rows, dtype=jnp.int32)
    )
    span_positions = span_start + jnp.arange(span_len, dtype=jnp.int32)
    all_positions = jnp.arange(stream_len, dtype=jnp.int32)
    key_docs = doc_numbers(doc_lengths, all_positions)
    query_docs = lax.dynamic_slice_in_dim(key_docs, span_start, span_len)
    score_scale = HEAD_DIM ** (-0.5)
    gathered = (
        lax.all_gather(query_weight, ("shard", "seq"), axis=0, tiled=True),
        lax.all_gather(key_weight, ("shard", "seq"), axis=0, tiled=True),
        lax.all_gather(value_weight, ("shard", "seq"), axis=0, tiled=True),
        lax.all_gather(output_weight, ("shard", "seq"), axis=0, tiled=True),
        lax.all_gather(norm_gain, ("shard", "seq"), axis=0, tiled=True),
        lax.all_gather(feed_gain, ("shard", "seq"), axis=0, tiled=True),
    )
    query_full, key_full, value_full, output_full = (
        gathered[0],
        gathered[1],
        gathered[2],
        gathered[3],
    )
    gain_one = gathered[4].astype(jnp.float32)
    gain_two = gathered[5].astype(jnp.float32)
    inputs = layer_input.astype(jnp.float32)
    normed, scale_one = normalize(inputs, gain_one)
    normed_low = normed.astype(jnp.bfloat16)
    own_cos, own_sin = rope_tables(own_positions, HEAD_DIM)
    query_proj = jnp.dot(normed_low, query_full, preferred_element_type=jnp.float32)
    key_proj = jnp.dot(normed_low, key_full, preferred_element_type=jnp.float32)
    value_proj = jnp.dot(normed_low, value_full, preferred_element_type=jnp.float32)
    query_rot = rotate(query_proj.reshape(tok_rows, -1, HEAD_DIM), own_cos, own_sin).reshape(
        tok_rows, width
    )
    key_rot = rotate(key_proj.reshape(tok_rows, -1, HEAD_DIM), own_cos, own_sin).reshape(
        tok_rows, width
    )
    stacked = jnp.stack(
        [
            query_rot.astype(jnp.bfloat16),
            key_rot.astype(jnp.bfloat16),
            value_proj.astype(jnp.bfloat16),
        ]
    )
    head_triple = lax.all_to_all(stacked, "seq", split_axis=2, concat_axis=1, tiled=True)
    head_width = head_triple.shape[2]
    heads_dev = head_width // HEAD_DIM
    head_query = head_triple[0].reshape(span_len, heads_dev, HEAD_DIM)
    key_value = lax.all_gather(head_triple[1:], "shard", axis=1, tiled=True)
    key_block = math.gcd(stream_len, max(512, stream_len // 16))
    block_count = stream_len // key_block
    key_blocks = key_value[0].reshape(block_count, key_block, heads_dev, HEAD_DIM)
    value_blocks = key_value[1].reshape(block_count, key_block, heads_dev, HEAD_DIM)
    pos_blocks = all_positions.reshape(block_count, key_block)
    doc_blocks = key_docs.reshape(block_count, key_block)

    def block_scores(key_blk, key_pos, key_doc):
        scores = (
            jnp.einsum("qhd,khd->hqk", head_query, key_blk, preferred_element_type=jnp.float32)
            * score_scale
        )
        allowed = (key_pos[None, :] <= span_positions[:, None]) & (
            key_doc[None, :] == query_docs[:, None]
        )
        return jnp.where(allowed[None], scores, -jnp.inf)

    def total_step(state_pair, pieces):
        run_max, run_sum = state_pair
        scores = block_scores(pieces[0], pieces[1], pieces[2])
        new_max = jnp.maximum(run_max, jnp.max(scores, axis=-1))
        new_sum = run_sum * jnp.exp(run_max - new_max) + jnp.sum(
            jnp.exp(scores - new_max[..., None]), axis=-1
        )
        return ((new_max, new_sum), None)

    start_max = jnp.full((heads_dev, span_len), -1e30, jnp.float32)
    start_sum = jnp.zeros((heads_dev, span_len), jnp.float32)
    totals, unused = lax.scan(
        total_step, (start_max, start_sum), (key_blocks, pos_blocks, doc_blocks)
    )
    log_total = totals[0] + jnp.log(totals[1])

    def output_step(accum, pieces):
        scores = block_scores(pieces[0], pieces[2], pieces[3])
        probs = jnp.exp(scores - log_total[..., None]).astype(jnp.bfloat16)
        return (
            accum
            + jnp.einsum("hqk,khd->qhd", probs, pieces[1], preferred_element_type=jnp.float32),
            None,
        )

    start_acc = jnp.zeros((span_len, heads_dev, HEAD_DIM), jnp.float32)
    head_out32, unused = lax.scan(
        output_step, start_acc, (key_blocks, value_blocks, pos_blocks, doc_blocks)
    )
    head_out = head_out32.reshape(span_len, head_width).astype(jnp.bfloat16)
    token_out = lax.all_to_all(head_out, "seq", split_axis=0, concat_axis=1, tiled=True)
    middle = inputs + jnp.dot(token_out, output_full, preferred_element_type=jnp.float32)
    normed_two, scale_two = normalize(middle, gain_two)
    feed_low = normed_two.astype(jnp.bfloat16)
    feed_mats = (
        lax.all_gather(gate_weight, ("shard", "seq"), axis=0, tiled=True),
        lax.all_gather(up_weight, ("shard", "seq"), axis=0, tiled=True),
        lax.all_gather(down_weight, ("shard", "seq"), axis=0, tiled=True),
    )
    gate_full, up_full, down_full = (feed_mats[0], feed_mats[1], feed_mats[2])
    gate_val = times_trans(feed_low, gate_full)
    up_val = times_trans(feed_low, up_full)
    hidden = (jax.nn.silu(gate_val) * up_val).astype(jnp.bfloat16)
    down_val = jnp.dot(hidden, down_full, preferred_element_type=jnp.float32)
    layer_output = (middle + down_val).astype(jnp.bfloat16)
    hidden_grad = times_trans(output_grad, down_full)
    sigmoid_val = jax.nn.sigmoid(gate_val)
    gate_grad = (
        hidden_grad * up_val * (sigmoid_val * (1.0 + gate_val * (1.0 - sigmoid_val)))
    ).astype(jnp.bfloat16)
    up_grad = (hidden_grad * jax.nn.silu(gate_val)).astype(jnp.bfloat16)
    feed_grad = jnp.dot(gate_grad, gate_full, preferred_element_type=jnp.float32) + jnp.dot(
        up_grad, up_full, preferred_element_type=jnp.float32
    )
    feed_sums = lax.psum_scatter(
        jnp.stack(
            [
                trans_times(gate_grad, feed_low),
                trans_times(up_grad, feed_low),
                trans_times(hidden, output_grad),
            ],
            axis=1,
        ),
        ("shard", "seq"),
        scatter_dimension=0,
        tiled=True,
    )
    middle_norm_grad, gain_two_grad = norm_back(feed_grad, middle, scale_two, gain_two)
    middle_grad = output_grad.astype(jnp.float32) + middle_norm_grad
    attend_grad = middle_grad.astype(jnp.bfloat16)
    output_term = trans_times(token_out, attend_grad)
    token_out_grad = times_trans(attend_grad, output_full).astype(jnp.bfloat16)
    head_out_grad = lax.all_to_all(
        token_out_grad, "seq", split_axis=1, concat_axis=0, tiled=True
    ).reshape(span_len, heads_dev, HEAD_DIM)
    row_dots = jnp.transpose(jnp.sum(head_out_grad.astype(jnp.float32) * head_out32, axis=-1))

    def grad_step(query_acc, pieces):
        key_blk, value_blk, key_pos, key_doc = pieces
        scores = block_scores(key_blk, key_pos, key_doc)
        probs = jnp.exp(scores - log_total[..., None])
        prob_grad = jnp.einsum(
            "qhd,khd->hqk", head_out_grad, value_blk, preferred_element_type=jnp.float32
        )
        score_grad = (probs * (prob_grad - row_dots[..., None])).astype(jnp.bfloat16)
        query_next = query_acc + score_scale * jnp.einsum(
            "hqk,khd->qhd", score_grad, key_blk, preferred_element_type=jnp.float32
        )
        key_part = score_scale * jnp.einsum(
            "hqk,qhd->khd", score_grad, head_query, preferred_element_type=jnp.float32
        )
        value_part = jnp.einsum(
            "hqk,qhd->khd",
            probs.astype(jnp.bfloat16),
            head_out_grad,
            preferred_element_type=jnp.float32,
        )
        return (query_next, (key_part, value_part))

    query_grad, block_grads = lax.scan(
        grad_step, start_acc, (key_blocks, value_blocks, pos_blocks, doc_blocks)
    )
    pair_grads = jnp.stack(
        [
            block_grads[0].reshape(stream_len, head_width),
            block_grads[1].reshape(stream_len, head_width),
        ]
    )
    own_pair = lax.psum_scatter(
        pair_grads.astype(jnp.bfloat16), "shard", scatter_dimension=1, tiled=True
    ).astype(jnp.float32)
    span_cos, span_sin = rope_tables(span_positions, HEAD_DIM)
    query_back = unrotate(query_grad, span_cos, span_sin).reshape(span_len, head_width)
    key_back = unrotate(
        own_pair[0].reshape(span_len, heads_dev, HEAD_DIM), span_cos, span_sin
    ).reshape(span_len, head_width)
    back_stack = jnp.stack([query_back, key_back, own_pair[1]]).astype(jnp.bfloat16)
    token_grads = lax.all_to_all(back_stack, "seq", split_axis=1, concat_axis=2, tiled=True)
    norm_grad = (
        times_trans(token_grads[0], query_full)
        + times_trans(token_grads[1], key_full)
        + times_trans(token_grads[2], value_full)
    )
    input_norm_grad, gain_one_grad = norm_back(norm_grad, inputs, scale_one, gain_one)
    input_grad = (middle_grad + input_norm_grad).astype(jnp.bfloat16)
    query_term = trans_times(normed_low, token_grads[0])
    key_term = trans_times(normed_low, token_grads[1])
    value_term = trans_times(normed_low, token_grads[2])
    summed = (
        lax.psum_scatter(query_term, ("shard", "seq"), scatter_dimension=0, tiled=True),
        lax.psum_scatter(key_term, ("shard", "seq"), scatter_dimension=0, tiled=True),
        lax.psum_scatter(value_term, ("shard", "seq"), scatter_dimension=0, tiled=True),
        lax.psum_scatter(output_term, ("shard", "seq"), scatter_dimension=0, tiled=True),
        lax.psum_scatter(gain_one_grad, ("shard", "seq"), scatter_dimension=0, tiled=True),
        lax.psum_scatter(gain_two_grad, ("shard", "seq"), scatter_dimension=0, tiled=True),
    )
    query_wgrad, key_wgrad, value_wgrad = (summed[0], summed[1], summed[2])
    output_wgrad, gain_one_out, gain_two_out = (summed[3], summed[4], summed[5])
    return (
        layer_output,
        input_grad,
        gain_one_out,
        query_wgrad,
        key_wgrad,
        value_wgrad,
        output_wgrad,
        gain_two_out,
        feed_sums[:, 0],
        feed_sums[:, 1],
        feed_sums[:, 2],
    )


HEADS = 32
EXTRA = 16
BF16 = jnp.bfloat16
F32 = jnp.float32


SHORT = pl.CostEstimate(flops=0, bytes_accessed=0, transcendentals=0)


def in_hbm(arrays):
    return [pltpu.with_memory_space_constraint(array, pltpu.HBM) for array in arrays]


def dot_nn(lhs_mat, rhs_mat):
    return lax.dot_general(
        lhs_mat, rhs_mat, (((1,), (0,)), ((), ())), preferred_element_type=jnp.float32
    )


def slot_block(slot, place, half):
    z, core = place // 2, place % 2
    return ((z + slot // 2) % half) * 2 + (core + slot) % 2


def fwd_kernel(tok, place_ref, lo_ref, full_ref, start_ref, qkv_ref, gain_ref, out_ref, low_ref, blocks_ref, lse_ref,
               k_nat, m_s, l_s, acc_s):
    i = pl.program_id(0)
    spans, rows, span = qkv_ref.shape
    slots = span // tok
    place = place_ref[0]
    scale2 = HEAD_DIM ** -0.5 * math.log2(math.e)

    @pl.when(i == 0)
    def _():
        for s in range(spans):
            k_nat[pl.ds(s * span, span), :] = qkv_ref[s, HEAD_DIM : 2 * HEAD_DIM, :].T

    q_t = qkv_ref[i, :HEAD_DIM, :]
    m_s[...] = jnp.full_like(m_s, -1e30)
    l_s[...] = jnp.zeros_like(l_s)
    acc_s[...] = jnp.zeros_like(acc_s)

    def step(j, masked, same=False):
        s_t = dot_nn(k_nat[pl.ds(pl.multiple_of(j * span, span), span), :], q_t) * scale2
        if masked:
            s_t = jnp.where(allowed_pairs(i, j, place, tok, span, start_ref, same), s_t, -jnp.inf)
        m_old = m_s[...]
        m_new = jnp.maximum(m_old, jnp.max(s_t, axis=0, keepdims=True))
        alpha = jnp.exp2(m_old - m_new)
        p_t = jnp.exp2(s_t - m_new)
        l_s[...] = l_s[...] * alpha + jnp.sum(p_t, axis=0, keepdims=True)
        m_s[...] = m_new
        acc_s[...] = acc_s[...] * alpha + dot_nn(
            qkv_ref[j, 2 * HEAD_DIM :, :], p_t.astype(jnp.bfloat16)
        )

    def loop_body(masked):
        def body(j, carry):
            step(j, masked)
            return carry

        return body

    lax.fori_loop(lo_ref[i], full_ref[i], loop_body(True), 0)
    lax.fori_loop(full_ref[i], i, loop_body(False), 0)
    step(i, True, True)
    out = acc_s[...] / l_s[...]
    out_ref[0] = out
    low = out.astype(jnp.bfloat16)
    low_ref[0] = low
    lse_ref[0] = m_s[...] + jnp.log2(l_s[...])
    for slot in range(slots):
        at = slot_block(slot, place, slots // 2)
        blocks_ref[at, :HEAD_DIM] = low[:, slot * tok : (slot + 1) * tok]
        blocks_ref[at, HEAD_DIM:] = gain_ref[...]


def span_positions_of(lane, place, tok, span):
    half = span // tok // 2
    return slot_block(lane // tok, place, half) * tok + lane % tok


def allowed_pairs(i, j, place, tok, span, start_ref, same):
    k_lane = lax.broadcasted_iota(jnp.int32, (span, 128), 0)
    k_pos = (j * span + span_positions_of(k_lane, place, tok, span))[:, :1]
    begun = k_pos >= start_ref[i]
    if not same:
        return begun
    q_lane = lax.broadcasted_iota(jnp.int32, (8, span), 1)
    q_pos = (i * span + span_positions_of(q_lane, place, tok, span))[:1]
    return (k_pos <= q_pos) & begun


def bwd_kernel(tok, place_ref, hi_ref, full_ref, start_ref, qkv_ref, lse_ref, out_ref, dob_ref,
               cos_ref, sin_ref, back_ref, dq_s, dk_s, dv_s, do_s, di_s):
    j = pl.program_id(0)
    spans, rows, span = qkv_ref.shape
    slots = span // tok
    place = place_ref[0]
    scale = HEAD_DIM ** -0.5
    scale2 = scale * math.log2(math.e)

    @pl.when(j == 0)
    def _():
        dq_s[...] = jnp.zeros_like(dq_s)
        for s in range(spans):
            for slot in range(slots):
                do_s[s, :, slot * tok : (slot + 1) * tok] = dob_ref[
                    s * slots + slot_block(slot, place, slots // 2), :HEAD_DIM
                ]
            di_s[s] = jnp.sum(do_s[s].astype(jnp.float32) * out_ref[s], axis=0, keepdims=True)

    k_t = qkv_ref[j, HEAD_DIM : 2 * HEAD_DIM, :]
    k_nat = k_t.T
    v_nat = qkv_ref[j, 2 * HEAD_DIM :, :].T
    dk_s[...] = jnp.zeros_like(dk_s)
    dv_s[...] = jnp.zeros_like(dv_s)

    def step(i, masked, same=False):
        q_t = qkv_ref[i, :HEAD_DIM, :]
        p_t = jnp.exp2(dot_nn(k_nat, q_t) * scale2 - lse_ref[i])
        if masked:
            p_t = jnp.where(allowed_pairs(i, j, place, tok, span, start_ref, same), p_t, 0.0)
        do_t = do_s[i]
        dv_s[...] += times_trans(do_t, p_t.astype(jnp.bfloat16))
        ds_t = (p_t * (dot_nn(v_nat, do_t) - di_s[i])).astype(jnp.bfloat16)
        dk_s[...] += times_trans(q_t, ds_t)
        dq_s[i] += dot_nn(k_t, ds_t)

    step(j, True, True)

    def body(i, carry):
        whole = full_ref[i] <= j

        @pl.when(whole)
        def _():
            step(i, False)

        @pl.when(jnp.logical_not(whole))
        def _():
            step(i, True)

        return carry

    lax.fori_loop(j + 1, hi_ref[j], body, 0)

    def turned_back(grad):
        front, back_half = grad[: HEAD_DIM // 2], grad[HEAD_DIM // 2 :]
        cos_t, sin_t = cos_ref[0], sin_ref[0]
        return jnp.concatenate(
            [front * cos_t + back_half * sin_t, back_half * cos_t - front * sin_t], axis=0
        ).astype(jnp.bfloat16)

    back_ref[0, :HEAD_DIM] = turned_back(dq_s[j] * scale)
    back_ref[0, HEAD_DIM : 2 * HEAD_DIM] = turned_back(dk_s[...] * scale)
    back_ref[0, 2 * HEAD_DIM :] = dv_s[...].astype(jnp.bfloat16)


def doc_bounds(doc_lengths, positions):
    spans, span = positions.shape
    ends = jnp.cumsum(doc_lengths)
    over = ends[:, None, None] <= positions[None]
    start = jnp.max(jnp.where(over, ends[:, None, None], 0), axis=0).astype(jnp.int32)
    stop = jnp.min(jnp.where(over, spans * span, ends[:, None, None]), axis=0).astype(jnp.int32)
    first = jnp.min(start, axis=1) // span
    whole = jnp.minimum(
        (jnp.max(start, axis=1) + span - 1) // span, jnp.arange(spans, dtype=jnp.int32)
    )
    last = (jnp.max(stop, axis=1) + span - 1) // span
    return start[:, None, :], first, whole, last


def attend(qkv, gain_rows, tok, place, bounds):
    spans, rows, span = qkv.shape
    stream = spans * span
    slots = span // tok
    start, first, whole, last = bounds
    smem = pl.BlockSpec(memory_space=pltpu.SMEM)
    vmem = pl.BlockSpec(memory_space=pltpu.VMEM)

    def one(*block):
        return pl.BlockSpec((1,) + block, lambda i: (i, 0, 0))

    return pl.pallas_call(
        functools.partial(fwd_kernel, tok),
        grid=(spans,),
        in_specs=[smem, smem, smem, vmem, vmem, vmem],
        out_specs=[
            one(HEAD_DIM, span),
            one(HEAD_DIM, span),
            pl.BlockSpec((slots, HEAD_DIM + EXTRA, tok), lambda i: (i, 0, 0)),
            one(1, span),
        ],
        out_shape=[
            jax.ShapeDtypeStruct((spans, HEAD_DIM, span), jnp.float32),
            jax.ShapeDtypeStruct((spans, HEAD_DIM, span), jnp.bfloat16),
            pltpu.HBM((stream // tok, HEAD_DIM + EXTRA, tok), jnp.bfloat16),
            jax.ShapeDtypeStruct((spans, 1, span), jnp.float32),
        ],
        scratch_shapes=[
            pltpu.VMEM((stream, HEAD_DIM), jnp.bfloat16),
            pltpu.VMEM((1, span), jnp.float32),
            pltpu.VMEM((1, span), jnp.float32),
            pltpu.VMEM((HEAD_DIM, span), jnp.float32),
        ],
        compiler_params=pltpu.CompilerParams(vmem_limit_bytes=24 * 2**20),
        cost_estimate=pl.CostEstimate(
            flops=stream * stream * 256 * 5, bytes_accessed=stream * 1024, transcendentals=0
        ),
        name="attend",
    )(place, first, whole, start, qkv, gain_rows)


def attend_back(qkv, lse, out, out_grad, cos_t, sin_t, tok, place, bounds):
    spans, rows, span = qkv.shape
    stream = spans * span
    start, first, whole, last = bounds
    smem = pl.BlockSpec(memory_space=pltpu.SMEM)
    vmem = pl.BlockSpec(memory_space=pltpu.VMEM)

    def one(*block):
        return pl.BlockSpec((1,) + block, lambda j: (j, 0, 0))

    return pl.pallas_call(
        functools.partial(bwd_kernel, tok),
        grid=(spans,),
        in_specs=[smem, smem, smem, vmem, vmem, vmem, vmem, vmem]
        + [one(HEAD_DIM // 2, span)] * 2,
        out_specs=one(rows, span),
        out_shape=pltpu.HBM(qkv.shape, jnp.bfloat16),
        scratch_shapes=[
            pltpu.VMEM((spans, HEAD_DIM, span), jnp.float32),
            pltpu.VMEM((HEAD_DIM, span), jnp.float32),
            pltpu.VMEM((HEAD_DIM, span), jnp.float32),
            pltpu.VMEM((spans, HEAD_DIM, span), jnp.bfloat16),
            pltpu.VMEM((spans, 1, span), jnp.float32),
        ],
        compiler_params=pltpu.CompilerParams(vmem_limit_bytes=30 * 2**20),
        cost_estimate=pl.CostEstimate(
            flops=stream * stream * 256 * 7, bytes_accessed=stream * 1024, transcendentals=0
        ),
        name="attend_back",
    )(place, last, whole, start, qkv, lse, out, out_grad, *in_hbm([cos_t, sin_t]))


def pack_kernel(heads, place_ref, gain_ref, query_ref, key_ref, value_ref, out_ref):
    steps = out_ref.shape[1]
    seqs = 2 * steps
    z, core = place_ref[0] // 2, place_ref[0] % 2
    for m, ref in enumerate((query_ref, key_ref, value_ref)):
        rows = (ref[...].astype(jnp.float32) * gain_ref[...]).astype(jnp.bfloat16)
        for head in range(heads):
            at = (head // seqs * 3 + m) * HEAD_DIM
            other = (core + head) % 2
            step = (head % seqs // 2 + steps - z) % steps
            out_ref[other, step, :, at : at + HEAD_DIM] = rows[
                :, head * HEAD_DIM : (head + 1) * HEAD_DIM
            ]


def pack_columns(place, gain_col, weights, seqs):
    rows, width = weights[0].shape
    heads = width // HEAD_DIM
    vmem = pl.BlockSpec(memory_space=pltpu.VMEM)
    return pl.pallas_call(
        functools.partial(pack_kernel, heads),
        in_specs=[pl.BlockSpec(memory_space=pltpu.SMEM)] + [vmem] * 4,
        out_specs=vmem,
        out_shape=jax.ShapeDtypeStruct(
            (2, seqs // 2, rows, heads // seqs * 3 * HEAD_DIM), jnp.bfloat16
        ),
        cost_estimate=SHORT,
        name="pack_columns",
    )(place, gain_col, *weights)


def order_kernel(index_ref, *refs):
    out_ref = refs[-1]
    rows = out_ref.shape[1]
    count = 0
    for ref in refs[:-1]:
        for i in range(ref.shape[0] // rows):
            out_ref[index_ref[count]] = ref[i * rows : (i + 1) * rows]
            count += 1


def order_blocks(pieces, index, rows):
    vmem = pl.BlockSpec(memory_space=pltpu.VMEM)
    blocks = sum(piece.shape[0] for piece in pieces) // rows
    width = pieces[0].shape[1]
    return pl.pallas_call(
        order_kernel,
        in_specs=[pl.BlockSpec(memory_space=pltpu.SMEM)] + [vmem] * len(pieces),
        out_specs=vmem,
        out_shape=jax.ShapeDtypeStruct((blocks, rows, width), pieces[0].dtype),
        compiler_params=pltpu.CompilerParams(vmem_limit_bytes=12 * 2**20),
        cost_estimate=SHORT,
        name="order_blocks",
    )(index, *pieces).reshape(blocks * rows, width)


def spread_kernel(place_ref, own_ref, one_ref, two_ref, out_ref):
    steps, _, rows, _ = out_ref.shape
    z, core = place_ref[0] // 2, place_ref[0] % 2
    total = own_ref[...] + one_ref[...].astype(jnp.float32) + two_ref[...].astype(jnp.float32)
    total = total.astype(jnp.bfloat16)
    for q in range(2 * steps):
        out_ref[(q // 2 + steps - z) % steps, (core + q) % 2] = total[q * rows : (q + 1) * rows]


def spread_columns(place, own, one, two, steps):
    rows, width = own.shape
    vmem = pl.BlockSpec(memory_space=pltpu.VMEM)
    return pl.pallas_call(
        spread_kernel,
        in_specs=[pl.BlockSpec(memory_space=pltpu.SMEM)] + [vmem] * 3,
        out_specs=vmem,
        out_shape=jax.ShapeDtypeStruct((steps, 2, rows // (2 * steps), width), jnp.bfloat16),
        cost_estimate=SHORT,
        name="spread_columns",
    )(place, own, one, two)


def unpack_kernel(heads, place_ref, gain_ref, query_ref, key_ref, value_ref, other_ref, *refs):
    steps = other_ref.shape[0]
    near, out_refs, cols_s = refs[:steps], refs[steps:-1], refs[-1]
    seqs = 2 * steps
    z, core = place_ref[0] // 2, place_ref[0] % 2
    for step in range(steps):
        cols_s[0, step] = near[step][0]
    cols_s[1] = other_ref[...]
    total = jnp.zeros((gain_ref.shape[0], 1), jnp.float32)
    for m, ref in enumerate((query_ref, key_ref, value_ref)):
        rows = jnp.concatenate(
            [
                cols_s[
                    (core + head) % 2,
                    (z + steps - head % seqs // 2) % steps,
                    :,
                    (head // seqs * 3 + m) * HEAD_DIM : (head // seqs * 3 + m + 1) * HEAD_DIM,
                ]
                for head in range(heads)
            ],
            axis=1,
        ).astype(jnp.float32)
        total += jnp.sum(rows * ref[...].astype(jnp.float32), axis=1, keepdims=True)
        out_refs[m][...] = rows * gain_ref[...]
    out_refs[3][...] = total


def unpack_columns(place, gain_col, weights, near, other):
    rows, width = weights[0].shape
    vmem = pl.BlockSpec(memory_space=pltpu.VMEM)
    return pl.pallas_call(
        functools.partial(unpack_kernel, width // HEAD_DIM),
        in_specs=[pl.BlockSpec(memory_space=pltpu.SMEM)] + [vmem] * (5 + len(near)),
        out_specs=[vmem] * 4,
        out_shape=[jax.ShapeDtypeStruct((rows, width), jnp.float32)] * 3
        + [jax.ShapeDtypeStruct((rows, 1), jnp.float32)],
        scratch_shapes=[pltpu.VMEM((2,) + other.shape, other.dtype)],
        cost_estimate=SHORT,
        name="unpack_columns",
    )(place, gain_col, *weights, other, *near)


def unit_kernel(*refs):
    out_ref = refs[-1]
    tok = refs[0].shape[0]
    for slot, ref in enumerate(refs[:-1]):
        rows = ref[...].astype(jnp.float32)
        scale = lax.rsqrt(jnp.mean(rows * rows, axis=-1, keepdims=True) + NORM_EPS)
        out_ref[slot * tok : (slot + 1) * tok] = (rows * scale).astype(jnp.bfloat16)


def unit_tokens(slots):
    tok, width = slots[0].shape
    return pl.pallas_call(
        unit_kernel,
        out_shape=jax.ShapeDtypeStruct((len(slots) * tok, width), jnp.bfloat16),
        compiler_params=pltpu.CompilerParams(vmem_limit_bytes=16 * 2**20),
        cost_estimate=SHORT,
        name="unit_tokens",
    )(*slots)


def join_kernel(*refs):
    rows = refs[0].shape[0]
    for i, ref in enumerate(refs[:-1]):
        refs[-1][i * rows : (i + 1) * rows] = ref[...]


def join_rows(arrays):
    rows, width = arrays[0].shape
    vmem = pl.BlockSpec(memory_space=pltpu.VMEM)
    return pl.pallas_call(
        join_kernel,
        in_specs=[vmem] * len(arrays),
        out_specs=vmem,
        out_shape=jax.ShapeDtypeStruct((len(arrays) * rows, width), arrays[0].dtype),
        cost_estimate=SHORT,
        name="join_rows",
    )(*arrays)


def load_kernel(layout, *refs):
    pieces, out_ref, sem = refs[:-2], refs[-2], refs[-1]
    copies = [
        pltpu.make_async_copy(ref, out_ref.at[m, pl.ds(row, ref.shape[0])], sem.at[i])
        for i, (ref, (m, row)) in enumerate(zip(pieces, layout, strict=True))
    ]
    for copy in copies:
        copy.start()
    for copy in copies:
        copy.wait()


def load_weights(matrices):
    layout, pieces = [], []
    for m, matrix in enumerate(matrices):
        row = 0
        for piece in matrix:
            layout.append((m, row))
            pieces.append(piece)
            row += piece.shape[0]
    shape = (len(matrices), row, pieces[0].shape[1])
    return pl.pallas_call(
        functools.partial(load_kernel, tuple(layout)),
        in_specs=[pl.BlockSpec(memory_space=pl.ANY)] * len(pieces),
        out_specs=pl.BlockSpec(memory_space=pltpu.VMEM),
        out_shape=pltpu.VMEM(shape, pieces[0].dtype),
        scratch_shapes=[pltpu.SemaphoreType.DMA((len(pieces),))],
        cost_estimate=SHORT,
        compiler_params=pltpu.CompilerParams(vmem_limit_bytes=14 * 2**20),
        name="load_weights",
    )(*in_hbm(pieces))


def feed_kernel(call, aliased, *refs):
    shard_ref, tokens, grads, first_ref, down_ref = refs[0], refs[1:3], refs[3:5], refs[5], refs[6]
    refs = refs[7 + aliased :]
    part_near, part_other = refs[:2]
    all_refs = refs[2:9]
    tok_s, grad_s, hidden_s, gate_s, up_s, hidden_t, gate_t, up_t, down_s, sem = refs[9:]
    tok, width = tokens[0].shape
    shards, block = 4, down_ref.shape[1] // 4
    rows = pl.ds(2 * tok * call, 2 * tok)
    for c in range(2):
        tok_s[c * tok : (c + 1) * tok] = tokens[c][...]
        grad_s[c * tok : (c + 1) * tok] = grads[c][...]
    copies = [
        pltpu.make_async_copy(tok_s, all_refs[0].at[rows], sem.at[0]),
        pltpu.make_async_copy(grad_s, all_refs[1].at[rows], sem.at[1]),
    ]
    for copy in copies:
        copy.start()
    for b in range(shards):
        at = slice(b * block, (b + 1) * block)
        place = pl.ds(pl.multiple_of((shard_ref[0] ^ b) * block, block), block)
        gate_val = times_trans(tok_s[...], first_ref[0, at])
        up_val = times_trans(tok_s[...], first_ref[1, at])
        hidden_grad = times_trans(grad_s[...], down_ref[0, at])
        sigmoid_val = 1.0 / (1.0 + jnp.exp(-gate_val))
        silu_val = gate_val * sigmoid_val
        hidden = (silu_val * up_val).astype(jnp.bfloat16)
        gate_grad = (
            hidden_grad * up_val * (sigmoid_val + silu_val * (1.0 - sigmoid_val))
        ).astype(jnp.bfloat16)
        up_grad = (hidden_grad * silu_val).astype(jnp.bfloat16)
        for value, by_unit, by_token in (
            (hidden, hidden_t, hidden_s), (gate_grad, gate_t, gate_s), (up_grad, up_t, up_s)
        ):
            by_unit[place, :] = value.T
            by_token[:, at] = value
    late = [
        pltpu.make_async_copy(src, dst.at[:, rows], sem.at[2 + i])
        for i, (src, dst) in enumerate(zip((hidden_t, gate_t, up_t), all_refs[2:5], strict=True))
    ]
    for copy in late:
        copy.start()
    for c in range(4):
        at = slice(c * (width // 4), (c + 1) * (width // 4))
        part = dot_nn(gate_s[...], first_ref[0, :, at]) + dot_nn(up_s[...], first_ref[1, :, at])
        part_near[:, at] = part[:tok]
        part_other[:, at] = part[tok:].astype(jnp.bfloat16)
    for c in range(4):
        at = slice(c * (width // 4), (c + 1) * (width // 4))
        down = dot_nn(hidden_s[...], down_ref[0, :, at]).astype(jnp.bfloat16)
        down_s[0, :, at] = down[:tok]
        down_s[1, :, at] = down[tok:]
    last = [
        pltpu.make_async_copy(down_s.at[c], all_refs[5 + c].at[call], sem.at[5 + c])
        for c in range(2)
    ]
    for copy in last:
        copy.start()
    for copy in copies + late + last:
        copy.wait()


def feed_blocks(call, slots, shard, tokens, grads, first_two, down, whole):
    tok, width = tokens[0].shape
    units = down.shape[1]
    anywhere = pl.BlockSpec(memory_space=pl.ANY)
    vmem = pl.BlockSpec(memory_space=pltpu.VMEM)
    low, full = jnp.bfloat16, jnp.float32
    shapes = (
        [(slots * tok, width)] * 2
        + [(units, slots * tok)] * 3
        + [(slots // 2, tok, width)] * 2
    )
    whole = in_hbm(whole or [])
    out = pl.pallas_call(
        functools.partial(feed_kernel, call, len(whole)),
        in_specs=[pl.BlockSpec(memory_space=pltpu.SMEM)] + [vmem] * 6 + [anywhere] * len(whole),
        out_specs=[vmem] * 2 + [anywhere] * 7,
        out_shape=[jax.ShapeDtypeStruct((tok, width), full), jax.ShapeDtypeStruct((tok, width), low)]
        + [pltpu.HBM(shape, low) for shape in shapes],
        input_output_aliases={7 + i: 2 + i for i in range(len(whole))},
        scratch_shapes=[pltpu.VMEM((2 * tok, width), low)] * 2
        + [pltpu.VMEM((2 * tok, units), low)] * 3
        + [pltpu.VMEM((units, 2 * tok), low)] * 3
        + [pltpu.VMEM((2, tok, width), low), pltpu.SemaphoreType.DMA((7,))],
        compiler_params=pltpu.CompilerParams(vmem_limit_bytes=30 * 2**20),
        cost_estimate=SHORT,
        name="feed_blocks",
    )(
        shard,
        *tokens,
        *grads,
        *[pltpu.with_memory_space_constraint(weight, pltpu.VMEM) for weight in (first_two, down)],
        *whole,
    )
    return out[:2], out[2:]


def start_pieces(pieces, weight_s, sem):
    places, row = [], 0
    for i, ref in enumerate(pieces):
        at = pl.ds(row, ref.shape[0])
        copy = pltpu.make_async_copy(ref, weight_s.at[at], sem.at[i])
        copy.start()
        places.append((row, ref.shape[0], copy))
        row += ref.shape[0]
    return places


def project_kernel(index_ref, blocks_ref, input_ref, gain_ref, *refs):
    pieces, (middle_ref, normed_ref, scale_ref, weight_s, sem) = refs[:-5], refs[-5:]
    places = start_pieces(pieces, weight_s, sem)
    heads = blocks_ref.shape[0]
    rows = jnp.concatenate([blocks_ref[index_ref[i], :HEAD_DIM] for i in range(heads)]).T
    total = input_ref[...].astype(jnp.float32)
    for row, size, copy in places:
        copy.wait()
        total += dot_nn(rows[:, row : row + size], weight_s[row : row + size])
    scale = lax.rsqrt(jnp.mean(total * total, axis=-1, keepdims=True) + NORM_EPS)
    middle_ref[...] = total
    normed_ref[...] = (total * scale * gain_ref[...]).astype(jnp.bfloat16)
    scale_ref[...] = jnp.broadcast_to(scale, scale_ref.shape)


def project(index, blocks, inputs, gain, pieces):
    tok, width = inputs.shape
    vmem = pl.BlockSpec(memory_space=pltpu.VMEM)
    return pl.pallas_call(
        project_kernel,
        in_specs=[pl.BlockSpec(memory_space=pltpu.SMEM)]
        + [vmem] * 3
        + [pl.BlockSpec(memory_space=pl.ANY)] * len(pieces),
        out_specs=[vmem] * 3,
        out_shape=[
            jax.ShapeDtypeStruct((tok, width), jnp.float32),
            jax.ShapeDtypeStruct((tok, width), jnp.bfloat16),
            jax.ShapeDtypeStruct((tok, 128), jnp.float32),
        ],
        scratch_shapes=[
            pltpu.VMEM((HEADS * HEAD_DIM, width), jnp.bfloat16),
            pltpu.SemaphoreType.DMA((len(pieces),)),
        ],
        compiler_params=pltpu.CompilerParams(vmem_limit_bytes=18 * 2**20),
        cost_estimate=SHORT,
        name="project",
    )(index, blocks, inputs, gain, *in_hbm(pieces))


def token_grad_kernel(
    index_ref, own_ref, one_ref, two_ref, three_ref, middle_ref, scale_ref, gain_ref, grad_ref, *refs
):
    pieces, (middle_grad_ref, low_ref, out_ref, weight_s, sem) = refs[:-5], refs[-5:]
    places = start_pieces(pieces, weight_s, sem)
    normed_grad = own_ref[...]
    for ref in (one_ref, two_ref, three_ref):
        normed_grad += ref[...].astype(jnp.float32)
    tok = normed_grad.shape[0]
    scale = scale_ref[:, :1]
    unit = middle_ref[...] * scale
    gain_part = jnp.sum(normed_grad * unit, axis=0, keepdims=True)
    unit_grad = normed_grad * gain_ref[...]
    middle_grad = grad_ref[...].astype(jnp.float32) + scale * (
        unit_grad - unit * jnp.mean(unit_grad * unit, axis=-1, keepdims=True)
    )
    middle_grad_ref[...] = middle_grad
    low = middle_grad.astype(jnp.bfloat16)
    low_ref[...] = low
    grad_t = low.T
    for row, size, copy in places:
        copy.wait()
        out = dot_nn(weight_s[row : row + size], grad_t).astype(jnp.bfloat16)
        for i in range(size // HEAD_DIM):
            out_ref[index_ref[row // HEAD_DIM + i], :HEAD_DIM] = out[
                i * HEAD_DIM : (i + 1) * HEAD_DIM
            ]
    coarse = gain_part.astype(jnp.bfloat16)
    fine = (gain_part - coarse.astype(jnp.float32)).astype(jnp.bfloat16)
    wide = gain_part.shape[1] // out_ref.shape[0]
    for head in range(out_ref.shape[0]):
        at = slice(head * wide, (head + 1) * wide)
        row = jnp.concatenate([coarse[:, at], fine[:, at]], axis=1)
        out_ref[head, HEAD_DIM:] = jnp.broadcast_to(row, (EXTRA, tok))


def token_grad(index, sums, middle, scale, gain, output_grad, pieces):
    tok, width = middle.shape
    vmem = pl.BlockSpec(memory_space=pltpu.VMEM)
    return pl.pallas_call(
        token_grad_kernel,
        in_specs=[pl.BlockSpec(memory_space=pltpu.SMEM)]
        + [vmem] * 8
        + [pl.BlockSpec(memory_space=pl.ANY)] * len(pieces),
        out_specs=[vmem] * 3,
        out_shape=[
            jax.ShapeDtypeStruct((tok, width), jnp.float32),
            jax.ShapeDtypeStruct((tok, width), jnp.bfloat16),
            pltpu.HBM((HEADS, HEAD_DIM + EXTRA, tok), jnp.bfloat16),
        ],
        scratch_shapes=[
            pltpu.VMEM((HEADS * HEAD_DIM, width), jnp.bfloat16),
            pltpu.SemaphoreType.DMA((len(pieces),)),
        ],
        compiler_params=pltpu.CompilerParams(vmem_limit_bytes=18 * 2**20),
        cost_estimate=SHORT,
        name="token_grad",
    )(index, *sums, middle, scale, gain, output_grad, *in_hbm(pieces))


def feed_wgrad_kernel(gate_ref, up_ref, hidden_ref, tokens_ref, grads_ref, out_ref):
    tokens, grads = tokens_ref[...], grads_ref[...]
    out_ref[0, 0] = dot_nn(gate_ref[...], tokens).astype(jnp.bfloat16)
    out_ref[0, 1] = dot_nn(up_ref[...], tokens).astype(jnp.bfloat16)
    out_ref[0, 2] = dot_nn(hidden_ref[...], grads).astype(jnp.bfloat16)


def feed_wgrads(shards, gate_grad, up_grad, hidden, feed_low, span_grad):
    units, tokens = hidden.shape
    width = feed_low.shape[1]
    block = units // shards
    half = width // 2
    rows = pl.BlockSpec((block, tokens), lambda c, i: (i, 0))
    every = pl.BlockSpec((tokens, half), lambda c, i: (0, c))
    return pl.pallas_call(
        feed_wgrad_kernel,
        grid=(2, shards),
        in_specs=[rows] * 3 + [every] * 2,
        out_specs=pl.BlockSpec((1, 3, block, half), lambda c, i: (i, 0, 0, c)),
        out_shape=jax.ShapeDtypeStruct((shards, 3, block, width), jnp.bfloat16),
        compiler_params=pltpu.CompilerParams(vmem_limit_bytes=24 * 2**20),
        cost_estimate=SHORT,
        name="feed_wgrads",
    )(*in_hbm([gate_grad, up_grad, hidden, feed_low, span_grad]))


def output_wgrad_kernel(blocks, *refs):
    heads, grads, out_ref = refs[:4], refs[4 : 4 + blocks], refs[-1]
    tok = grads[0].shape[0]
    grad_rows = jnp.concatenate([ref[...] for ref in grads])
    for k in range(4):
        out_ref[k] = dot_nn(heads[k][...], grad_rows).astype(jnp.bfloat16)


def output_wgrad_parts(heads, grads):
    tok, width = grads[0].shape
    return pl.pallas_call(
        functools.partial(output_wgrad_kernel, len(grads)),
        out_shape=jax.ShapeDtypeStruct((4, HEAD_DIM, width), jnp.bfloat16),
        compiler_params=pltpu.CompilerParams(vmem_limit_bytes=14 * 2**20),
        cost_estimate=SHORT,
        name="output_wgrad",
    )(*heads, *grads)


def swap_cores(values):
    count = lax.axis_size("seq")
    return lax.ppermute(values, "seq", [(i, i ^ 1) for i in range(count)])


def from_chip(values, step):
    count = lax.axis_size("seq")
    return lax.ppermute(values, "seq", [((i + 2 * step) % count, i) for i in range(count)])


def from_shard(values, flip):
    return lax.ppermute(values, "shard", [(i, i ^ flip) for i in range(4)])


def both_cores(same):
    return [block for one in same for block in (one, swap_cores(one))]


def core_sum(near, other):
    return near.astype(F32) + swap_cores(other.astype(BF16)).astype(F32)


def after(token, values):
    return lax.optimization_barrier((values, token))[0]


def join(token, *values):
    return lax.optimization_barrier((token,) + values)[0]


def first_hops(block):
    return [from_shard(block, 1), from_shard(block, 2)]


def second_hops(first):
    rows = first[0].shape[0] // 2
    return [from_shard(first[0][:rows], 2), from_shard(first[1][rows:], 1)]


def scatter_shard_first(parts):
    rows = parts[3].shape[0] // 2
    low = parts[3].astype(BF16)
    return from_shard(low[:rows], 1), from_shard(low[rows:], 2)


def scatter_shard_last(parts, first):
    rows = parts[3].shape[0] // 2
    top, bottom = first
    one, two = parts[1].astype(F32), parts[2].astype(F32)
    one = jnp.concatenate([one[:rows], one[rows:] + bottom.astype(F32)])
    two = jnp.concatenate([two[:rows] + top.astype(F32), two[rows:]])
    return from_shard(one.astype(BF16), 1), from_shard(two.astype(BF16), 2)


def rotate_rows(front, back, cos_t, sin_t):
    return jnp.concatenate([front * cos_t - back * sin_t, back * cos_t + front * sin_t], axis=-2)


def per_device(
    layer_input,
    doc_lengths,
    norm_gain,
    query_weight,
    key_weight,
    value_weight,
    output_weight,
    feed_gain,
    gate_weight,
    up_weight,
    down_weight,
    output_grad,
):
    tok, width = layer_input.shape
    seqs, shards = lax.axis_size("seq"), lax.axis_size("shard")
    shard, seq = lax.axis_index("shard"), lax.axis_index("seq")
    span = tok * seqs
    half_head = HEAD_DIM // 2
    place = jnp.reshape(seq, (1,)).astype(jnp.int32)

    lanes = jnp.arange(span, dtype=jnp.int32)
    in_span = slot_block(lanes // tok, seq.astype(jnp.int32), seqs // 2) * tok + lanes % tok
    positions = jnp.arange(shards, dtype=jnp.int32)[:, None] * span + in_span[None]
    bounds = doc_bounds(doc_lengths, positions)
    exponent = -2.0 * jnp.arange(half_head, dtype=jnp.float32) / HEAD_DIM
    inverse = jnp.power(jnp.float32(ROPE_BASE), exponent)
    angles = positions.astype(F32)[:, None, :] * inverse[None, :, None]
    cos_all, sin_all = jnp.cos(angles), jnp.sin(angles)
    cos_own = lax.dynamic_index_in_dim(cos_all, shard, 0, keepdims=False)
    sin_own = lax.dynamic_index_in_dim(sin_all, shard, 0, keepdims=False)

    steps = seqs // 2
    z, core = seq // 2, seq % 2
    shard_at = jnp.reshape(shard, (1,)).astype(jnp.int32)
    gain_col = norm_gain.astype(F32)[:, None]
    heads_here = HEADS // seqs
    own_rows = query_weight.shape[0]
    attn_weights = (query_weight, key_weight, value_weight)
    slot = jnp.arange(HEADS, dtype=jnp.int32)

    packed = pack_columns(place, gain_col, attn_weights, seqs)
    point = join(jnp.zeros((), F32), packed)
    from_other = swap_cores(packed[1])
    gate_first = first_hops(after(point, gate_weight))
    col_blocks = []
    for step in range(steps):
        block = jnp.concatenate([packed[0, step], from_other[step]])
        col_blocks.append(from_chip(block, -step) if step else block)
    point = join(point, gate_first, col_blocks)
    col_block = jnp.concatenate(after(point, col_blocks))
    col_first = first_hops(col_block)
    own_input = after(point, layer_input)
    input_one, input_three = from_chip(own_input, 1), from_chip(own_input, -1)
    point = join(point, col_first, input_one, input_three)
    col_far = second_hops(after(point, col_first))
    input_two = from_chip(after(point, input_one), 1)
    input_slots = both_cores([own_input, after(point, input_one)])
    input_last = both_cores([after(point, input_three)])
    point = join(point, col_far, input_two, input_slots, input_last)
    input_slots += both_cores([after(point, input_two)]) + input_last
    rel_blocks = (
        (shard ^ (slot // seqs)) * seqs
        + (z + steps - slot % seqs // 2) % steps * 2
        + (core ^ (slot % 2))
    ).astype(jnp.int32)
    columns = order_blocks([col_block] + col_first + after(point, col_far), rel_blocks, own_rows)
    unit_low = unit_tokens(input_slots)
    qkv = lax.dot_general(
        columns, unit_low, (((0,), (1,)), ((), ())), preferred_element_type=F32
    ).reshape(shards, 3, HEAD_DIM, span)
    turned = rotate_rows(
        qkv[:, :2, :half_head], qkv[:, :2, half_head:], cos_own[None, None], sin_own[None, None]
    )
    qkv_low = jnp.concatenate([turned, qkv[:, 2:]], axis=1).astype(BF16)
    qkv_low = qkv_low.reshape(shards, 3 * HEAD_DIM, span)
    gate_far = second_hops(after(point, gate_first))
    output_own = after(point, output_weight)
    output_one, output_three = from_chip(output_own, 1), from_chip(output_own, -1)
    up_top, up_bottom = up_weight[: up_weight.shape[0] // 2], up_weight[up_weight.shape[0] // 2 :]
    up_first = [from_shard(after(point, up_top), flip) for flip in (1, 2)]
    point = join(point, qkv_low, gate_far, output_one, output_three, up_first)

    head_qkv = lax.all_to_all(
        after(point, qkv_low), "shard", split_axis=0, concat_axis=0, tiled=True
    )
    output_two = from_chip(after(point, output_one), 1)
    own_grad = after(point, output_grad)
    grad_one = from_chip(own_grad, 1)
    up_first += [from_shard(after(point, up_bottom), flip) for flip in (1, 2)]
    point = join(point, head_qkv, output_two, grad_one, up_first)
    output_own = jnp.concatenate(after(point, [output_own, output_one, output_two, output_three]))
    output_first = first_hops(output_own)
    output_swapped = [swap_cores(output_own)]
    grad_two, grad_three = from_chip(after(point, grad_one), 1), from_chip(own_grad, -1)
    gain_rows = jnp.pad(feed_gain[None, :], ((0, EXTRA - 1), (0, tok - own_rows)))
    head_out, head_low, out_blocks, lse = attend(
        after(point, head_qkv), gain_rows, tok, place, bounds
    )
    point = join(point, out_blocks, output_first, output_swapped, grad_two, grad_three)
    token_blocks = lax.all_to_all(
        after(point, out_blocks), ("shard", "seq"), split_axis=0, concat_axis=0, tiled=True
    )
    output_far = second_hops(after(point, output_first))
    up_far = [from_shard(after(point, up_first[0]), 2), from_shard(after(point, up_first[3]), 1)]
    output_swapped += [swap_cores(piece) for piece in after(point, output_first)]
    point = join(point, token_blocks, output_far, up_far, output_swapped)
    gain_two = token_blocks[:, HEAD_DIM, :own_rows].astype(F32).reshape(1, width)
    output_swapped += [swap_cores(piece) for piece in after(point, output_far)]
    output_pieces = [output_own] + output_first + output_far + output_swapped
    rel_heads = (
        (shard ^ (slot // steps % shards)) * seqs
        + (z + slot % steps) % steps * 2
        + (core ^ (slot // (HEADS // 2)))
    ).astype(jnp.int32)
    middle, normed_two, scale_two = project(
        rel_heads, after(point, token_blocks), layer_input, gain_two, output_pieces
    )
    point = join(point, normed_two)

    own_tokens = after(point, normed_two)
    tokens_one, tokens_three = from_chip(own_tokens, 1), from_chip(own_tokens, -1)
    down_first = first_hops(after(point, down_weight))
    grad_slots = both_cores(after(point, [output_grad, grad_one, grad_two, grad_three]))
    first_two = load_weights(
        [
            after(point, [gate_weight, *gate_first, *gate_far]),
            [up_weight, up_first[0], up_first[2], up_first[1], up_first[3], *up_far],
        ]
    )
    point = join(point, tokens_one, tokens_three, down_first, grad_slots, first_two)
    tokens_two = from_chip(after(point, tokens_one), 1)
    down_far = second_hops(after(point, down_first))
    feed_slots = both_cores([own_tokens, after(point, tokens_one)])
    feed_last = both_cores([after(point, tokens_three)])
    point = join(point, tokens_two, down_far, feed_slots, feed_last)
    feed_slots += both_cores([after(point, tokens_two)]) + feed_last
    down_here = load_weights([[down_weight, *down_first, *after(point, down_far)]])
    order = (2, 1, 3, 0)

    def feed(step, tokens, whole):
        here = slice(2 * step, 2 * step + 2)
        return feed_blocks(
            order.index(step), seqs, shard_at, tokens, grad_slots[here], first_two, down_here, whole
        )

    parts_two, whole = feed(2, feed_slots[4:6], None)
    sum_two = core_sum(*parts_two).astype(BF16)
    point = join(point, sum_two)
    arrived_two = from_chip(after(point, sum_two), -2)
    parts_one, whole = feed(1, after(point, feed_slots[2:4]), whole)
    parts_three, whole = feed(3, feed_slots[6:8], whole)
    point = join(point, arrived_two, parts_one, parts_three)
    sum_one = core_sum(*after(point, parts_one)).astype(BF16)
    sum_three = core_sum(*after(point, parts_three)).astype(BF16)
    point = join(point, sum_one, sum_three)
    arrived_one = from_chip(after(point, sum_one), -1)
    arrived_three = from_chip(after(point, sum_three), 1)
    parts_own, whole = feed(0, after(point, feed_slots[0:2]), whole)
    feed_low, span_grad, hidden, gate_grad, up_grad, down_near, down_other = whole
    feed_wparts = feed_wgrads(shards, gate_grad, up_grad, hidden, feed_low, span_grad)
    head_slots = [
        lax.dynamic_index_in_dim(after(point, head_low), shard ^ k, 0, keepdims=False)
        for k in range(4)
    ]
    head_slots = head_slots[:1] + [from_shard(head_slots[k], k) for k in range(1, 4)]
    point = join(point, parts_own, feed_wparts, arrived_one, arrived_three, head_slots)
    sum_own = core_sum(*after(point, parts_own))
    middle_grad, attend_grad, head_grad = token_grad(
        rel_heads,
        [sum_own, arrived_one, arrived_two, arrived_three],
        middle,
        scale_two,
        gain_two,
        output_grad,
        output_pieces,
    )
    point = join(point, head_grad)

    out_grad_blocks = lax.all_to_all(
        after(point, head_grad), ("shard", "seq"), split_axis=0, concat_axis=0, tiled=True
    )
    feed_wsum = lax.psum_scatter(
        after(point, feed_wparts).reshape(-1, width), "shard", scatter_dimension=0, tiled=True
    ).reshape(3, -1, width)
    own_agrad = after(point, attend_grad)
    agrad_one = from_chip(own_agrad, 1)
    down_all = core_sum(after(point, down_near), down_other).astype(BF16)
    down_sums = [down_all[order.index(step)] for step in range(steps)]
    point = join(point, out_grad_blocks, agrad_one, down_sums)
    agrad_three = from_chip(after(point, own_agrad), -1)
    down_two = from_chip(after(point, down_sums[2]), -1)
    down_three = from_chip(after(point, down_sums[3]), 1)
    back = attend_back(
        head_qkv, lse, head_out, after(point, out_grad_blocks), cos_all, sin_all, tok, place, bounds
    )
    point = join(point, back, agrad_three, down_two, down_three)
    span_back = lax.all_to_all(
        after(point, back), "shard", split_axis=0, concat_axis=0, tiled=True
    ).reshape(heads_here * 3 * HEAD_DIM, span)
    agrad_two = from_chip(after(point, agrad_one), 1)
    down_one = from_chip(
        (down_sums[1].astype(F32) + after(point, down_two).astype(F32)).astype(BF16), -1
    )
    agrad_slots = both_cores([after(point, own_agrad), agrad_one, agrad_two, agrad_three])
    out_part = output_wgrad_parts(head_slots, agrad_slots)
    point = join(point, span_back, down_one, out_part)
    layer_output = (
        middle
        + down_sums[0].astype(F32)
        + after(point, down_one).astype(F32)
        + down_three.astype(F32)
    ).astype(BF16)

    span_back = after(point, span_back)
    cols_part = lax.dot_general(
        unit_low, span_back, (((0,), (1,)), ((), ())), preferred_element_type=F32
    ).reshape(shards, seqs * own_rows, heads_here * 3 * HEAD_DIM)
    cols_parts = [
        lax.dynamic_index_in_dim(cols_part, shard ^ k, 0, keepdims=False) for k in range(4)
    ]
    cols_first = scatter_shard_first(cols_parts)
    unit_sums = []
    for step in range(steps):
        lanes_here = after(cols_part, span_back)[:, 2 * step * tok : 2 * (step + 1) * tok]
        part = lax.dot_general(
            lanes_here, columns, (((0,), (1,)), ((), ())), preferred_element_type=F32
        )
        unit_sums.append(core_sum(part[:tok], part[tok:]))
    point = join(point, cols_first, unit_sums, layer_output)
    unit_two = from_chip(after(point, unit_sums[2]).astype(BF16), -1)
    unit_three = from_chip(after(point, unit_sums[3]).astype(BF16), 1)
    cols_last = scatter_shard_last(cols_parts, after(point, cols_first))
    point = join(point, unit_two, unit_three, cols_last)
    unit_one = from_chip((unit_sums[1] + after(point, unit_two).astype(F32)).astype(BF16), -1)
    out_parts = [after(point, out_part)[k] for k in range(4)]
    out_first = scatter_shard_first(out_parts)
    cols_spread = spread_columns(place, cols_parts[0], *after(point, cols_last), steps)
    point = join(point, unit_one, cols_spread, out_first)
    cols_same = [cols_spread[0]] + [
        from_chip(after(point, cols_spread)[step], -step) for step in range(1, steps)
    ]
    out_last = scatter_shard_last(out_parts, after(point, out_first))
    unit_grad = unit_sums[0] + after(point, unit_one).astype(F32) + unit_three.astype(F32)
    inputs = layer_input.astype(F32)
    scale_one = lax.rsqrt(jnp.mean(inputs * inputs, axis=-1, keepdims=True) + NORM_EPS)
    unit_rows = inputs * scale_one
    input_grad = (
        middle_grad
        + scale_one * (unit_grad - unit_rows * jnp.mean(unit_grad * unit_rows, axis=-1, keepdims=True))
    ).astype(BF16)
    gate_wgrad, up_wgrad, down_wgrad = [
        after(point, feed_wsum)[m].astype(F32) for m in range(3)
    ]
    gain_rows_back = out_grad_blocks[:, HEAD_DIM].astype(F32)
    gain_two_out = jnp.sum(
        gain_rows_back[:, :own_rows] + gain_rows_back[:, own_rows : 2 * own_rows], axis=0
    )
    point = join(
        point, cols_same, out_last, input_grad, gate_wgrad, up_wgrad, down_wgrad, gain_two_out
    )
    cols_same = after(point, cols_same)
    cols_other = swap_cores(jnp.stack([block[1] for block in cols_same]))
    query_wgrad, key_wgrad, value_wgrad, gain_one_out = unpack_columns(
        place, gain_col, attn_weights, cols_same, cols_other
    )
    out_one, out_two = after(point, out_last)
    output_wgrad = out_parts[0].astype(F32) + out_one.astype(F32) + out_two.astype(F32)
    return (
        layer_output,
        input_grad,
        gain_one_out.reshape(-1),
        query_wgrad,
        key_wgrad,
        value_wgrad,
        output_wgrad,
        gain_two_out,
        gate_wgrad,
        up_wgrad,
        down_wgrad,
    )


def solution(mesh):
    shards, seqs = mesh.shape["shard"], mesh.shape["seq"]
    body = per_device if shards == 4 and shards * seqs == HEADS else per_device_any
    return jax.shard_map(
        body,
        mesh=mesh,
        in_specs=(
            P(("shard", "seq"), None),
            P(),
            P(("shard", "seq")),
            P(("shard", "seq"), None),
            P(("shard", "seq"), None),
            P(("shard", "seq"), None),
            P(("shard", "seq"), None),
            P(("shard", "seq")),
            P(("shard", "seq"), None),
            P(("shard", "seq"), None),
            P(("shard", "seq"), None),
            P(("shard", "seq"), None),
        ),
        out_specs=(
            P(("shard", "seq"), None),
            P(("shard", "seq"), None),
            P(("shard", "seq")),
            P(("shard", "seq"), None),
            P(("shard", "seq"), None),
            P(("shard", "seq"), None),
            P(("shard", "seq"), None),
            P(("shard", "seq")),
            P(("shard", "seq"), None),
            P(("shard", "seq"), None),
            P(("shard", "seq"), None),
        ),
        check_vma=False,
    )
```

```python
import functools
import math

import jax
import jax.numpy as jnp
from jax import lax
from jax.experimental import pallas as pl
from jax.experimental.pallas import tpu as pltpu
from jax.sharding import PartitionSpec as P

HEAD_DIM = 64


NORM_EPS = 1e-05
ROPE_BASE = 130000.0


def rope_tables(positions, width):
    half_width = width // 2
    exponent = -2.0 * jnp.arange(half_width, dtype=jnp.float32) / width
    inverse = jnp.power(jnp.float32(ROPE_BASE), exponent)
    angles = positions.astype(jnp.float32)[:, None] * inverse[None, :]
    return (jnp.cos(angles), jnp.sin(angles))


def rotate(values, cos_table, sin_table):
    half_width = values.shape[-1] // 2
    front = values[..., :half_width]
    back_half = values[..., half_width:]
    cos_wide = cos_table[:, None, :]
    sin_wide = sin_table[:, None, :]
    return jnp.concatenate(
        [front * cos_wide - back_half * sin_wide, back_half * cos_wide + front * sin_wide], axis=-1
    )


def unrotate(values, cos_table, sin_table):
    half_width = values.shape[-1] // 2
    front = values[..., :half_width]
    back_half = values[..., half_width:]
    cos_wide = cos_table[:, None, :]
    sin_wide = sin_table[:, None, :]
    return jnp.concatenate(
        [front * cos_wide + back_half * sin_wide, back_half * cos_wide - front * sin_wide], axis=-1
    )


def doc_numbers(doc_lengths, positions):
    doc_ends = jnp.cumsum(doc_lengths)
    return jnp.sum((doc_ends[:, None] <= positions[None, :]).astype(jnp.int32), axis=0)


def normalize(values, gain_vec):
    scale_row = lax.rsqrt(jnp.mean(values * values, axis=-1, keepdims=True) + NORM_EPS)
    return (values * scale_row * gain_vec, scale_row)


def norm_back(grad_in, values, scale_row, gain_vec):
    unit_rows = values * scale_row
    gain_grad = jnp.sum(grad_in * unit_rows, axis=0)
    unit_grad = grad_in * gain_vec
    value_grad = scale_row * (
        unit_grad - unit_rows * jnp.mean(unit_grad * unit_rows, axis=-1, keepdims=True)
    )
    return (value_grad, gain_grad)


def times_trans(lhs_mat, rhs_mat):
    return lax.dot_general(
        lhs_mat, rhs_mat, (((1,), (1,)), ((), ())), preferred_element_type=jnp.float32
    )


def trans_times(lhs_mat, rhs_mat):
    return lax.dot_general(
        lhs_mat, rhs_mat, (((0,), (0,)), ((), ())), preferred_element_type=jnp.float32
    )


def per_device_any(
    layer_input,
    doc_lengths,
    norm_gain,
    query_weight,
    key_weight,
    value_weight,
    output_weight,
    feed_gain,
    gate_weight,
    up_weight,
    down_weight,
    output_grad,
):
    tok_rows = layer_input.shape[0]
    width = layer_input.shape[1]
    seq_count = lax.axis_size("seq")
    shard_count = lax.axis_size("shard")
    span_len = tok_rows * seq_count
    stream_len = span_len * shard_count
    span_start = lax.axis_index("shard") * span_len
    own_positions = (
        span_start + lax.axis_index("seq") * tok_rows + jnp.arange(tok_rows, dtype=jnp.int32)
    )
    span_positions = span_start + jnp.arange(span_len, dtype=jnp.int32)
    all_positions = jnp.arange(stream_len, dtype=jnp.int32)
    key_docs = doc_numbers(doc_lengths, all_positions)
    query_docs = lax.dynamic_slice_in_dim(key_docs, span_start, span_len)
    score_scale = HEAD_DIM ** (-0.5)
    gathered = (
        lax.all_gather(query_weight, ("shard", "seq"), axis=0, tiled=True),
        lax.all_gather(key_weight, ("shard", "seq"), axis=0, tiled=True),
        lax.all_gather(value_weight, ("shard", "seq"), axis=0, tiled=True),
        lax.all_gather(output_weight, ("shard", "seq"), axis=0, tiled=True),
        lax.all_gather(norm_gain, ("shard", "seq"), axis=0, tiled=True),
        lax.all_gather(feed_gain, ("shard", "seq"), axis=0, tiled=True),
    )
    query_full, key_full, value_full, output_full = (
        gathered[0],
        gathered[1],
        gathered[2],
        gathered[3],
    )
    gain_one = gathered[4].astype(jnp.float32)
    gain_two = gathered[5].astype(jnp.float32)
    inputs = layer_input.astype(jnp.float32)
    normed, scale_one = normalize(inputs, gain_one)
    normed_low = normed.astype(jnp.bfloat16)
    own_cos, own_sin = rope_tables(own_positions, HEAD_DIM)
    query_proj = jnp.dot(normed_low, query_full, preferred_element_type=jnp.float32)
    key_proj = jnp.dot(normed_low, key_full, preferred_element_type=jnp.float32)
    value_proj = jnp.dot(normed_low, value_full, preferred_element_type=jnp.float32)
    query_rot = rotate(query_proj.reshape(tok_rows, -1, HEAD_DIM), own_cos, own_sin).reshape(
        tok_rows, width
    )
    key_rot = rotate(key_proj.reshape(tok_rows, -1, HEAD_DIM), own_cos, own_sin).reshape(
        tok_rows, width
    )
    stacked = jnp.stack(
        [
            query_rot.astype(jnp.bfloat16),
            key_rot.astype(jnp.bfloat16),
            value_proj.astype(jnp.bfloat16),
        ]
    )
    head_triple = lax.all_to_all(stacked, "seq", split_axis=2, concat_axis=1, tiled=True)
    head_width = head_triple.shape[2]
    heads_dev = head_width // HEAD_DIM
    head_query = head_triple[0].reshape(span_len, heads_dev, HEAD_DIM)
    key_value = lax.all_gather(head_triple[1:], "shard", axis=1, tiled=True)
    key_block = math.gcd(stream_len, max(512, stream_len // 16))
    block_count = stream_len // key_block
    key_blocks = key_value[0].reshape(block_count, key_block, heads_dev, HEAD_DIM)
    value_blocks = key_value[1].reshape(block_count, key_block, heads_dev, HEAD_DIM)
    pos_blocks = all_positions.reshape(block_count, key_block)
    doc_blocks = key_docs.reshape(block_count, key_block)

    def block_scores(key_blk, key_pos, key_doc):
        scores = (
            jnp.einsum("qhd,khd->hqk", head_query, key_blk, preferred_element_type=jnp.float32)
            * score_scale
        )
        allowed = (key_pos[None, :] <= span_positions[:, None]) & (
            key_doc[None, :] == query_docs[:, None]
        )
        return jnp.where(allowed[None], scores, -jnp.inf)

    def total_step(state_pair, pieces):
        run_max, run_sum = state_pair
        scores = block_scores(pieces[0], pieces[1], pieces[2])
        new_max = jnp.maximum(run_max, jnp.max(scores, axis=-1))
        new_sum = run_sum * jnp.exp(run_max - new_max) + jnp.sum(
            jnp.exp(scores - new_max[..., None]), axis=-1
        )
        return ((new_max, new_sum), None)

    start_max = jnp.full((heads_dev, span_len), -1e30, jnp.float32)
    start_sum = jnp.zeros((heads_dev, span_len), jnp.float32)
    totals, unused = lax.scan(
        total_step, (start_max, start_sum), (key_blocks, pos_blocks, doc_blocks)
    )
    log_total = totals[0] + jnp.log(totals[1])

    def output_step(accum, pieces):
        scores = block_scores(pieces[0], pieces[2], pieces[3])
        probs = jnp.exp(scores - log_total[..., None]).astype(jnp.bfloat16)
        return (
            accum
            + jnp.einsum("hqk,khd->qhd", probs, pieces[1], preferred_element_type=jnp.float32),
            None,
        )

    start_acc = jnp.zeros((span_len, heads_dev, HEAD_DIM), jnp.float32)
    head_out32, unused = lax.scan(
        output_step, start_acc, (key_blocks, value_blocks, pos_blocks, doc_blocks)
    )
    head_out = head_out32.reshape(span_len, head_width).astype(jnp.bfloat16)
    token_out = lax.all_to_all(head_out, "seq", split_axis=0, concat_axis=1, tiled=True)
    middle = inputs + jnp.dot(token_out, output_full, preferred_element_type=jnp.float32)
    normed_two, scale_two = normalize(middle, gain_two)
    feed_low = normed_two.astype(jnp.bfloat16)
    feed_mats = (
        lax.all_gather(gate_weight, ("shard", "seq"), axis=0, tiled=True),
        lax.all_gather(up_weight, ("shard", "seq"), axis=0, tiled=True),
        lax.all_gather(down_weight, ("shard", "seq"), axis=0, tiled=True),
    )
    gate_full, up_full, down_full = (feed_mats[0], feed_mats[1], feed_mats[2])
    gate_val = times_trans(feed_low, gate_full)
    up_val = times_trans(feed_low, up_full)
    hidden = (jax.nn.silu(gate_val) * up_val).astype(jnp.bfloat16)
    down_val = jnp.dot(hidden, down_full, preferred_element_type=jnp.float32)
    layer_output = (middle + down_val).astype(jnp.bfloat16)
    hidden_grad = times_trans(output_grad, down_full)
    sigmoid_val = jax.nn.sigmoid(gate_val)
    gate_grad = (
        hidden_grad * up_val * (sigmoid_val * (1.0 + gate_val * (1.0 - sigmoid_val)))
    ).astype(jnp.bfloat16)
    up_grad = (hidden_grad * jax.nn.silu(gate_val)).astype(jnp.bfloat16)
    feed_grad = jnp.dot(gate_grad, gate_full, preferred_element_type=jnp.float32) + jnp.dot(
        up_grad, up_full, preferred_element_type=jnp.float32
    )
    feed_sums = lax.psum_scatter(
        jnp.stack(
            [
                trans_times(gate_grad, feed_low),
                trans_times(up_grad, feed_low),
                trans_times(hidden, output_grad),
            ],
            axis=1,
        ),
        ("shard", "seq"),
        scatter_dimension=0,
        tiled=True,
    )
    middle_norm_grad, gain_two_grad = norm_back(feed_grad, middle, scale_two, gain_two)
    middle_grad = output_grad.astype(jnp.float32) + middle_norm_grad
    attend_grad = middle_grad.astype(jnp.bfloat16)
    output_term = trans_times(token_out, attend_grad)
    token_out_grad = times_trans(attend_grad, output_full).astype(jnp.bfloat16)
    head_out_grad = lax.all_to_all(
        token_out_grad, "seq", split_axis=1, concat_axis=0, tiled=True
    ).reshape(span_len, heads_dev, HEAD_DIM)
    row_dots = jnp.transpose(jnp.sum(head_out_grad.astype(jnp.float32) * head_out32, axis=-1))

    def grad_step(query_acc, pieces):
        key_blk, value_blk, key_pos, key_doc = pieces
        scores = block_scores(key_blk, key_pos, key_doc)
        probs = jnp.exp(scores - log_total[..., None])
        prob_grad = jnp.einsum(
            "qhd,khd->hqk", head_out_grad, value_blk, preferred_element_type=jnp.float32
        )
        score_grad = (probs * (prob_grad - row_dots[..., None])).astype(jnp.bfloat16)
        query_next = query_acc + score_scale * jnp.einsum(
            "hqk,khd->qhd", score_grad, key_blk, preferred_element_type=jnp.float32
        )
        key_part = score_scale * jnp.einsum(
            "hqk,qhd->khd", score_grad, head_query, preferred_element_type=jnp.float32
        )
        value_part = jnp.einsum(
            "hqk,qhd->khd",
            probs.astype(jnp.bfloat16),
            head_out_grad,
            preferred_element_type=jnp.float32,
        )
        return (query_next, (key_part, value_part))

    query_grad, block_grads = lax.scan(
        grad_step, start_acc, (key_blocks, value_blocks, pos_blocks, doc_blocks)
    )
    pair_grads = jnp.stack(
        [
            block_grads[0].reshape(stream_len, head_width),
            block_grads[1].reshape(stream_len, head_width),
        ]
    )
    own_pair = lax.psum_scatter(
        pair_grads.astype(jnp.bfloat16), "shard", scatter_dimension=1, tiled=True
    ).astype(jnp.float32)
    span_cos, span_sin = rope_tables(span_positions, HEAD_DIM)
    query_back = unrotate(query_grad, span_cos, span_sin).reshape(span_len, head_width)
    key_back = unrotate(
        own_pair[0].reshape(span_len, heads_dev, HEAD_DIM), span_cos, span_sin
    ).reshape(span_len, head_width)
    back_stack = jnp.stack([query_back, key_back, own_pair[1]]).astype(jnp.bfloat16)
    token_grads = lax.all_to_all(back_stack, "seq", split_axis=1, concat_axis=2, tiled=True)
    norm_grad = (
        times_trans(token_grads[0], query_full)
        + times_trans(token_grads[1], key_full)
        + times_trans(token_grads[2], value_full)
    )
    input_norm_grad, gain_one_grad = norm_back(norm_grad, inputs, scale_one, gain_one)
    input_grad = (middle_grad + input_norm_grad).astype(jnp.bfloat16)
    query_term = trans_times(normed_low, token_grads[0])
    key_term = trans_times(normed_low, token_grads[1])
    value_term = trans_times(normed_low, token_grads[2])
    summed = (
        lax.psum_scatter(query_term, ("shard", "seq"), scatter_dimension=0, tiled=True),
        lax.psum_scatter(key_term, ("shard", "seq"), scatter_dimension=0, tiled=True),
        lax.psum_scatter(value_term, ("shard", "seq"), scatter_dimension=0, tiled=True),
        lax.psum_scatter(output_term, ("shard", "seq"), scatter_dimension=0, tiled=True),
        lax.psum_scatter(gain_one_grad, ("shard", "seq"), scatter_dimension=0, tiled=True),
        lax.psum_scatter(gain_two_grad, ("shard", "seq"), scatter_dimension=0, tiled=True),
    )
    query_wgrad, key_wgrad, value_wgrad = (summed[0], summed[1], summed[2])
    output_wgrad, gain_one_out, gain_two_out = (summed[3], summed[4], summed[5])
    return (
        layer_output,
        input_grad,
        gain_one_out,
        query_wgrad,
        key_wgrad,
        value_wgrad,
        output_wgrad,
        gain_two_out,
        feed_sums[:, 0],
        feed_sums[:, 1],
        feed_sums[:, 2],
    )


HEADS = 32
EXTRA = 16
BF16 = jnp.bfloat16
F32 = jnp.float32


SHORT = pl.CostEstimate(flops=0, bytes_accessed=0, transcendentals=0)


def in_hbm(arrays):
    return [pltpu.with_memory_space_constraint(array, pltpu.HBM) for array in arrays]


def dot_nn(lhs_mat, rhs_mat):
    return lax.dot_general(
        lhs_mat, rhs_mat, (((1,), (0,)), ((), ())), preferred_element_type=jnp.float32
    )


def allowed_pairs(i, j, keys, cols, span, start_ref, same):
    shape = (keys.stop - keys.start, cols.stop - cols.start)
    k_pos = j * span + keys.start + lax.broadcasted_iota(jnp.int32, shape, 0)
    begun = k_pos >= start_ref[i][:, cols]
    if not same:
        return begun
    q_pos = i * span + cols.start + lax.broadcasted_iota(jnp.int32, shape, 1)
    return (k_pos <= q_pos) & begun


def own_span_parts(span):
    half = span // 2
    return (slice(0, half), slice(0, half)), (slice(0, span), slice(half, span))


def fwd_kernel(tok, shard_ref, lo_ref, full_ref, start_ref, qkv_ref, gain_ref, out_ref, low_ref, blocks_ref,
               lse_ref, k_nat, m_s, l_s, acc_s):
    i = pl.program_id(0)
    spans, rows, span = qkv_ref.shape
    slots = span // tok
    scale2 = HEAD_DIM ** -0.5 * math.log2(math.e)

    @pl.when(i == 0)
    def _():
        for s in range(spans):
            k_nat[pl.ds(s * span, span), :] = qkv_ref[s, HEAD_DIM : 2 * HEAD_DIM, :].T

    m_s[...] = jnp.full_like(m_s, -1e30)
    l_s[...] = jnp.zeros_like(l_s)
    acc_s[...] = jnp.zeros_like(acc_s)

    def step(j, masked, same=False, keys=slice(0, span), cols=slice(0, span)):
        k_rows = pl.ds(pl.multiple_of(j * span + keys.start, 128), keys.stop - keys.start)
        s_t = dot_nn(k_nat[k_rows, :], qkv_ref[i, :HEAD_DIM, cols]) * scale2
        if masked:
            s_t = jnp.where(allowed_pairs(i, j, keys, cols, span, start_ref, same), s_t, -jnp.inf)
        m_old = m_s[:, cols]
        m_new = jnp.maximum(m_old, jnp.max(s_t, axis=0, keepdims=True))
        alpha = jnp.exp2(m_old - m_new)
        p_t = jnp.exp2(s_t - m_new)
        l_s[:, cols] = l_s[:, cols] * alpha + jnp.sum(p_t, axis=0, keepdims=True)
        m_s[:, cols] = m_new
        acc_s[:, cols] = acc_s[:, cols] * alpha + dot_nn(
            qkv_ref[j, 2 * HEAD_DIM :, keys], p_t.astype(jnp.bfloat16)
        )

    def loop_body(masked):
        def body(j, carry):
            step(j, masked)
            return carry

        return body

    lax.fori_loop(lo_ref[i], full_ref[i], loop_body(True), 0)
    lax.fori_loop(full_ref[i], i, loop_body(False), 0)
    for keys, cols in own_span_parts(span):
        step(i, True, True, keys, cols)
    out = acc_s[...] / l_s[...]
    out_ref[0] = out
    low = out.astype(jnp.bfloat16)
    low_ref[i ^ shard_ref[0]] = low
    lse_ref[0] = m_s[...] + jnp.log2(l_s[...])
    for slot in range(slots):
        blocks_ref[slot, :HEAD_DIM] = low[:, slot * tok : (slot + 1) * tok]
        blocks_ref[slot, HEAD_DIM:] = gain_ref[...]


def bwd_kernel(tok, hi_ref, full_ref, start_ref, qkv_ref, lse_ref, out_hbm, dob_ref,
               cos_ref, sin_ref, back_ref, dq_s, dk_s, dv_s, do_s, di_s, out_ref, sem):
    j = pl.program_id(0)
    spans, rows, span = qkv_ref.shape
    slots = span // tok
    scale = HEAD_DIM ** -0.5
    scale2 = scale * math.log2(math.e)

    @pl.when(j == 0)
    def _():
        copy = pltpu.make_async_copy(out_hbm, out_ref, sem)
        copy.start()
        dq_s[...] = jnp.zeros_like(dq_s)
        for s in range(spans):
            for slot in range(slots):
                do_s[s, :, slot * tok : (slot + 1) * tok] = dob_ref[s * slots + slot, :HEAD_DIM]
        copy.wait()
        for s in range(spans):
            di_s[s] = jnp.sum(do_s[s].astype(jnp.float32) * out_ref[s], axis=0, keepdims=True)

    k_nat = qkv_ref[j, HEAD_DIM : 2 * HEAD_DIM, :].T
    v_nat = qkv_ref[j, 2 * HEAD_DIM :, :].T
    dk_s[...] = jnp.zeros_like(dk_s)
    dv_s[...] = jnp.zeros_like(dv_s)

    def step(i, masked, same=False, keys=slice(0, span), cols=slice(0, span)):
        q_t = qkv_ref[i, :HEAD_DIM, cols]
        p_t = jnp.exp2(dot_nn(k_nat[keys], q_t) * scale2 - lse_ref[i][:, cols])
        if masked:
            p_t = jnp.where(allowed_pairs(i, j, keys, cols, span, start_ref, same), p_t, 0.0)
        do_t = do_s[i, :, cols]
        dv_s[:, keys] += times_trans(do_t, p_t.astype(jnp.bfloat16))
        ds_t = (p_t * (dot_nn(v_nat[keys], do_t) - di_s[i][:, cols])).astype(jnp.bfloat16)
        dk_s[:, keys] += times_trans(q_t, ds_t)
        dq_s[i, :, cols] += dot_nn(qkv_ref[j, HEAD_DIM : 2 * HEAD_DIM, keys], ds_t)

    for keys, cols in own_span_parts(span):
        step(j, True, True, keys, cols)

    def body(i, carry):
        whole = full_ref[i] <= j

        @pl.when(whole)
        def _():
            step(i, False)

        @pl.when(jnp.logical_not(whole))
        def _():
            step(i, True)

        return carry

    lax.fori_loop(j + 1, hi_ref[j], body, 0)

    def turned_back(grad):
        front, back_half = grad[: HEAD_DIM // 2], grad[HEAD_DIM // 2 :]
        cos_t, sin_t = cos_ref[0], sin_ref[0]
        return jnp.concatenate(
            [front * cos_t + back_half * sin_t, back_half * cos_t - front * sin_t], axis=0
        ).astype(jnp.bfloat16)

    back_ref[0, :HEAD_DIM] = turned_back(dq_s[j] * scale)
    back_ref[0, HEAD_DIM : 2 * HEAD_DIM] = turned_back(dk_s[...] * scale)
    back_ref[0, 2 * HEAD_DIM :] = dv_s[...].astype(jnp.bfloat16)


def doc_bounds(doc_lengths, positions):
    spans, span = positions.shape
    ends = jnp.cumsum(doc_lengths)
    over = ends[:, None, None] <= positions[None]
    start = jnp.max(jnp.where(over, ends[:, None, None], 0), axis=0).astype(jnp.int32)
    stop = jnp.min(jnp.where(over, spans * span, ends[:, None, None]), axis=0).astype(jnp.int32)
    first = jnp.min(start, axis=1) // span
    whole = jnp.minimum(
        (jnp.max(start, axis=1) + span - 1) // span, jnp.arange(spans, dtype=jnp.int32)
    )
    last = (jnp.max(stop, axis=1) + span - 1) // span
    return start[:, None, :], first, whole, last


def attend(qkv, gain_rows, tok, shard, bounds):
    spans, rows, span = qkv.shape
    stream = spans * span
    slots = span // tok
    start, first, whole, last = bounds
    smem = pl.BlockSpec(memory_space=pltpu.SMEM)
    vmem = pl.BlockSpec(memory_space=pltpu.VMEM)

    def one(*block):
        return pl.BlockSpec((1,) + block, lambda i: (i, 0, 0))

    return pl.pallas_call(
        functools.partial(fwd_kernel, tok),
        grid=(spans,),
        in_specs=[smem, smem, smem, vmem, vmem, vmem],
        out_specs=[
            one(HEAD_DIM, span),
            pl.BlockSpec((spans, HEAD_DIM, span), lambda i: (0, 0, 0)),
            pl.BlockSpec((slots, HEAD_DIM + EXTRA, tok), lambda i: (i, 0, 0)),
            one(1, span),
        ],
        out_shape=[
            pltpu.HBM((spans, HEAD_DIM, span), jnp.float32),
            pltpu.HBM((spans, HEAD_DIM, span), jnp.bfloat16),
            pltpu.HBM((stream // tok, HEAD_DIM + EXTRA, tok), jnp.bfloat16),
            jax.ShapeDtypeStruct((spans, 1, span), jnp.float32),
        ],
        scratch_shapes=[
            pltpu.VMEM((stream, HEAD_DIM), jnp.bfloat16),
            pltpu.VMEM((1, span), jnp.float32),
            pltpu.VMEM((1, span), jnp.float32),
            pltpu.VMEM((HEAD_DIM, span), jnp.float32),
        ],
        compiler_params=pltpu.CompilerParams(vmem_limit_bytes=24 * 2**20),
        cost_estimate=pl.CostEstimate(
            flops=stream * stream * 256 * 5, bytes_accessed=stream * 1024, transcendentals=0
        ),
        name="attend",
    )(shard, first, whole, start, qkv, gain_rows)


def attend_back(qkv, lse, out, out_grad, cos_t, sin_t, tok, bounds):
    spans, rows, span = qkv.shape
    stream = spans * span
    start, first, whole, last = bounds
    smem = pl.BlockSpec(memory_space=pltpu.SMEM)
    vmem = pl.BlockSpec(memory_space=pltpu.VMEM)

    def one(*block):
        return pl.BlockSpec((1,) + block, lambda j: (j, 0, 0))

    return pl.pallas_call(
        functools.partial(bwd_kernel, tok),
        grid=(spans,),
        in_specs=[smem, smem, vmem, vmem, vmem, pl.BlockSpec(memory_space=pl.ANY), vmem]
        + [one(HEAD_DIM // 2, span)] * 2,
        out_specs=one(rows, span),
        out_shape=pltpu.HBM(qkv.shape, jnp.bfloat16),
        scratch_shapes=[
            pltpu.VMEM((spans, HEAD_DIM, span), jnp.float32),
            pltpu.VMEM((HEAD_DIM, span), jnp.float32),
            pltpu.VMEM((HEAD_DIM, span), jnp.float32),
            pltpu.VMEM((spans, HEAD_DIM, span), jnp.bfloat16),
            pltpu.VMEM((spans, 1, span), jnp.float32),
            pltpu.VMEM((spans, HEAD_DIM, span), jnp.float32),
            pltpu.SemaphoreType.DMA,
        ],
        compiler_params=pltpu.CompilerParams(vmem_limit_bytes=32 * 2**20),
        cost_estimate=pl.CostEstimate(
            flops=stream * stream * 256 * 7, bytes_accessed=stream * 1024, transcendentals=0
        ),
        name="attend_back",
    )(last, whole, start, qkv, lse, *in_hbm([out]), out_grad, *in_hbm([cos_t, sin_t]))


def as_column(row):
    shape = (row.shape[1], row.shape[1])
    same = lax.broadcasted_iota(jnp.int32, shape, 0) == lax.broadcasted_iota(jnp.int32, shape, 1)
    return jnp.sum(jnp.where(same, row.astype(jnp.float32), 0.0), axis=1, keepdims=True)


def pack_kernel(heads, place_ref, gain_ref, query_ref, key_ref, value_ref, out_ref):
    steps = out_ref.shape[1]
    seqs = 2 * steps
    z, core = place_ref[0] // 2, place_ref[0] % 2
    gain_col = as_column(gain_ref[...])
    for m, ref in enumerate((query_ref, key_ref, value_ref)):
        rows = (ref[...].astype(jnp.float32) * gain_col).astype(jnp.bfloat16)
        for head in range(heads):
            at = (head // seqs * 3 + m) * HEAD_DIM
            other = (core + head) % 2
            step = (head % seqs // 2 + steps - z) % steps
            out_ref[other, step, :, at : at + HEAD_DIM] = rows[
                :, head * HEAD_DIM : (head + 1) * HEAD_DIM
            ]


def pack_columns(place, gain_row, weights, seqs):
    rows, width = weights[0].shape
    heads = width // HEAD_DIM
    vmem = pl.BlockSpec(memory_space=pltpu.VMEM)
    return pl.pallas_call(
        functools.partial(pack_kernel, heads),
        in_specs=[pl.BlockSpec(memory_space=pltpu.SMEM)] + [vmem] * 4,
        out_specs=vmem,
        out_shape=jax.ShapeDtypeStruct(
            (2, seqs // 2, rows, heads // seqs * 3 * HEAD_DIM), jnp.bfloat16
        ),
        cost_estimate=SHORT,
        name="pack_columns",
    )(place, gain_row, *weights)


def order_kernel(index_ref, *refs):
    out_ref = refs[-1]
    rows = out_ref.shape[1]
    count = 0
    for ref in refs[:-1]:
        for i in range(ref.shape[0] // rows):
            out_ref[index_ref[count]] = ref[i * rows : (i + 1) * rows]
            count += 1


def order_blocks(pieces, index, rows):
    vmem = pl.BlockSpec(memory_space=pltpu.VMEM)
    blocks = sum(piece.shape[0] for piece in pieces) // rows
    width = pieces[0].shape[1]
    return pl.pallas_call(
        order_kernel,
        in_specs=[pl.BlockSpec(memory_space=pltpu.SMEM)] + [vmem] * len(pieces),
        out_specs=vmem,
        out_shape=jax.ShapeDtypeStruct((blocks, rows, width), pieces[0].dtype),
        compiler_params=pltpu.CompilerParams(vmem_limit_bytes=12 * 2**20),
        cost_estimate=SHORT,
        name="order_blocks",
    )(index, *pieces).reshape(blocks * rows, width)


def cols_kernel(shard_ref, back_ref, unit_ref, out_ref):
    slots, _, width = out_ref.shape
    back = back_ref[...]
    for k in range(slots):
        at = pl.ds(pl.multiple_of((shard_ref[0] ^ k) * width, width), width)
        out_ref[k] = dot_nn(back, unit_ref[:, at]).astype(jnp.bfloat16)


def cols_parts_of(shard, back, unit_low, slots):
    rows = back.shape[0]
    width = unit_low.shape[1] // slots
    vmem = pl.BlockSpec(memory_space=pltpu.VMEM)
    return pl.pallas_call(
        cols_kernel,
        in_specs=[pl.BlockSpec(memory_space=pltpu.SMEM)] + [vmem] * 2,
        out_specs=vmem,
        out_shape=jax.ShapeDtypeStruct((slots, rows, width), jnp.bfloat16),
        compiler_params=pltpu.CompilerParams(vmem_limit_bytes=24 * 2**20),
        cost_estimate=SHORT,
        name="cols_parts",
    )(shard, back, unit_low)


def unit_back_kernel(index_ref, back_ref, columns_ref, near_ref, other_ref):
    steps, tok, _ = near_ref.shape
    for step in range(steps):
        lanes = [
            back_ref[:, pl.ds(pl.multiple_of(index_ref[2 * step + c] * tok, tok), tok)]
            for c in range(2)
        ]
        part = times_trans(jnp.concatenate(lanes, axis=1).T, columns_ref[...])
        near_ref[step] = part[:tok]
        other_ref[step] = part[tok:].astype(jnp.bfloat16)


def unit_back(index, back, columns, tok):
    steps = back.shape[1] // (2 * tok)
    width = columns.shape[0]
    vmem = pl.BlockSpec(memory_space=pltpu.VMEM)
    return pl.pallas_call(
        unit_back_kernel,
        in_specs=[pl.BlockSpec(memory_space=pltpu.SMEM)] + [vmem] * 2,
        out_specs=[vmem] * 2,
        out_shape=[
            jax.ShapeDtypeStruct((steps, tok, width), jnp.float32),
            jax.ShapeDtypeStruct((steps, tok, width), jnp.bfloat16),
        ],
        compiler_params=pltpu.CompilerParams(vmem_limit_bytes=24 * 2**20),
        cost_estimate=SHORT,
        name="unit_back",
    )(index, back, columns)


def spread_kernel(place_ref, own_ref, one_ref, two_ref, out_ref):
    _, steps, rows, _ = out_ref.shape
    z, core = place_ref[0] // 2, place_ref[0] % 2
    total = own_ref[...].astype(jnp.float32)
    total += one_ref[...].astype(jnp.float32) + two_ref[...].astype(jnp.float32)
    total = total.T.astype(jnp.bfloat16)
    for q in range(2 * steps):
        out_ref[(core + q) % 2, (q // 2 + steps - z) % steps] = total[q * rows : (q + 1) * rows]


def spread_columns(place, own, one, two, steps):
    columns, rows = own.shape
    vmem = pl.BlockSpec(memory_space=pltpu.VMEM)
    return pl.pallas_call(
        spread_kernel,
        in_specs=[pl.BlockSpec(memory_space=pltpu.SMEM)] + [vmem] * 3,
        out_specs=vmem,
        out_shape=jax.ShapeDtypeStruct((2, steps, rows // (2 * steps), columns), jnp.bfloat16),
        cost_estimate=SHORT,
        name="spread_columns",
    )(place, own, one, two)


def pair_kernel(spread_ref, other_ref, *out_refs):
    for step, out_ref in enumerate(out_refs):
        out_ref[...] = jnp.concatenate([spread_ref[0, step], other_ref[step]])


def pair_columns(spread, other):
    steps, rows, columns = other.shape
    vmem = pl.BlockSpec(memory_space=pltpu.VMEM)
    return pl.pallas_call(
        pair_kernel,
        in_specs=[vmem] * 2,
        out_specs=[vmem] * steps,
        out_shape=[jax.ShapeDtypeStruct((2 * rows, columns), other.dtype)] * steps,
        cost_estimate=SHORT,
        name="pair_columns",
    )(spread, other)


def unpack_kernel(heads, place_ref, gain_ref, query_ref, key_ref, value_ref, *refs):
    out_refs, cols_s = refs[-5:-1], refs[-1]
    steps = len(refs) - 5
    rows = query_ref.shape[0]
    seqs = 2 * steps
    z, core = place_ref[0] // 2, place_ref[0] % 2
    for step in range(steps):
        cols_s[0, step] = refs[step][:rows]
        cols_s[1, step] = refs[step][rows:]
    gain_col = as_column(gain_ref[...])
    total = jnp.zeros((rows, 1), jnp.float32)
    for m, ref in enumerate((query_ref, key_ref, value_ref)):
        grads = jnp.concatenate(
            [
                cols_s[
                    (core + head) % 2,
                    (z + steps - head % seqs // 2) % steps,
                    :,
                    (head // seqs * 3 + m) * HEAD_DIM : (head // seqs * 3 + m + 1) * HEAD_DIM,
                ]
                for head in range(heads)
            ],
            axis=1,
        ).astype(jnp.float32)
        total += jnp.sum(grads * ref[...].astype(jnp.float32), axis=1, keepdims=True)
        out_refs[m][...] = grads * gain_col
    out_refs[3][...] = jnp.broadcast_to(total, (rows, 128)).T[:8]


def unpack_columns(place, gain_row, weights, cols):
    rows, width = weights[0].shape
    vmem = pl.BlockSpec(memory_space=pltpu.VMEM)
    return pl.pallas_call(
        functools.partial(unpack_kernel, width // HEAD_DIM),
        in_specs=[pl.BlockSpec(memory_space=pltpu.SMEM)] + [vmem] * (4 + len(cols)),
        out_specs=[vmem] * 4,
        out_shape=[jax.ShapeDtypeStruct((rows, width), jnp.float32)] * 3
        + [jax.ShapeDtypeStruct((8, rows), jnp.float32)],
        scratch_shapes=[pltpu.VMEM((2, len(cols), rows, cols[0].shape[1]), cols[0].dtype)],
        cost_estimate=SHORT,
        name="unpack_columns",
    )(place, gain_row, *weights, *cols)


def unit_kernel(index_ref, *refs):
    out_ref = refs[-1]
    tok = refs[0].shape[0]
    for slot, ref in enumerate(refs[:-1]):
        rows = ref[...].astype(jnp.float32)
        scale = lax.rsqrt(jnp.mean(rows * rows, axis=-1, keepdims=True) + NORM_EPS)
        at = pl.ds(pl.multiple_of(index_ref[slot] * tok, tok), tok)
        out_ref[at, :] = (rows * scale).astype(jnp.bfloat16)


def unit_tokens(index, slots):
    tok, width = slots[0].shape
    vmem = pl.BlockSpec(memory_space=pltpu.VMEM)
    return pl.pallas_call(
        unit_kernel,
        in_specs=[pl.BlockSpec(memory_space=pltpu.SMEM)] + [vmem] * len(slots),
        out_specs=vmem,
        out_shape=jax.ShapeDtypeStruct((len(slots) * tok, width), jnp.bfloat16),
        compiler_params=pltpu.CompilerParams(vmem_limit_bytes=16 * 2**20),
        cost_estimate=SHORT,
        name="unit_tokens",
    )(index, *slots)


def join_kernel(*refs):
    rows = refs[0].shape[0]
    for i, ref in enumerate(refs[:-1]):
        refs[-1][i * rows : (i + 1) * rows] = ref[...]


def join_rows(arrays):
    rows, width = arrays[0].shape
    vmem = pl.BlockSpec(memory_space=pltpu.VMEM)
    return pl.pallas_call(
        join_kernel,
        in_specs=[vmem] * len(arrays),
        out_specs=vmem,
        out_shape=jax.ShapeDtypeStruct((len(arrays) * rows, width), arrays[0].dtype),
        cost_estimate=SHORT,
        name="join_rows",
    )(*arrays)


def load_kernel(layout, *refs):
    pieces, out_ref, sem = refs[:-2], refs[-2], refs[-1]
    copies = [
        pltpu.make_async_copy(ref, out_ref.at[m, pl.ds(row, ref.shape[0])], sem.at[i])
        for i, (ref, (m, row)) in enumerate(zip(pieces, layout, strict=True))
    ]
    for copy in copies:
        copy.start()
    for copy in copies:
        copy.wait()


def load_weights(matrices):
    layout, pieces = [], []
    for m, matrix in enumerate(matrices):
        row = 0
        for piece in matrix:
            layout.append((m, row))
            pieces.append(piece)
            row += piece.shape[0]
    shape = (len(matrices), row, pieces[0].shape[1])
    return pl.pallas_call(
        functools.partial(load_kernel, tuple(layout)),
        in_specs=[pl.BlockSpec(memory_space=pl.ANY)] * len(pieces),
        out_specs=pl.BlockSpec(memory_space=pltpu.VMEM),
        out_shape=pltpu.VMEM(shape, pieces[0].dtype),
        scratch_shapes=[pltpu.SemaphoreType.DMA((len(pieces),))],
        cost_estimate=SHORT,
        compiler_params=pltpu.CompilerParams(vmem_limit_bytes=14 * 2**20),
        name="load_weights",
    )(*in_hbm(pieces))


def feed_kernel(call, aliased, *refs):
    shard_ref, tokens, grads, first_ref, down_ref = refs[0], refs[1:3], refs[3:5], refs[5], refs[6]
    refs = refs[7 + aliased :]
    part_near, part_other = refs[:2]
    all_refs = refs[2:9]
    tok_s, grad_s, hidden_s, gate_s, up_s, hidden_t, gate_t, up_t, down_s, sem = refs[9:]
    tok, width = tokens[0].shape
    shards, block = 4, down_ref.shape[1] // 4
    rows = pl.ds(2 * tok * call, 2 * tok)
    for c in range(2):
        tok_s[c * tok : (c + 1) * tok] = tokens[c][...]
        grad_s[c * tok : (c + 1) * tok] = grads[c][...]
    copies = [
        pltpu.make_async_copy(tok_s, all_refs[0].at[rows], sem.at[0]),
        pltpu.make_async_copy(grad_s, all_refs[1].at[rows], sem.at[1]),
    ]
    for copy in copies:
        copy.start()
    for b in range(shards):
        at = slice(b * block, (b + 1) * block)
        place = pl.ds(pl.multiple_of((shard_ref[0] ^ b) * block, block), block)
        gate_val = times_trans(tok_s[...], first_ref[0, at])
        up_val = times_trans(tok_s[...], first_ref[1, at])
        hidden_grad = times_trans(grad_s[...], down_ref[0, at])
        sigmoid_val = 1.0 / (1.0 + jnp.exp(-gate_val))
        silu_val = gate_val * sigmoid_val
        hidden = (silu_val * up_val).astype(jnp.bfloat16)
        gate_grad = (
            hidden_grad * up_val * (sigmoid_val + silu_val * (1.0 - sigmoid_val))
        ).astype(jnp.bfloat16)
        up_grad = (hidden_grad * silu_val).astype(jnp.bfloat16)
        for value, by_unit, by_token in (
            (hidden, hidden_t, hidden_s), (gate_grad, gate_t, gate_s), (up_grad, up_t, up_s)
        ):
            by_unit[place, :] = value.T
            by_token[:, at] = value
    late = [
        pltpu.make_async_copy(src, dst.at[:, rows], sem.at[2 + i])
        for i, (src, dst) in enumerate(zip((hidden_t, gate_t, up_t), all_refs[2:5], strict=True))
    ]
    for copy in late:
        copy.start()
    for c in range(4):
        at = slice(c * (width // 4), (c + 1) * (width // 4))
        part = dot_nn(gate_s[...], first_ref[0, :, at]) + dot_nn(up_s[...], first_ref[1, :, at])
        part_near[:, at] = part[:tok]
        part_other[:, at] = part[tok:].astype(jnp.bfloat16)
    for c in range(4):
        at = slice(c * (width // 4), (c + 1) * (width // 4))
        down = dot_nn(hidden_s[...], down_ref[0, :, at]).astype(jnp.bfloat16)
        down_s[0, :, at] = down[:tok]
        down_s[1, :, at] = down[tok:]
    last = [
        pltpu.make_async_copy(down_s.at[c], all_refs[5 + c].at[call], sem.at[5 + c])
        for c in range(2)
    ]
    for copy in last:
        copy.start()
    for copy in copies + late + last:
        copy.wait()


def feed_blocks(call, slots, shard, tokens, grads, first_two, down, whole):
    tok, width = tokens[0].shape
    units = down.shape[1]
    anywhere = pl.BlockSpec(memory_space=pl.ANY)
    vmem = pl.BlockSpec(memory_space=pltpu.VMEM)
    low, full = jnp.bfloat16, jnp.float32
    shapes = (
        [(slots * tok, width)] * 2
        + [(units, slots * tok)] * 3
        + [(slots // 2, tok, width)] * 2
    )
    whole = in_hbm(whole or [])
    out = pl.pallas_call(
        functools.partial(feed_kernel, call, len(whole)),
        in_specs=[pl.BlockSpec(memory_space=pltpu.SMEM)] + [vmem] * 6 + [anywhere] * len(whole),
        out_specs=[vmem] * 2 + [anywhere] * 7,
        out_shape=[jax.ShapeDtypeStruct((tok, width), full), jax.ShapeDtypeStruct((tok, width), low)]
        + [pltpu.HBM(shape, low) for shape in shapes],
        input_output_aliases={7 + i: 2 + i for i in range(len(whole))},
        scratch_shapes=[pltpu.VMEM((2 * tok, width), low)] * 2
        + [pltpu.VMEM((2 * tok, units), low)] * 3
        + [pltpu.VMEM((units, 2 * tok), low)] * 3
        + [pltpu.VMEM((2, tok, width), low), pltpu.SemaphoreType.DMA((7,))],
        compiler_params=pltpu.CompilerParams(vmem_limit_bytes=30 * 2**20),
        cost_estimate=SHORT,
        name="feed_blocks",
    )(
        shard,
        *tokens,
        *grads,
        *[pltpu.with_memory_space_constraint(weight, pltpu.VMEM) for weight in (first_two, down)],
        *whole,
    )
    return out[:2], out[2:]


def start_pieces(pieces, weight_s, sem):
    places, row = [], 0
    for i, ref in enumerate(pieces):
        at = pl.ds(row, ref.shape[0])
        copy = pltpu.make_async_copy(ref, weight_s.at[at], sem.at[i])
        copy.start()
        places.append((row, ref.shape[0], copy))
        row += ref.shape[0]
    return places


def project_kernel(index_ref, blocks_ref, input_ref, gain_ref, *refs):
    pieces, (middle_ref, normed_ref, scale_ref, weight_s, sem) = refs[:-5], refs[-5:]
    places = start_pieces(pieces, weight_s, sem)
    heads = blocks_ref.shape[0]
    rows = jnp.concatenate([blocks_ref[index_ref[i], :HEAD_DIM] for i in range(heads)]).T
    total = input_ref[...].astype(jnp.float32)
    for row, size, copy in places:
        copy.wait()
        total += dot_nn(rows[:, row : row + size], weight_s[row : row + size])
    scale = lax.rsqrt(jnp.mean(total * total, axis=-1, keepdims=True) + NORM_EPS)
    middle_ref[...] = total
    normed_ref[...] = (total * scale * gain_ref[...]).astype(jnp.bfloat16)
    scale_ref[...] = jnp.broadcast_to(scale, scale_ref.shape)


def project(index, blocks, inputs, gain, pieces):
    tok, width = inputs.shape
    vmem = pl.BlockSpec(memory_space=pltpu.VMEM)
    return pl.pallas_call(
        project_kernel,
        in_specs=[pl.BlockSpec(memory_space=pltpu.SMEM)]
        + [vmem] * 3
        + [pl.BlockSpec(memory_space=pl.ANY)] * len(pieces),
        out_specs=[vmem] * 3,
        out_shape=[
            jax.ShapeDtypeStruct((tok, width), jnp.float32),
            jax.ShapeDtypeStruct((tok, width), jnp.bfloat16),
            jax.ShapeDtypeStruct((tok, 128), jnp.float32),
        ],
        scratch_shapes=[
            pltpu.VMEM((HEADS * HEAD_DIM, width), jnp.bfloat16),
            pltpu.SemaphoreType.DMA((len(pieces),)),
        ],
        compiler_params=pltpu.CompilerParams(vmem_limit_bytes=18 * 2**20),
        cost_estimate=SHORT,
        name="project",
    )(index, blocks, inputs, gain, *in_hbm(pieces))


def token_grad_kernel(
    index_ref, own_ref, one_ref, two_ref, three_ref, middle_ref, scale_ref, gain_ref, grad_ref, *refs
):
    weight_ref, middle_grad_ref, low_ref, out_ref = refs
    normed_grad = own_ref[...]
    for ref in (one_ref, two_ref, three_ref):
        normed_grad += ref[...].astype(jnp.float32)
    tok = normed_grad.shape[0]
    scale = scale_ref[:, :1]
    unit = middle_ref[...] * scale
    gain_part = jnp.sum(normed_grad * unit, axis=0, keepdims=True)
    unit_grad = normed_grad * gain_ref[...]
    middle_grad = grad_ref[...].astype(jnp.float32) + scale * (
        unit_grad - unit * jnp.mean(unit_grad * unit, axis=-1, keepdims=True)
    )
    middle_grad_ref[...] = middle_grad
    low = middle_grad.astype(jnp.bfloat16)
    low_ref[...] = low
    grad_t = low.T
    size = weight_ref.shape[1] // 8
    for row in range(0, weight_ref.shape[1], size):
        out = dot_nn(weight_ref[0, row : row + size], grad_t).astype(jnp.bfloat16)
        for i in range(size // HEAD_DIM):
            out_ref[index_ref[row // HEAD_DIM + i], :HEAD_DIM] = out[
                i * HEAD_DIM : (i + 1) * HEAD_DIM
            ]
    coarse = gain_part.astype(jnp.bfloat16)
    fine = (gain_part - coarse.astype(jnp.float32)).astype(jnp.bfloat16)
    wide = gain_part.shape[1] // out_ref.shape[0]
    for head in range(out_ref.shape[0]):
        at = slice(head * wide, (head + 1) * wide)
        row = jnp.concatenate([coarse[:, at], fine[:, at]], axis=1)
        out_ref[head, HEAD_DIM:] = jnp.broadcast_to(row, (EXTRA, tok))


def token_grad(index, sums, middle, scale, gain, output_grad, weight):
    tok, width = middle.shape
    vmem = pl.BlockSpec(memory_space=pltpu.VMEM)
    return pl.pallas_call(
        token_grad_kernel,
        in_specs=[pl.BlockSpec(memory_space=pltpu.SMEM)]
        + [vmem] * 9,
        out_specs=[vmem] * 3,
        out_shape=[
            jax.ShapeDtypeStruct((tok, width), jnp.float32),
            jax.ShapeDtypeStruct((tok, width), jnp.bfloat16),
            pltpu.HBM((HEADS, HEAD_DIM + EXTRA, tok), jnp.bfloat16),
        ],
        compiler_params=pltpu.CompilerParams(vmem_limit_bytes=20 * 2**20),
        cost_estimate=SHORT,
        name="token_grad",
    )(
        index,
        *sums,
        middle,
        scale,
        gain,
        output_grad,
        pltpu.with_memory_space_constraint(weight, pltpu.VMEM),
    )


def feed_wgrad_kernel(gate_ref, up_ref, hidden_ref, tokens_ref, grads_ref, out_ref):
    tokens, grads = tokens_ref[...], grads_ref[...]
    out_ref[0, 0] = dot_nn(gate_ref[...], tokens).astype(jnp.bfloat16)
    out_ref[0, 1] = dot_nn(up_ref[...], tokens).astype(jnp.bfloat16)
    out_ref[0, 2] = dot_nn(hidden_ref[...], grads).astype(jnp.bfloat16)


def feed_wgrads(shards, gate_grad, up_grad, hidden, feed_low, span_grad):
    units, tokens = hidden.shape
    width = feed_low.shape[1]
    block = units // shards
    cuts = 2
    half = width // cuts
    rows = pl.BlockSpec((block, tokens), lambda c, i: (i, 0))
    every = pl.BlockSpec((tokens, half), lambda c, i: (0, c))
    return pl.pallas_call(
        feed_wgrad_kernel,
        grid=(cuts, shards),
        in_specs=[rows] * 3 + [every] * 2,
        out_specs=pl.BlockSpec((1, 3, block, half), lambda c, i: (i, 0, 0, c)),
        out_shape=pltpu.HBM((shards, 3, block, width), jnp.bfloat16),
        compiler_params=pltpu.CompilerParams(vmem_limit_bytes=24 * 2**20),
        cost_estimate=SHORT,
        name="feed_wgrads",
    )(*in_hbm([gate_grad, up_grad, hidden, feed_low, span_grad]))


def output_wgrad_kernel(index_ref, heads_ref, *refs):
    grads, (out_ref, grads_s) = refs[:-2], refs[-2:]
    tok = grads[0].shape[0]
    for slot, ref in enumerate(grads):
        grads_s[pl.ds(pl.multiple_of(index_ref[slot] * tok, tok), tok), :] = ref[...]
    for k in range(heads_ref.shape[0]):
        out_ref[k] = dot_nn(heads_ref[k], grads_s[...]).astype(jnp.bfloat16)


def output_wgrad_parts(index, heads, grads):
    tok, width = grads[0].shape
    vmem = pl.BlockSpec(memory_space=pltpu.VMEM)
    return pl.pallas_call(
        output_wgrad_kernel,
        in_specs=[pl.BlockSpec(memory_space=pltpu.SMEM)] + [vmem] * (1 + len(grads)),
        out_specs=vmem,
        out_shape=jax.ShapeDtypeStruct((heads.shape[0], HEAD_DIM, width), jnp.bfloat16),
        scratch_shapes=[pltpu.VMEM((len(grads) * tok, width), jnp.bfloat16)],
        compiler_params=pltpu.CompilerParams(vmem_limit_bytes=18 * 2**20),
        cost_estimate=SHORT,
        name="output_wgrad",
    )(index, heads, *grads)


def swap_cores(values):
    count = lax.axis_size("seq")
    return lax.ppermute(values, "seq", [(i, i ^ 1) for i in range(count)])


def from_chip(values, step):
    count = lax.axis_size("seq")
    return lax.ppermute(values, "seq", [((i + 2 * step) % count, i) for i in range(count)])


def from_shard(values, flip):
    return lax.ppermute(values, "shard", [(i, i ^ flip) for i in range(4)])


def both_cores(same):
    return [block for one in same for block in (one, swap_cores(one))]


def core_sum(near, other):
    return near.astype(F32) + swap_cores(other.astype(BF16)).astype(F32)


def after(token, values):
    return lax.optimization_barrier((values, token))[0]


def join(token, *values):
    return lax.optimization_barrier((token,) + values)[0]


def first_hops(block):
    return [from_shard(block, 1), from_shard(block, 2)]


def second_hops(first):
    rows = first[0].shape[0] // 2
    return [from_shard(first[0][:rows], 2), from_shard(first[1][rows:], 1)]


def scatter_shard_first(parts):
    rows = parts[3].shape[0] // 2
    low = parts[3].astype(BF16)
    return from_shard(low[:rows], 1), from_shard(low[rows:], 2)


def scatter_shard_last(parts, first):
    rows = parts[3].shape[0] // 2
    top, bottom = first
    one, two = parts[1].astype(F32), parts[2].astype(F32)
    one = jnp.concatenate([one[:rows], one[rows:] + bottom.astype(F32)])
    two = jnp.concatenate([two[:rows] + top.astype(F32), two[rows:]])
    return from_shard(one.astype(BF16), 1), from_shard(two.astype(BF16), 2)


def slot_block(slot, place, half):
    z, core = place // 2, place % 2
    return ((z + slot // 2) % half) * 2 + (core + slot) % 2


def rotate_rows(front, back, cos_t, sin_t):
    return jnp.concatenate([front * cos_t - back * sin_t, back * cos_t + front * sin_t], axis=-2)


def per_device(
    layer_input,
    doc_lengths,
    norm_gain,
    query_weight,
    key_weight,
    value_weight,
    output_weight,
    feed_gain,
    gate_weight,
    up_weight,
    down_weight,
    output_grad,
):
    tok, width = layer_input.shape
    seqs, shards = lax.axis_size("seq"), lax.axis_size("shard")
    shard, seq = lax.axis_index("shard"), lax.axis_index("seq")
    span = tok * seqs
    half_head = HEAD_DIM // 2
    place = jnp.reshape(seq, (1,)).astype(jnp.int32)

    positions = jnp.arange(shards * span, dtype=jnp.int32).reshape(shards, span)
    span_blocks = slot_block(jnp.arange(seqs, dtype=jnp.int32), seq.astype(jnp.int32), seqs // 2)
    bounds = doc_bounds(doc_lengths, positions)
    exponent = -2.0 * jnp.arange(half_head, dtype=jnp.float32) / HEAD_DIM
    inverse = jnp.power(jnp.float32(ROPE_BASE), exponent)
    angles = positions.astype(F32)[:, None, :] * inverse[None, :, None]
    cos_all, sin_all = jnp.cos(angles), jnp.sin(angles)
    cos_own = lax.dynamic_index_in_dim(cos_all, shard, 0, keepdims=False)
    sin_own = lax.dynamic_index_in_dim(sin_all, shard, 0, keepdims=False)

    steps = seqs // 2
    z, core = seq // 2, seq % 2
    shard_at = jnp.reshape(shard, (1,)).astype(jnp.int32)
    gain_row = norm_gain[None, :]
    heads_here = HEADS // seqs
    own_rows = query_weight.shape[0]
    attn_weights = (query_weight, key_weight, value_weight)
    slot = jnp.arange(HEADS, dtype=jnp.int32)

    packed = pack_columns(place, gain_row, attn_weights, seqs)
    point = join(jnp.zeros((), F32), packed)
    from_other = swap_cores(packed[1])
    gate_first = first_hops(after(point, gate_weight))
    col_blocks = []
    for step in range(steps):
        block = jnp.concatenate([packed[0, step], from_other[step]])
        col_blocks.append(from_chip(block, -step) if step else block)
    point = join(point, col_blocks)
    col_block = jnp.concatenate(after(point, col_blocks))
    col_first = first_hops(col_block)
    own_input = after(point, layer_input)
    input_one, input_three = from_chip(own_input, 1), from_chip(own_input, -1)
    point = join(point, col_first, input_one, input_three, gate_first)
    col_far = second_hops(after(point, col_first))
    input_two = from_chip(after(point, input_one), 1)
    input_slots = both_cores([own_input, after(point, input_one)])
    input_last = both_cores([after(point, input_three)])
    output_own = after(point, output_weight)
    output_three = from_chip(output_own, -1)
    point = join(point, col_far, input_two, input_slots, input_last, output_three)
    input_slots += both_cores([after(point, input_two)]) + input_last
    rel_blocks = (
        (shard ^ (slot // seqs)) * seqs
        + (z + steps - slot % seqs // 2) % steps * 2
        + (core ^ (slot % 2))
    ).astype(jnp.int32)
    columns = order_blocks([col_block] + col_first + after(point, col_far), rel_blocks, own_rows)
    unit_low = unit_tokens(span_blocks, input_slots)
    qkv = lax.dot_general(
        columns, unit_low, (((0,), (1,)), ((), ())), preferred_element_type=F32
    ).reshape(shards, 3, HEAD_DIM, span)
    turned = rotate_rows(
        qkv[:, :2, :half_head], qkv[:, :2, half_head:], cos_own[None, None], sin_own[None, None]
    )
    qkv_low = jnp.concatenate([turned, qkv[:, 2:]], axis=1).astype(BF16)
    qkv_low = qkv_low.reshape(shards, 3 * HEAD_DIM, span)
    gate_far = second_hops(after(point, gate_first))
    output_one = from_chip(after(point, output_weight), 1)
    up_top, up_bottom = up_weight[: up_weight.shape[0] // 2], up_weight[up_weight.shape[0] // 2 :]
    up_first = [from_shard(after(point, up_top), flip) for flip in (1, 2)]
    point = join(point, qkv_low, gate_far, output_one, up_first)

    head_qkv = lax.all_to_all(
        after(point, qkv_low), "shard", split_axis=0, concat_axis=0, tiled=True
    )
    output_two = from_chip(after(point, output_one), 1)
    own_grad = after(point, output_grad)
    grad_one = from_chip(own_grad, 1)
    up_first += [from_shard(after(point, up_bottom), flip) for flip in (1, 2)]
    point = join(point, head_qkv, output_two, grad_one, up_first)
    output_own = jnp.concatenate(after(point, [output_own, output_one, output_two, output_three]))
    output_first = first_hops(output_own)
    output_swapped = [swap_cores(output_own)]
    grad_two, grad_three = from_chip(after(point, grad_one), 1), from_chip(own_grad, -1)
    gain_rows = jnp.pad(feed_gain[None, :], ((0, EXTRA - 1), (0, tok - own_rows)))
    head_out, head_low, out_blocks, lse = attend(
        after(point, head_qkv), gain_rows, tok, shard_at, bounds
    )
    point = join(point, out_blocks, output_first, output_swapped, grad_two, grad_three)
    token_blocks = lax.all_to_all(
        after(point, out_blocks), ("shard", "seq"), split_axis=0, concat_axis=0, tiled=True
    )
    output_far = second_hops(after(point, output_first))
    output_swapped += [swap_cores(piece) for piece in after(point, output_first)]
    point = join(point, token_blocks, output_far, output_swapped)
    gain_two = token_blocks[:, HEAD_DIM, :own_rows].astype(F32).reshape(1, width)
    output_swapped += [swap_cores(piece) for piece in after(point, output_far)]
    up_far = [from_shard(after(point, up_first[0]), 2), from_shard(after(point, up_first[3]), 1)]
    output_pieces = [output_own] + output_first + output_far + output_swapped
    rel_heads = (
        (shard ^ (slot // steps % shards)) * seqs
        + (z + slot % steps) % steps * 2
        + (core ^ (slot // (HEADS // 2)))
    ).astype(jnp.int32)
    middle, normed_two, scale_two = project(
        rel_heads, after(point, token_blocks), layer_input, gain_two, output_pieces
    )
    point = join(point, normed_two, up_far)

    own_tokens = after(point, normed_two)
    tokens_one, tokens_three = from_chip(own_tokens, 1), from_chip(own_tokens, -1)
    down_first = first_hops(after(point, down_weight))
    grad_slots = both_cores(after(point, [output_grad, grad_one, grad_two, grad_three]))
    first_two = load_weights(
        [
            after(point, [gate_weight, *gate_first, *gate_far]),
            [up_weight, up_first[0], up_first[2], up_first[1], up_first[3], *up_far],
        ]
    )
    point = join(point, tokens_one, tokens_three, down_first, grad_slots, first_two)
    tokens_two = from_chip(after(point, tokens_one), 1)
    down_far = second_hops(after(point, down_first))
    feed_slots = both_cores([own_tokens, after(point, tokens_one)])
    output_here = load_weights([after(point, output_pieces)])
    feed_last = both_cores([after(point, tokens_three)])
    point = join(point, tokens_two, down_far, feed_slots, feed_last, output_here)
    feed_slots += both_cores([after(point, tokens_two)]) + feed_last
    down_here = load_weights([[down_weight, *down_first, *after(point, down_far)]])
    order = (2, 1, 3, 0)

    def feed(step, tokens, whole):
        here = slice(2 * step, 2 * step + 2)
        return feed_blocks(
            order.index(step), seqs, shard_at, tokens, grad_slots[here], first_two, down_here, whole
        )

    parts_two, whole = feed(2, feed_slots[4:6], None)
    sum_two = core_sum(*parts_two).astype(BF16)
    point = join(point, sum_two)
    arrived_two = from_chip(after(point, sum_two), -2)
    parts_one, whole = feed(1, after(point, feed_slots[2:4]), whole)
    parts_three, whole = feed(3, feed_slots[6:8], whole)
    parts_own, whole = feed(0, feed_slots[0:2], whole)
    point = join(point, arrived_two, parts_one, parts_three, parts_own)
    sum_one = core_sum(*after(point, parts_one)).astype(BF16)
    sum_three = core_sum(*after(point, parts_three)).astype(BF16)
    point = join(point, sum_one, sum_three)
    arrived_one = from_chip(after(point, sum_one), -1)
    arrived_three = from_chip(after(point, sum_three), 1)
    sum_own = core_sum(*after(point, parts_own))
    feed_low, span_grad, hidden, gate_grad, up_grad, down_near, down_other = after(point, whole)
    feed_wparts = feed_wgrads(shards, gate_grad, up_grad, hidden, feed_low, span_grad)
    point = join(point, sum_own, feed_wparts, arrived_one, arrived_three)
    middle_grad, attend_grad, head_grad = token_grad(
        rel_heads,
        [sum_own, *after(point, [arrived_one, arrived_two, arrived_three])],
        middle,
        scale_two,
        gain_two,
        output_grad,
        output_here,
    )
    point = join(point, head_grad)

    out_grad_blocks = lax.all_to_all(
        after(point, head_grad), ("shard", "seq"), split_axis=0, concat_axis=0, tiled=True
    )
    feed_wsum = lax.psum_scatter(
        after(point, feed_wparts).reshape(-1, width), "shard", scatter_dimension=0, tiled=True
    ).reshape(3, -1, width)
    own_agrad = after(point, attend_grad)
    agrad_one = from_chip(own_agrad, 1)
    down_all = core_sum(after(point, down_near), down_other).astype(BF16)
    down_sums = [down_all[order.index(step)] for step in range(steps)]
    head_slots = [head_low[0]] + [from_shard(after(point, head_low[k]), k) for k in range(1, 4)]
    point = join(point, out_grad_blocks, agrad_one, down_sums, head_slots)
    both = from_chip(jnp.concatenate([own_agrad, after(point, down_sums[2])]), -1)
    down_three = from_chip(after(point, down_sums[3]), 1)
    back = attend_back(
        head_qkv, lse, head_out, after(point, out_grad_blocks), cos_all, sin_all, tok, bounds
    )
    point = join(point, back, both, down_three)
    agrad_three, down_two = both[:tok], both[tok:]
    span_back = lax.all_to_all(
        after(point, back), "shard", split_axis=0, concat_axis=0, tiled=True
    ).reshape(heads_here * 3 * HEAD_DIM, span)
    agrad_two = from_chip(after(point, agrad_one), 1)
    down_one = from_chip(
        (down_sums[1].astype(F32) + after(point, down_two).astype(F32)).astype(BF16), -1
    )
    agrad_slots = both_cores([after(point, own_agrad), agrad_one, agrad_two, agrad_three])
    out_part = output_wgrad_parts(span_blocks, jnp.stack(head_slots), agrad_slots)
    out_parts = [out_part[k] for k in range(4)]
    out_first = scatter_shard_first(out_parts)
    point = join(point, span_back, down_one, out_first)

    span_back = after(point, span_back)
    cols_part = cols_parts_of(shard_at, span_back, unit_low, shards)
    point = join(point, cols_part)
    cols_parts = [after(point, cols_part)[k] for k in range(4)]
    cols_first = scatter_shard_first(cols_parts)
    unit_near, unit_other = unit_back(span_blocks, after(point, span_back), columns, tok)
    unit_swapped = swap_cores(unit_other)
    point = join(point, unit_near, unit_swapped)
    unit_sums = unit_near + after(point, unit_swapped).astype(F32)
    unit_two = from_chip(unit_sums[2].astype(BF16), -1)
    unit_three = from_chip(unit_sums[3].astype(BF16), 1)
    out_last = scatter_shard_last(out_parts, after(point, out_first))
    layer_output = (
        middle
        + down_sums[0].astype(F32)
        + after(point, down_one).astype(F32)
        + down_three.astype(F32)
    ).astype(BF16)
    point, layer_output = lax.optimization_barrier(
        (join(point, unit_two, unit_three, cols_first, out_last), layer_output)
    )
    unit_one = from_chip((unit_sums[1] + after(point, unit_two).astype(F32)).astype(BF16), -1)
    cols_last = scatter_shard_last(cols_parts, after(point, cols_first))
    point = join(point, unit_one, cols_last)
    cols_spread = spread_columns(place, cols_parts[0], *after(point, cols_last), steps)
    cols_other = swap_cores(cols_spread[1])
    cols_blocks = pair_columns(cols_spread, cols_other)
    point = join(point, cols_blocks)
    cols_same = list(after(point, cols_blocks))
    cols_same = cols_same[:1] + [from_chip(cols_same[step], -step) for step in range(1, steps)]
    out_one, out_two = after(point, out_last)
    output_wgrad = out_parts[0].astype(F32) + out_one.astype(F32) + out_two.astype(F32)
    unit_grad = unit_sums[0] + after(point, unit_one).astype(F32) + unit_three.astype(F32)
    inputs = layer_input.astype(F32)
    scale_one = lax.rsqrt(jnp.mean(inputs * inputs, axis=-1, keepdims=True) + NORM_EPS)
    unit_rows = inputs * scale_one
    input_grad = (
        middle_grad
        + scale_one * (unit_grad - unit_rows * jnp.mean(unit_grad * unit_rows, axis=-1, keepdims=True))
    ).astype(BF16)
    gate_wgrad, up_wgrad, down_wgrad = [
        after(point, feed_wsum)[m].astype(F32) for m in range(3)
    ]
    gain_rows_back = out_grad_blocks[:, HEAD_DIM].astype(F32)
    gain_two_out = jnp.sum(
        gain_rows_back[:, :own_rows] + gain_rows_back[:, own_rows : 2 * own_rows], axis=0
    )
    point, output_wgrad, input_grad, gate_wgrad, up_wgrad, down_wgrad, gain_two_out, cols_same = (
        lax.optimization_barrier(
            (
                *(point, output_wgrad, input_grad, gate_wgrad, up_wgrad, down_wgrad, gain_two_out),
                cols_same,
            )
        )
    )
    query_wgrad, key_wgrad, value_wgrad, gain_one_out = unpack_columns(
        place, gain_row, attn_weights, after(point, cols_same)
    )
    return (
        layer_output,
        input_grad,
        gain_one_out[0],
        query_wgrad,
        key_wgrad,
        value_wgrad,
        output_wgrad,
        gain_two_out,
        gate_wgrad,
        up_wgrad,
        down_wgrad,
    )


def solution(mesh):
    shards, seqs = mesh.shape["shard"], mesh.shape["seq"]
    body = per_device if shards == 4 and shards * seqs == HEADS else per_device_any
    return jax.shard_map(
        body,
        mesh=mesh,
        in_specs=(
            P(("shard", "seq"), None),
            P(),
            P(("shard", "seq")),
            P(("shard", "seq"), None),
            P(("shard", "seq"), None),
            P(("shard", "seq"), None),
            P(("shard", "seq"), None),
            P(("shard", "seq")),
            P(("shard", "seq"), None),
            P(("shard", "seq"), None),
            P(("shard", "seq"), None),
            P(("shard", "seq"), None),
        ),
        out_specs=(
            P(("shard", "seq"), None),
            P(("shard", "seq"), None),
            P(("shard", "seq")),
            P(("shard", "seq"), None),
            P(("shard", "seq"), None),
            P(("shard", "seq"), None),
            P(("shard", "seq"), None),
            P(("shard", "seq")),
            P(("shard", "seq"), None),
            P(("shard", "seq"), None),
            P(("shard", "seq"), None),
        ),
        check_vma=False,
    )
```

```python
import functools
import math

import jax
import jax.numpy as jnp
from jax import lax
from jax.experimental import pallas as pl
from jax.experimental.pallas import tpu as pltpu
from jax.sharding import PartitionSpec as P

HEAD_DIM = 64


NORM_EPS = 1e-05
ROPE_BASE = 130000.0


def rope_tables(positions, width):
    half_width = width // 2
    exponent = -2.0 * jnp.arange(half_width, dtype=jnp.float32) / width
    inverse = jnp.power(jnp.float32(ROPE_BASE), exponent)
    angles = positions.astype(jnp.float32)[:, None] * inverse[None, :]
    return (jnp.cos(angles), jnp.sin(angles))


def rotate(values, cos_table, sin_table):
    half_width = values.shape[-1] // 2
    front = values[..., :half_width]
    back_half = values[..., half_width:]
    cos_wide = cos_table[:, None, :]
    sin_wide = sin_table[:, None, :]
    return jnp.concatenate(
        [front * cos_wide - back_half * sin_wide, back_half * cos_wide + front * sin_wide], axis=-1
    )


def unrotate(values, cos_table, sin_table):
    half_width = values.shape[-1] // 2
    front = values[..., :half_width]
    back_half = values[..., half_width:]
    cos_wide = cos_table[:, None, :]
    sin_wide = sin_table[:, None, :]
    return jnp.concatenate(
        [front * cos_wide + back_half * sin_wide, back_half * cos_wide - front * sin_wide], axis=-1
    )


def doc_numbers(doc_lengths, positions):
    doc_ends = jnp.cumsum(doc_lengths)
    return jnp.sum((doc_ends[:, None] <= positions[None, :]).astype(jnp.int32), axis=0)


def normalize(values, gain_vec):
    scale_row = lax.rsqrt(jnp.mean(values * values, axis=-1, keepdims=True) + NORM_EPS)
    return (values * scale_row * gain_vec, scale_row)


def norm_back(grad_in, values, scale_row, gain_vec):
    unit_rows = values * scale_row
    gain_grad = jnp.sum(grad_in * unit_rows, axis=0)
    unit_grad = grad_in * gain_vec
    value_grad = scale_row * (
        unit_grad - unit_rows * jnp.mean(unit_grad * unit_rows, axis=-1, keepdims=True)
    )
    return (value_grad, gain_grad)


def times_trans(lhs_mat, rhs_mat):
    return lax.dot_general(
        lhs_mat, rhs_mat, (((1,), (1,)), ((), ())), preferred_element_type=jnp.float32
    )


def trans_times(lhs_mat, rhs_mat):
    return lax.dot_general(
        lhs_mat, rhs_mat, (((0,), (0,)), ((), ())), preferred_element_type=jnp.float32
    )


def per_device_any(
    layer_input,
    doc_lengths,
    norm_gain,
    query_weight,
    key_weight,
    value_weight,
    output_weight,
    feed_gain,
    gate_weight,
    up_weight,
    down_weight,
    output_grad,
):
    tok_rows = layer_input.shape[0]
    width = layer_input.shape[1]
    seq_count = lax.axis_size("seq")
    shard_count = lax.axis_size("shard")
    span_len = tok_rows * seq_count
    stream_len = span_len * shard_count
    span_start = lax.axis_index("shard") * span_len
    own_positions = (
        span_start + lax.axis_index("seq") * tok_rows + jnp.arange(tok_rows, dtype=jnp.int32)
    )
    span_positions = span_start + jnp.arange(span_len, dtype=jnp.int32)
    all_positions = jnp.arange(stream_len, dtype=jnp.int32)
    key_docs = doc_numbers(doc_lengths, all_positions)
    query_docs = lax.dynamic_slice_in_dim(key_docs, span_start, span_len)
    score_scale = HEAD_DIM ** (-0.5)
    gathered = (
        lax.all_gather(query_weight, ("shard", "seq"), axis=0, tiled=True),
        lax.all_gather(key_weight, ("shard", "seq"), axis=0, tiled=True),
        lax.all_gather(value_weight, ("shard", "seq"), axis=0, tiled=True),
        lax.all_gather(output_weight, ("shard", "seq"), axis=0, tiled=True),
        lax.all_gather(norm_gain, ("shard", "seq"), axis=0, tiled=True),
        lax.all_gather(feed_gain, ("shard", "seq"), axis=0, tiled=True),
    )
    query_full, key_full, value_full, output_full = (
        gathered[0],
        gathered[1],
        gathered[2],
        gathered[3],
    )
    gain_one = gathered[4].astype(jnp.float32)
    gain_two = gathered[5].astype(jnp.float32)
    inputs = layer_input.astype(jnp.float32)
    normed, scale_one = normalize(inputs, gain_one)
    normed_low = normed.astype(jnp.bfloat16)
    own_cos, own_sin = rope_tables(own_positions, HEAD_DIM)
    query_proj = jnp.dot(normed_low, query_full, preferred_element_type=jnp.float32)
    key_proj = jnp.dot(normed_low, key_full, preferred_element_type=jnp.float32)
    value_proj = jnp.dot(normed_low, value_full, preferred_element_type=jnp.float32)
    query_rot = rotate(query_proj.reshape(tok_rows, -1, HEAD_DIM), own_cos, own_sin).reshape(
        tok_rows, width
    )
    key_rot = rotate(key_proj.reshape(tok_rows, -1, HEAD_DIM), own_cos, own_sin).reshape(
        tok_rows, width
    )
    stacked = jnp.stack(
        [
            query_rot.astype(jnp.bfloat16),
            key_rot.astype(jnp.bfloat16),
            value_proj.astype(jnp.bfloat16),
        ]
    )
    head_triple = lax.all_to_all(stacked, "seq", split_axis=2, concat_axis=1, tiled=True)
    head_width = head_triple.shape[2]
    heads_dev = head_width // HEAD_DIM
    head_query = head_triple[0].reshape(span_len, heads_dev, HEAD_DIM)
    key_value = lax.all_gather(head_triple[1:], "shard", axis=1, tiled=True)
    key_block = math.gcd(stream_len, max(512, stream_len // 16))
    block_count = stream_len // key_block
    key_blocks = key_value[0].reshape(block_count, key_block, heads_dev, HEAD_DIM)
    value_blocks = key_value[1].reshape(block_count, key_block, heads_dev, HEAD_DIM)
    pos_blocks = all_positions.reshape(block_count, key_block)
    doc_blocks = key_docs.reshape(block_count, key_block)

    def block_scores(key_blk, key_pos, key_doc):
        scores = (
            jnp.einsum("qhd,khd->hqk", head_query, key_blk, preferred_element_type=jnp.float32)
            * score_scale
        )
        allowed = (key_pos[None, :] <= span_positions[:, None]) & (
            key_doc[None, :] == query_docs[:, None]
        )
        return jnp.where(allowed[None], scores, -jnp.inf)

    def total_step(state_pair, pieces):
        run_max, run_sum = state_pair
        scores = block_scores(pieces[0], pieces[1], pieces[2])
        new_max = jnp.maximum(run_max, jnp.max(scores, axis=-1))
        new_sum = run_sum * jnp.exp(run_max - new_max) + jnp.sum(
            jnp.exp(scores - new_max[..., None]), axis=-1
        )
        return ((new_max, new_sum), None)

    start_max = jnp.full((heads_dev, span_len), -1e30, jnp.float32)
    start_sum = jnp.zeros((heads_dev, span_len), jnp.float32)
    totals, unused = lax.scan(
        total_step, (start_max, start_sum), (key_blocks, pos_blocks, doc_blocks)
    )
    log_total = totals[0] + jnp.log(totals[1])

    def output_step(accum, pieces):
        scores = block_scores(pieces[0], pieces[2], pieces[3])
        probs = jnp.exp(scores - log_total[..., None]).astype(jnp.bfloat16)
        return (
            accum
            + jnp.einsum("hqk,khd->qhd", probs, pieces[1], preferred_element_type=jnp.float32),
            None,
        )

    start_acc = jnp.zeros((span_len, heads_dev, HEAD_DIM), jnp.float32)
    head_out32, unused = lax.scan(
        output_step, start_acc, (key_blocks, value_blocks, pos_blocks, doc_blocks)
    )
    head_out = head_out32.reshape(span_len, head_width).astype(jnp.bfloat16)
    token_out = lax.all_to_all(head_out, "seq", split_axis=0, concat_axis=1, tiled=True)
    middle = inputs + jnp.dot(token_out, output_full, preferred_element_type=jnp.float32)
    normed_two, scale_two = normalize(middle, gain_two)
    feed_low = normed_two.astype(jnp.bfloat16)
    feed_mats = (
        lax.all_gather(gate_weight, ("shard", "seq"), axis=0, tiled=True),
        lax.all_gather(up_weight, ("shard", "seq"), axis=0, tiled=True),
        lax.all_gather(down_weight, ("shard", "seq"), axis=0, tiled=True),
    )
    gate_full, up_full, down_full = (feed_mats[0], feed_mats[1], feed_mats[2])
    gate_val = times_trans(feed_low, gate_full)
    up_val = times_trans(feed_low, up_full)
    hidden = (jax.nn.silu(gate_val) * up_val).astype(jnp.bfloat16)
    down_val = jnp.dot(hidden, down_full, preferred_element_type=jnp.float32)
    layer_output = (middle + down_val).astype(jnp.bfloat16)
    hidden_grad = times_trans(output_grad, down_full)
    sigmoid_val = jax.nn.sigmoid(gate_val)
    gate_grad = (
        hidden_grad * up_val * (sigmoid_val * (1.0 + gate_val * (1.0 - sigmoid_val)))
    ).astype(jnp.bfloat16)
    up_grad = (hidden_grad * jax.nn.silu(gate_val)).astype(jnp.bfloat16)
    feed_grad = jnp.dot(gate_grad, gate_full, preferred_element_type=jnp.float32) + jnp.dot(
        up_grad, up_full, preferred_element_type=jnp.float32
    )
    feed_sums = lax.psum_scatter(
        jnp.stack(
            [
                trans_times(gate_grad, feed_low),
                trans_times(up_grad, feed_low),
                trans_times(hidden, output_grad),
            ],
            axis=1,
        ),
        ("shard", "seq"),
        scatter_dimension=0,
        tiled=True,
    )
    middle_norm_grad, gain_two_grad = norm_back(feed_grad, middle, scale_two, gain_two)
    middle_grad = output_grad.astype(jnp.float32) + middle_norm_grad
    attend_grad = middle_grad.astype(jnp.bfloat16)
    output_term = trans_times(token_out, attend_grad)
    token_out_grad = times_trans(attend_grad, output_full).astype(jnp.bfloat16)
    head_out_grad = lax.all_to_all(
        token_out_grad, "seq", split_axis=1, concat_axis=0, tiled=True
    ).reshape(span_len, heads_dev, HEAD_DIM)
    row_dots = jnp.transpose(jnp.sum(head_out_grad.astype(jnp.float32) * head_out32, axis=-1))

    def grad_step(query_acc, pieces):
        key_blk, value_blk, key_pos, key_doc = pieces
        scores = block_scores(key_blk, key_pos, key_doc)
        probs = jnp.exp(scores - log_total[..., None])
        prob_grad = jnp.einsum(
            "qhd,khd->hqk", head_out_grad, value_blk, preferred_element_type=jnp.float32
        )
        score_grad = (probs * (prob_grad - row_dots[..., None])).astype(jnp.bfloat16)
        query_next = query_acc + score_scale * jnp.einsum(
            "hqk,khd->qhd", score_grad, key_blk, preferred_element_type=jnp.float32
        )
        key_part = score_scale * jnp.einsum(
            "hqk,qhd->khd", score_grad, head_query, preferred_element_type=jnp.float32
        )
        value_part = jnp.einsum(
            "hqk,qhd->khd",
            probs.astype(jnp.bfloat16),
            head_out_grad,
            preferred_element_type=jnp.float32,
        )
        return (query_next, (key_part, value_part))

    query_grad, block_grads = lax.scan(
        grad_step, start_acc, (key_blocks, value_blocks, pos_blocks, doc_blocks)
    )
    pair_grads = jnp.stack(
        [
            block_grads[0].reshape(stream_len, head_width),
            block_grads[1].reshape(stream_len, head_width),
        ]
    )
    own_pair = lax.psum_scatter(
        pair_grads.astype(jnp.bfloat16), "shard", scatter_dimension=1, tiled=True
    ).astype(jnp.float32)
    span_cos, span_sin = rope_tables(span_positions, HEAD_DIM)
    query_back = unrotate(query_grad, span_cos, span_sin).reshape(span_len, head_width)
    key_back = unrotate(
        own_pair[0].reshape(span_len, heads_dev, HEAD_DIM), span_cos, span_sin
    ).reshape(span_len, head_width)
    back_stack = jnp.stack([query_back, key_back, own_pair[1]]).astype(jnp.bfloat16)
    token_grads = lax.all_to_all(back_stack, "seq", split_axis=1, concat_axis=2, tiled=True)
    norm_grad = (
        times_trans(token_grads[0], query_full)
        + times_trans(token_grads[1], key_full)
        + times_trans(token_grads[2], value_full)
    )
    input_norm_grad, gain_one_grad = norm_back(norm_grad, inputs, scale_one, gain_one)
    input_grad = (middle_grad + input_norm_grad).astype(jnp.bfloat16)
    query_term = trans_times(normed_low, token_grads[0])
    key_term = trans_times(normed_low, token_grads[1])
    value_term = trans_times(normed_low, token_grads[2])
    summed = (
        lax.psum_scatter(query_term, ("shard", "seq"), scatter_dimension=0, tiled=True),
        lax.psum_scatter(key_term, ("shard", "seq"), scatter_dimension=0, tiled=True),
        lax.psum_scatter(value_term, ("shard", "seq"), scatter_dimension=0, tiled=True),
        lax.psum_scatter(output_term, ("shard", "seq"), scatter_dimension=0, tiled=True),
        lax.psum_scatter(gain_one_grad, ("shard", "seq"), scatter_dimension=0, tiled=True),
        lax.psum_scatter(gain_two_grad, ("shard", "seq"), scatter_dimension=0, tiled=True),
    )
    query_wgrad, key_wgrad, value_wgrad = (summed[0], summed[1], summed[2])
    output_wgrad, gain_one_out, gain_two_out = (summed[3], summed[4], summed[5])
    return (
        layer_output,
        input_grad,
        gain_one_out,
        query_wgrad,
        key_wgrad,
        value_wgrad,
        output_wgrad,
        gain_two_out,
        feed_sums[:, 0],
        feed_sums[:, 1],
        feed_sums[:, 2],
    )


HEADS = 32
EXTRA = 16
BF16 = jnp.bfloat16
F32 = jnp.float32


SHORT = pl.CostEstimate(flops=0, bytes_accessed=0, transcendentals=0)


def in_hbm(arrays):
    return [pltpu.with_memory_space_constraint(array, pltpu.HBM) for array in arrays]


def dot_nn(lhs_mat, rhs_mat):
    return lax.dot_general(
        lhs_mat, rhs_mat, (((1,), (0,)), ((), ())), preferred_element_type=jnp.float32
    )


def allowed_pairs(i, j, keys, cols, span, start_ref, same):
    shape = (keys.stop - keys.start, cols.stop - cols.start)
    k_pos = j * span + keys.start + lax.broadcasted_iota(jnp.int32, shape, 0)
    begun = k_pos >= start_ref[i][:, cols]
    if not same:
        return begun
    q_pos = i * span + cols.start + lax.broadcasted_iota(jnp.int32, shape, 1)
    return (k_pos <= q_pos) & begun


def own_span_parts(span):
    half = span // 2
    return (slice(0, half), slice(0, half)), (slice(0, span), slice(half, span))


def fwd_kernel(tok, shard_ref, lo_ref, full_ref, start_ref, qkv_ref, gain_ref, out_ref, low_ref, blocks_ref,
               lse_ref, k_nat, m_s, l_s, acc_s):
    i = pl.program_id(0)
    spans, rows, span = qkv_ref.shape
    slots = span // tok
    scale2 = HEAD_DIM ** -0.5 * math.log2(math.e)

    @pl.when(i == 0)
    def _():
        for s in range(spans):
            k_nat[pl.ds(s * span, span), :] = qkv_ref[s, HEAD_DIM : 2 * HEAD_DIM, :].T

    m_s[...] = jnp.full_like(m_s, -1e30)
    l_s[...] = jnp.zeros_like(l_s)
    acc_s[...] = jnp.zeros_like(acc_s)

    def step(j, masked, same=False, keys=slice(0, span), cols=slice(0, span)):
        k_rows = pl.ds(pl.multiple_of(j * span + keys.start, 128), keys.stop - keys.start)
        s_t = dot_nn(k_nat[k_rows, :], qkv_ref[i, :HEAD_DIM, cols]) * scale2
        if masked:
            s_t = jnp.where(allowed_pairs(i, j, keys, cols, span, start_ref, same), s_t, -jnp.inf)
        m_old = m_s[:, cols]
        m_new = jnp.maximum(m_old, jnp.max(s_t, axis=0, keepdims=True))
        alpha = jnp.exp2(m_old - m_new)
        p_t = jnp.exp2(s_t - m_new)
        l_s[:, cols] = l_s[:, cols] * alpha + jnp.sum(p_t, axis=0, keepdims=True)
        m_s[:, cols] = m_new
        acc_s[:, cols] = acc_s[:, cols] * alpha + dot_nn(
            qkv_ref[j, 2 * HEAD_DIM :, keys], p_t.astype(jnp.bfloat16)
        )

    def loop_body(masked):
        def body(j, carry):
            step(j, masked)
            return carry

        return body

    lax.fori_loop(lo_ref[i], full_ref[i], loop_body(True), 0)
    lax.fori_loop(full_ref[i], i, loop_body(False), 0)
    for keys, cols in own_span_parts(span):
        step(i, True, True, keys, cols)
    out = acc_s[...] / l_s[...]
    out_ref[0] = out
    low = out.astype(jnp.bfloat16)
    low_ref[i ^ shard_ref[0]] = low
    lse_ref[0] = m_s[...] + jnp.log2(l_s[...])
    for slot in range(slots):
        blocks_ref[slot, :HEAD_DIM] = low[:, slot * tok : (slot + 1) * tok]
        blocks_ref[slot, HEAD_DIM:] = gain_ref[...]


def bwd_kernel(tok, hi_ref, full_ref, start_ref, qkv_ref, lse_ref, out_hbm, dob_ref,
               cos_ref, sin_ref, back_ref, dq_s, dk_s, dv_s, do_s, di_s, out_ref, sem):
    j = pl.program_id(0)
    spans, rows, span = qkv_ref.shape
    slots = span // tok
    scale = HEAD_DIM ** -0.5
    scale2 = scale * math.log2(math.e)

    @pl.when(j == 0)
    def _():
        copy = pltpu.make_async_copy(out_hbm, out_ref, sem)
        copy.start()
        dq_s[...] = jnp.zeros_like(dq_s)
        for s in range(spans):
            for slot in range(slots):
                do_s[s, :, slot * tok : (slot + 1) * tok] = dob_ref[s * slots + slot, :HEAD_DIM]
        copy.wait()
        for s in range(spans):
            di_s[s] = jnp.sum(do_s[s].astype(jnp.float32) * out_ref[s], axis=0, keepdims=True)

    k_nat = qkv_ref[j, HEAD_DIM : 2 * HEAD_DIM, :].T
    v_nat = qkv_ref[j, 2 * HEAD_DIM :, :].T
    dk_s[...] = jnp.zeros_like(dk_s)
    dv_s[...] = jnp.zeros_like(dv_s)

    def step(i, masked, same=False, keys=slice(0, span), cols=slice(0, span)):
        q_t = qkv_ref[i, :HEAD_DIM, cols]
        p_t = jnp.exp2(dot_nn(k_nat[keys], q_t) * scale2 - lse_ref[i][:, cols])
        if masked:
            p_t = jnp.where(allowed_pairs(i, j, keys, cols, span, start_ref, same), p_t, 0.0)
        do_t = do_s[i, :, cols]
        dv_s[:, keys] += times_trans(do_t, p_t.astype(jnp.bfloat16))
        ds_t = (p_t * (dot_nn(v_nat[keys], do_t) - di_s[i][:, cols])).astype(jnp.bfloat16)
        dk_s[:, keys] += times_trans(q_t, ds_t)
        dq_s[i, :, cols] += dot_nn(qkv_ref[j, HEAD_DIM : 2 * HEAD_DIM, keys], ds_t)

    for keys, cols in own_span_parts(span):
        step(j, True, True, keys, cols)

    def body(i, carry):
        whole = full_ref[i] <= j

        @pl.when(whole)
        def _():
            step(i, False)

        @pl.when(jnp.logical_not(whole))
        def _():
            step(i, True)

        return carry

    lax.fori_loop(j + 1, hi_ref[j], body, 0)

    def turned_back(grad):
        front, back_half = grad[: HEAD_DIM // 2], grad[HEAD_DIM // 2 :]
        cos_t, sin_t = cos_ref[0], sin_ref[0]
        return jnp.concatenate(
            [front * cos_t + back_half * sin_t, back_half * cos_t - front * sin_t], axis=0
        ).astype(jnp.bfloat16)

    back_ref[0, :HEAD_DIM] = turned_back(dq_s[j] * scale)
    back_ref[0, HEAD_DIM : 2 * HEAD_DIM] = turned_back(dk_s[...] * scale)
    back_ref[0, 2 * HEAD_DIM :] = dv_s[...].astype(jnp.bfloat16)


def doc_bounds(doc_lengths, positions):
    spans, span = positions.shape
    ends = jnp.cumsum(doc_lengths)
    over = ends[:, None, None] <= positions[None]
    start = jnp.max(jnp.where(over, ends[:, None, None], 0), axis=0).astype(jnp.int32)
    stop = jnp.min(jnp.where(over, spans * span, ends[:, None, None]), axis=0).astype(jnp.int32)
    first = jnp.min(start, axis=1) // span
    whole = jnp.minimum(
        (jnp.max(start, axis=1) + span - 1) // span, jnp.arange(spans, dtype=jnp.int32)
    )
    last = (jnp.max(stop, axis=1) + span - 1) // span
    return start[:, None, :], first, whole, last


def attend(qkv, gain_rows, tok, shard, bounds):
    spans, rows, span = qkv.shape
    stream = spans * span
    slots = span // tok
    start, first, whole, last = bounds
    smem = pl.BlockSpec(memory_space=pltpu.SMEM)
    vmem = pl.BlockSpec(memory_space=pltpu.VMEM)

    def one(*block):
        return pl.BlockSpec((1,) + block, lambda i: (i, 0, 0))

    return pl.pallas_call(
        functools.partial(fwd_kernel, tok),
        grid=(spans,),
        in_specs=[smem, smem, smem, vmem, vmem, vmem],
        out_specs=[
            one(HEAD_DIM, span),
            pl.BlockSpec((spans, HEAD_DIM, span), lambda i: (0, 0, 0)),
            pl.BlockSpec((slots, HEAD_DIM + EXTRA, tok), lambda i: (i, 0, 0)),
            one(1, span),
        ],
        out_shape=[
            pltpu.HBM((spans, HEAD_DIM, span), jnp.float32),
            pltpu.HBM((spans, HEAD_DIM, span), jnp.bfloat16),
            pltpu.HBM((stream // tok, HEAD_DIM + EXTRA, tok), jnp.bfloat16),
            jax.ShapeDtypeStruct((spans, 1, span), jnp.float32),
        ],
        scratch_shapes=[
            pltpu.VMEM((stream, HEAD_DIM), jnp.bfloat16),
            pltpu.VMEM((1, span), jnp.float32),
            pltpu.VMEM((1, span), jnp.float32),
            pltpu.VMEM((HEAD_DIM, span), jnp.float32),
        ],
        compiler_params=pltpu.CompilerParams(vmem_limit_bytes=24 * 2**20),
        cost_estimate=pl.CostEstimate(
            flops=stream * stream * 256 * 5, bytes_accessed=stream * 1024, transcendentals=0
        ),
        name="attend",
    )(shard, first, whole, start, qkv, gain_rows)


def attend_back(qkv, lse, out, out_grad, cos_t, sin_t, tok, bounds):
    spans, rows, span = qkv.shape
    stream = spans * span
    start, first, whole, last = bounds
    smem = pl.BlockSpec(memory_space=pltpu.SMEM)
    vmem = pl.BlockSpec(memory_space=pltpu.VMEM)

    def one(*block):
        return pl.BlockSpec((1,) + block, lambda j: (j, 0, 0))

    return pl.pallas_call(
        functools.partial(bwd_kernel, tok),
        grid=(spans,),
        in_specs=[smem, smem, vmem, vmem, vmem, pl.BlockSpec(memory_space=pl.ANY), vmem]
        + [one(HEAD_DIM // 2, span)] * 2,
        out_specs=one(rows, span),
        out_shape=pltpu.HBM(qkv.shape, jnp.bfloat16),
        scratch_shapes=[
            pltpu.VMEM((spans, HEAD_DIM, span), jnp.float32),
            pltpu.VMEM((HEAD_DIM, span), jnp.float32),
            pltpu.VMEM((HEAD_DIM, span), jnp.float32),
            pltpu.VMEM((spans, HEAD_DIM, span), jnp.bfloat16),
            pltpu.VMEM((spans, 1, span), jnp.float32),
            pltpu.VMEM((spans, HEAD_DIM, span), jnp.float32),
            pltpu.SemaphoreType.DMA,
        ],
        compiler_params=pltpu.CompilerParams(vmem_limit_bytes=32 * 2**20),
        cost_estimate=pl.CostEstimate(
            flops=stream * stream * 256 * 7, bytes_accessed=stream * 1024, transcendentals=0
        ),
        name="attend_back",
    )(last, whole, start, qkv, lse, *in_hbm([out]), out_grad, *in_hbm([cos_t, sin_t]))


def as_column(row):
    shape = (row.shape[1], row.shape[1])
    same = lax.broadcasted_iota(jnp.int32, shape, 0) == lax.broadcasted_iota(jnp.int32, shape, 1)
    return jnp.sum(jnp.where(same, row.astype(jnp.float32), 0.0), axis=1, keepdims=True)


def pack_kernel(heads, place_ref, gain_ref, query_ref, key_ref, value_ref, out_ref):
    steps = out_ref.shape[1]
    seqs = 2 * steps
    z, core = place_ref[0] // 2, place_ref[0] % 2
    gain_col = as_column(gain_ref[...])
    for m, ref in enumerate((query_ref, key_ref, value_ref)):
        rows = (ref[...].astype(jnp.float32) * gain_col).astype(jnp.bfloat16)
        for head in range(heads):
            at = (head // seqs * 3 + m) * HEAD_DIM
            other = (core + head) % 2
            step = (head % seqs // 2 + steps - z) % steps
            out_ref[other, step, :, at : at + HEAD_DIM] = rows[
                :, head * HEAD_DIM : (head + 1) * HEAD_DIM
            ]


def pack_columns(place, gain_row, weights, seqs):
    rows, width = weights[0].shape
    heads = width // HEAD_DIM
    vmem = pl.BlockSpec(memory_space=pltpu.VMEM)
    return pl.pallas_call(
        functools.partial(pack_kernel, heads),
        in_specs=[pl.BlockSpec(memory_space=pltpu.SMEM)] + [vmem] * 4,
        out_specs=vmem,
        out_shape=jax.ShapeDtypeStruct(
            (2, seqs // 2, rows, heads // seqs * 3 * HEAD_DIM), jnp.bfloat16
        ),
        cost_estimate=SHORT,
        name="pack_columns",
    )(place, gain_row, *weights)


def order_kernel(index_ref, *refs):
    out_ref = refs[-1]
    rows = out_ref.shape[1]
    count = 0
    for ref in refs[:-1]:
        for i in range(ref.shape[0] // rows):
            out_ref[index_ref[count]] = ref[i * rows : (i + 1) * rows]
            count += 1


def order_blocks(pieces, index, rows):
    vmem = pl.BlockSpec(memory_space=pltpu.VMEM)
    blocks = sum(piece.shape[0] for piece in pieces) // rows
    width = pieces[0].shape[1]
    return pl.pallas_call(
        order_kernel,
        in_specs=[pl.BlockSpec(memory_space=pltpu.SMEM)] + [vmem] * len(pieces),
        out_specs=vmem,
        out_shape=jax.ShapeDtypeStruct((blocks, rows, width), pieces[0].dtype),
        compiler_params=pltpu.CompilerParams(vmem_limit_bytes=12 * 2**20),
        cost_estimate=SHORT,
        name="order_blocks",
    )(index, *pieces).reshape(blocks * rows, width)


def cols_kernel(shard_ref, back_ref, unit_hbm, out_ref, unit_s, sem):
    slots, _, width = out_ref.shape
    copies = [
        pltpu.make_async_copy(
            unit_hbm.at[:, pl.ds(pl.multiple_of((shard_ref[0] ^ k) * width, width), width)],
            unit_s.at[k],
            sem.at[k],
        )
        for k in range(slots)
    ]
    for copy in copies:
        copy.start()
    for k in range(slots):
        copies[k].wait()
        out_ref[k] = dot_nn(back_ref[...], unit_s[k]).astype(jnp.bfloat16)


def cols_parts_of(shard, back, unit_low, slots):
    rows = back.shape[0]
    tokens = unit_low.shape[0]
    width = unit_low.shape[1] // slots
    vmem = pl.BlockSpec(memory_space=pltpu.VMEM)
    return pl.pallas_call(
        cols_kernel,
        in_specs=[
            pl.BlockSpec(memory_space=pltpu.SMEM), vmem, pl.BlockSpec(memory_space=pl.ANY)
        ],
        out_specs=vmem,
        out_shape=jax.ShapeDtypeStruct((slots, rows, width), jnp.bfloat16),
        scratch_shapes=[
            pltpu.VMEM((slots, tokens, width), unit_low.dtype),
            pltpu.SemaphoreType.DMA((slots,)),
        ],
        compiler_params=pltpu.CompilerParams(vmem_limit_bytes=24 * 2**20),
        cost_estimate=SHORT,
        name="cols_parts",
    )(shard, back, *in_hbm([unit_low]))


def unit_back_kernel(index_ref, back_ref, columns_ref, near_ref, other_ref):
    steps, tok, _ = near_ref.shape
    for step in range(steps):
        lanes = [
            back_ref[:, pl.ds(pl.multiple_of(index_ref[2 * step + c] * tok, tok), tok)]
            for c in range(2)
        ]
        part = times_trans(jnp.concatenate(lanes, axis=1).T, columns_ref[...])
        near_ref[step] = part[:tok]
        other_ref[step] = part[tok:].astype(jnp.bfloat16)


def unit_back(index, back, columns, tok):
    steps = back.shape[1] // (2 * tok)
    width = columns.shape[0]
    vmem = pl.BlockSpec(memory_space=pltpu.VMEM)
    return pl.pallas_call(
        unit_back_kernel,
        in_specs=[pl.BlockSpec(memory_space=pltpu.SMEM)] + [vmem] * 2,
        out_specs=[vmem] * 2,
        out_shape=[
            jax.ShapeDtypeStruct((steps, tok, width), jnp.float32),
            jax.ShapeDtypeStruct((steps, tok, width), jnp.bfloat16),
        ],
        compiler_params=pltpu.CompilerParams(vmem_limit_bytes=24 * 2**20),
        cost_estimate=SHORT,
        name="unit_back",
    )(index, back, columns)


def spread_kernel(place_ref, own_ref, one_ref, two_ref, near_ref, other_ref, both_s):
    steps, rows, _ = near_ref.shape
    z, core = place_ref[0] // 2, place_ref[0] % 2
    total = own_ref[...].astype(jnp.float32)
    total += one_ref[...].astype(jnp.float32) + two_ref[...].astype(jnp.float32)
    total = total.T.astype(jnp.bfloat16)
    for q in range(2 * steps):
        both_s[(core + q) % 2, (q // 2 + steps - z) % steps] = total[q * rows : (q + 1) * rows]
    near_ref[...] = both_s[0]
    other_ref[...] = both_s[1]


def spread_columns(place, own, one, two, steps):
    columns, rows = own.shape
    vmem = pl.BlockSpec(memory_space=pltpu.VMEM)
    shape = (steps, rows // (2 * steps), columns)
    return pl.pallas_call(
        spread_kernel,
        in_specs=[pl.BlockSpec(memory_space=pltpu.SMEM)] + [vmem] * 3,
        out_specs=[vmem] * 2,
        out_shape=[jax.ShapeDtypeStruct(shape, jnp.bfloat16)] * 2,
        scratch_shapes=[pltpu.VMEM((2,) + shape, jnp.bfloat16)],
        cost_estimate=SHORT,
        name="spread_columns",
    )(place, own, one, two)


def pair_kernel(spread_ref, other_ref, *out_refs):
    for step, out_ref in enumerate(out_refs):
        out_ref[...] = jnp.concatenate([spread_ref[step], other_ref[step]])


def pair_columns(spread, other):
    steps, rows, columns = other.shape
    vmem = pl.BlockSpec(memory_space=pltpu.VMEM)
    return pl.pallas_call(
        pair_kernel,
        in_specs=[vmem] * 2,
        out_specs=[vmem] * steps,
        out_shape=[jax.ShapeDtypeStruct((2 * rows, columns), other.dtype)] * steps,
        cost_estimate=SHORT,
        name="pair_columns",
    )(spread, other)


def unpack_kernel(heads, place_ref, gain_ref, query_ref, key_ref, value_ref, *refs):
    out_refs, cols_s = refs[-5:-1], refs[-1]
    steps = len(refs) - 5
    rows = query_ref.shape[0]
    seqs = 2 * steps
    z, core = place_ref[0] // 2, place_ref[0] % 2
    for step in range(steps):
        cols_s[0, step] = refs[step][:rows]
        cols_s[1, step] = refs[step][rows:]
    gain_col = as_column(gain_ref[...])
    total = jnp.zeros((rows, 1), jnp.float32)
    for m, ref in enumerate((query_ref, key_ref, value_ref)):
        grads = jnp.concatenate(
            [
                cols_s[
                    (core + head) % 2,
                    (z + steps - head % seqs // 2) % steps,
                    :,
                    (head // seqs * 3 + m) * HEAD_DIM : (head // seqs * 3 + m + 1) * HEAD_DIM,
                ]
                for head in range(heads)
            ],
            axis=1,
        ).astype(jnp.float32)
        total += jnp.sum(grads * ref[...].astype(jnp.float32), axis=1, keepdims=True)
        out_refs[m][...] = grads * gain_col
    out_refs[3][...] = jnp.broadcast_to(total, (rows, 128)).T[:1]


def unpack_columns(place, gain_row, weights, cols):
    rows, width = weights[0].shape
    vmem = pl.BlockSpec(memory_space=pltpu.VMEM)
    return pl.pallas_call(
        functools.partial(unpack_kernel, width // HEAD_DIM),
        in_specs=[pl.BlockSpec(memory_space=pltpu.SMEM)] + [vmem] * (4 + len(cols)),
        out_specs=[vmem] * 4,
        out_shape=[jax.ShapeDtypeStruct((rows, width), jnp.float32)] * 3
        + [jax.ShapeDtypeStruct((1, rows), jnp.float32)],
        scratch_shapes=[pltpu.VMEM((2, len(cols), rows, cols[0].shape[1]), cols[0].dtype)],
        cost_estimate=SHORT,
        name="unpack_columns",
    )(place, gain_row, *weights, *cols)


def unit_kernel(index_ref, *refs):
    out_ref = refs[-1]
    tok = refs[0].shape[0]
    for slot, ref in enumerate(refs[:-1]):
        rows = ref[...].astype(jnp.float32)
        scale = lax.rsqrt(jnp.mean(rows * rows, axis=-1, keepdims=True) + NORM_EPS)
        at = pl.ds(pl.multiple_of(index_ref[slot] * tok, tok), tok)
        out_ref[at, :] = (rows * scale).astype(jnp.bfloat16)


def unit_tokens(index, slots):
    tok, width = slots[0].shape
    vmem = pl.BlockSpec(memory_space=pltpu.VMEM)
    return pl.pallas_call(
        unit_kernel,
        in_specs=[pl.BlockSpec(memory_space=pltpu.SMEM)] + [vmem] * len(slots),
        out_specs=vmem,
        out_shape=jax.ShapeDtypeStruct((len(slots) * tok, width), jnp.bfloat16),
        compiler_params=pltpu.CompilerParams(vmem_limit_bytes=16 * 2**20),
        cost_estimate=SHORT,
        name="unit_tokens",
    )(index, *slots)


def join_kernel(*refs):
    rows = refs[0].shape[0]
    for i, ref in enumerate(refs[:-1]):
        refs[-1][i * rows : (i + 1) * rows] = ref[...]


def join_rows(arrays):
    rows, width = arrays[0].shape
    vmem = pl.BlockSpec(memory_space=pltpu.VMEM)
    return pl.pallas_call(
        join_kernel,
        in_specs=[vmem] * len(arrays),
        out_specs=vmem,
        out_shape=jax.ShapeDtypeStruct((len(arrays) * rows, width), arrays[0].dtype),
        cost_estimate=SHORT,
        name="join_rows",
    )(*arrays)


def load_kernel(layout, *refs):
    pieces, out_ref, sem = refs[:-2], refs[-2], refs[-1]
    copies = [
        pltpu.make_async_copy(ref, out_ref.at[m, pl.ds(row, ref.shape[0])], sem.at[i])
        for i, (ref, (m, row)) in enumerate(zip(pieces, layout, strict=True))
    ]
    for copy in copies:
        copy.start()
    for copy in copies:
        copy.wait()


def load_weights(matrices):
    layout, pieces = [], []
    for m, matrix in enumerate(matrices):
        row = 0
        for piece in matrix:
            layout.append((m, row))
            pieces.append(piece)
            row += piece.shape[0]
    shape = (len(matrices), row, pieces[0].shape[1])
    return pl.pallas_call(
        functools.partial(load_kernel, tuple(layout)),
        in_specs=[pl.BlockSpec(memory_space=pl.ANY)] * len(pieces),
        out_specs=pl.BlockSpec(memory_space=pltpu.VMEM),
        out_shape=pltpu.VMEM(shape, pieces[0].dtype),
        scratch_shapes=[pltpu.SemaphoreType.DMA((len(pieces),))],
        cost_estimate=SHORT,
        compiler_params=pltpu.CompilerParams(vmem_limit_bytes=14 * 2**20),
        name="load_weights",
    )(*in_hbm(pieces))


def feed_kernel(call, aliased, *refs):
    shard_ref, tokens, grads, first_ref, down_ref = refs[0], refs[1:3], refs[3:5], refs[5], refs[6]
    refs = refs[7 + aliased :]
    part_near, part_other = refs[:2]
    all_refs = refs[2:9]
    tok_s, grad_s, hidden_s, gate_s, up_s, hidden_t, gate_t, up_t, down_s, sem = refs[9:]
    tok, width = tokens[0].shape
    shards, block = 4, down_ref.shape[1] // 4
    rows = pl.ds(2 * tok * call, 2 * tok)
    for c in range(2):
        tok_s[c * tok : (c + 1) * tok] = tokens[c][...]
        grad_s[c * tok : (c + 1) * tok] = grads[c][...]
    copies = [
        pltpu.make_async_copy(tok_s, all_refs[0].at[rows], sem.at[0]),
        pltpu.make_async_copy(grad_s, all_refs[1].at[rows], sem.at[1]),
    ]
    for copy in copies:
        copy.start()
    for b in range(shards):
        at = slice(b * block, (b + 1) * block)
        place = pl.ds(pl.multiple_of((shard_ref[0] ^ b) * block, block), block)
        gate_val = times_trans(tok_s[...], first_ref[0, at])
        up_val = times_trans(tok_s[...], first_ref[1, at])
        hidden_grad = times_trans(grad_s[...], down_ref[0, at])
        sigmoid_val = 1.0 / (1.0 + jnp.exp(-gate_val))
        silu_val = gate_val * sigmoid_val
        hidden = (silu_val * up_val).astype(jnp.bfloat16)
        gate_grad = (
            hidden_grad * up_val * (sigmoid_val + silu_val * (1.0 - sigmoid_val))
        ).astype(jnp.bfloat16)
        up_grad = (hidden_grad * silu_val).astype(jnp.bfloat16)
        for value, by_unit, by_token in (
            (hidden, hidden_t, hidden_s), (gate_grad, gate_t, gate_s), (up_grad, up_t, up_s)
        ):
            by_unit[place, :] = value.T
            by_token[:, at] = value
    late = [
        pltpu.make_async_copy(src, dst.at[:, rows], sem.at[2 + i])
        for i, (src, dst) in enumerate(zip((hidden_t, gate_t, up_t), all_refs[2:5], strict=True))
    ]
    for copy in late:
        copy.start()
    for c in range(4):
        at = slice(c * (width // 4), (c + 1) * (width // 4))
        down = dot_nn(hidden_s[...], down_ref[0, :, at]).astype(jnp.bfloat16)
        down_s[0, :, at] = down[:tok]
        down_s[1, :, at] = down[tok:]
    last = [
        pltpu.make_async_copy(down_s.at[c], all_refs[5 + c].at[call], sem.at[5 + c])
        for c in range(2)
    ]
    for copy in last:
        copy.start()
    for c in range(4):
        at = slice(c * (width // 4), (c + 1) * (width // 4))
        part = dot_nn(gate_s[...], first_ref[0, :, at]) + dot_nn(up_s[...], first_ref[1, :, at])
        part_near[:, at] = part[:tok]
        part_other[:, at] = part[tok:].astype(jnp.bfloat16)
    for copy in copies + late + last:
        copy.wait()


def feed_blocks(call, slots, shard, tokens, grads, first_two, down, whole):
    tok, width = tokens[0].shape
    units = down.shape[1]
    anywhere = pl.BlockSpec(memory_space=pl.ANY)
    vmem = pl.BlockSpec(memory_space=pltpu.VMEM)
    low, full = jnp.bfloat16, jnp.float32
    shapes = (
        [(slots * tok, width)] * 2
        + [(units, slots * tok)] * 3
        + [(slots // 2, tok, width)] * 2
    )
    whole = in_hbm(whole or [])
    out = pl.pallas_call(
        functools.partial(feed_kernel, call, len(whole)),
        in_specs=[pl.BlockSpec(memory_space=pltpu.SMEM)] + [vmem] * 6 + [anywhere] * len(whole),
        out_specs=[vmem] * 2 + [anywhere] * 7,
        out_shape=[jax.ShapeDtypeStruct((tok, width), full), jax.ShapeDtypeStruct((tok, width), low)]
        + [pltpu.HBM(shape, low) for shape in shapes],
        input_output_aliases={7 + i: 2 + i for i in range(len(whole))},
        scratch_shapes=[pltpu.VMEM((2 * tok, width), low)] * 2
        + [pltpu.VMEM((2 * tok, units), low)] * 3
        + [pltpu.VMEM((units, 2 * tok), low)] * 3
        + [pltpu.VMEM((2, tok, width), low), pltpu.SemaphoreType.DMA((7,))],
        compiler_params=pltpu.CompilerParams(vmem_limit_bytes=30 * 2**20),
        cost_estimate=SHORT,
        name="feed_blocks",
    )(
        shard,
        *tokens,
        *grads,
        *[pltpu.with_memory_space_constraint(weight, pltpu.VMEM) for weight in (first_two, down)],
        *whole,
    )
    return out[:2], out[2:]


def start_pieces(pieces, weight_s, sem):
    places, row = [], 0
    for i, ref in enumerate(pieces):
        at = pl.ds(row, ref.shape[0])
        copy = pltpu.make_async_copy(ref, weight_s.at[at], sem.at[i])
        copy.start()
        places.append((row, ref.shape[0], copy))
        row += ref.shape[0]
    return places


def project_kernel(index_ref, blocks_ref, input_ref, gain_ref, *refs):
    pieces, (middle_ref, normed_ref, scale_ref, weight_s, sem) = refs[:-5], refs[-5:]
    places = start_pieces(pieces, weight_s, sem)
    heads = blocks_ref.shape[0]
    rows = jnp.concatenate([blocks_ref[index_ref[i], :HEAD_DIM] for i in range(heads)]).T
    total = input_ref[...].astype(jnp.float32)
    for row, size, copy in places:
        copy.wait()
        total += dot_nn(rows[:, row : row + size], weight_s[row : row + size])
    scale = lax.rsqrt(jnp.mean(total * total, axis=-1, keepdims=True) + NORM_EPS)
    middle_ref[...] = total
    normed_ref[...] = (total * scale * gain_ref[...]).astype(jnp.bfloat16)
    scale_ref[...] = jnp.broadcast_to(scale, scale_ref.shape)


def project(index, blocks, inputs, gain, pieces):
    tok, width = inputs.shape
    vmem = pl.BlockSpec(memory_space=pltpu.VMEM)
    return pl.pallas_call(
        project_kernel,
        in_specs=[pl.BlockSpec(memory_space=pltpu.SMEM)]
        + [vmem] * 3
        + [pl.BlockSpec(memory_space=pl.ANY)] * len(pieces),
        out_specs=[vmem] * 3,
        out_shape=[
            jax.ShapeDtypeStruct((tok, width), jnp.float32),
            jax.ShapeDtypeStruct((tok, width), jnp.bfloat16),
            jax.ShapeDtypeStruct((tok, 128), jnp.float32),
        ],
        scratch_shapes=[
            pltpu.VMEM((HEADS * HEAD_DIM, width), jnp.bfloat16),
            pltpu.SemaphoreType.DMA((len(pieces),)),
        ],
        compiler_params=pltpu.CompilerParams(vmem_limit_bytes=18 * 2**20),
        cost_estimate=SHORT,
        name="project",
    )(index, blocks, inputs, gain, *in_hbm(pieces))


def token_grad_kernel(
    index_ref, own_ref, one_ref, two_ref, three_ref, middle_ref, scale_ref, gain_ref, grad_ref, *refs
):
    weight_ref, middle_grad_ref, low_ref, out_ref = refs
    normed_grad = own_ref[...]
    for ref in (one_ref, two_ref, three_ref):
        normed_grad += ref[...].astype(jnp.float32)
    tok = normed_grad.shape[0]
    scale = scale_ref[:, :1]
    unit = middle_ref[...] * scale
    gain_part = jnp.sum(normed_grad * unit, axis=0, keepdims=True)
    unit_grad = normed_grad * gain_ref[...]
    middle_grad = grad_ref[...].astype(jnp.float32) + scale * (
        unit_grad - unit * jnp.mean(unit_grad * unit, axis=-1, keepdims=True)
    )
    middle_grad_ref[...] = middle_grad
    low = middle_grad.astype(jnp.bfloat16)
    low_ref[...] = low
    grad_t = low.T
    size = weight_ref.shape[1] // 8
    for row in range(0, weight_ref.shape[1], size):
        out = dot_nn(weight_ref[0, row : row + size], grad_t).astype(jnp.bfloat16)
        for i in range(size // HEAD_DIM):
            out_ref[index_ref[row // HEAD_DIM + i], :HEAD_DIM] = out[
                i * HEAD_DIM : (i + 1) * HEAD_DIM
            ]
    coarse = gain_part.astype(jnp.bfloat16)
    fine = (gain_part - coarse.astype(jnp.float32)).astype(jnp.bfloat16)
    wide = gain_part.shape[1] // out_ref.shape[0]
    for head in range(out_ref.shape[0]):
        at = slice(head * wide, (head + 1) * wide)
        row = jnp.concatenate([coarse[:, at], fine[:, at]], axis=1)
        out_ref[head, HEAD_DIM:] = jnp.broadcast_to(row, (EXTRA, tok))


def token_grad(index, sums, middle, scale, gain, output_grad, weight):
    tok, width = middle.shape
    vmem = pl.BlockSpec(memory_space=pltpu.VMEM)
    return pl.pallas_call(
        token_grad_kernel,
        in_specs=[pl.BlockSpec(memory_space=pltpu.SMEM)]
        + [vmem] * 9,
        out_specs=[vmem] * 3,
        out_shape=[
            jax.ShapeDtypeStruct((tok, width), jnp.float32),
            jax.ShapeDtypeStruct((tok, width), jnp.bfloat16),
            pltpu.HBM((HEADS, HEAD_DIM + EXTRA, tok), jnp.bfloat16),
        ],
        compiler_params=pltpu.CompilerParams(vmem_limit_bytes=20 * 2**20),
        cost_estimate=SHORT,
        name="token_grad",
    )(
        index,
        *sums,
        middle,
        scale,
        gain,
        output_grad,
        pltpu.with_memory_space_constraint(weight, pltpu.VMEM),
    )


def feed_wgrad_kernel(gate_ref, up_ref, hidden_ref, tokens_ref, grads_ref, out_ref):
    tokens, grads = tokens_ref[...], grads_ref[...]
    out_ref[0, 0] = dot_nn(gate_ref[...], tokens).astype(jnp.bfloat16)
    out_ref[0, 1] = dot_nn(up_ref[...], tokens).astype(jnp.bfloat16)
    out_ref[0, 2] = dot_nn(hidden_ref[...], grads).astype(jnp.bfloat16)


def feed_wgrads(shards, gate_grad, up_grad, hidden, feed_low, span_grad):
    units, tokens = hidden.shape
    width = feed_low.shape[1]
    block = units // shards
    cuts = 2
    half = width // cuts
    rows = pl.BlockSpec((block, tokens), lambda c, i: (i, 0))
    every = pl.BlockSpec((tokens, half), lambda c, i: (0, c))
    return pl.pallas_call(
        feed_wgrad_kernel,
        grid=(cuts, shards),
        in_specs=[rows] * 3 + [every] * 2,
        out_specs=pl.BlockSpec((1, 3, block, half), lambda c, i: (i, 0, 0, c)),
        out_shape=pltpu.HBM((shards, 3, block, width), jnp.bfloat16),
        compiler_params=pltpu.CompilerParams(vmem_limit_bytes=24 * 2**20),
        cost_estimate=SHORT,
        name="feed_wgrads",
    )(*in_hbm([gate_grad, up_grad, hidden, feed_low, span_grad]))


def output_wgrad_kernel(index_ref, heads_ref, *refs):
    grads, (out_ref, grads_s) = refs[:-2], refs[-2:]
    tok = grads[0].shape[0]
    for slot, ref in enumerate(grads):
        grads_s[pl.ds(pl.multiple_of(index_ref[slot] * tok, tok), tok), :] = ref[...]
    for k in range(heads_ref.shape[0]):
        out_ref[k] = dot_nn(heads_ref[k], grads_s[...]).astype(jnp.bfloat16)


def output_wgrad_parts(index, heads, grads):
    tok, width = grads[0].shape
    vmem = pl.BlockSpec(memory_space=pltpu.VMEM)
    return pl.pallas_call(
        output_wgrad_kernel,
        in_specs=[pl.BlockSpec(memory_space=pltpu.SMEM)] + [vmem] * (1 + len(grads)),
        out_specs=vmem,
        out_shape=jax.ShapeDtypeStruct((heads.shape[0], HEAD_DIM, width), jnp.bfloat16),
        scratch_shapes=[pltpu.VMEM((len(grads) * tok, width), jnp.bfloat16)],
        compiler_params=pltpu.CompilerParams(vmem_limit_bytes=18 * 2**20),
        cost_estimate=SHORT,
        name="output_wgrad",
    )(index, heads, *grads)


def swap_cores(values):
    count = lax.axis_size("seq")
    return lax.ppermute(values, "seq", [(i, i ^ 1) for i in range(count)])


def from_chip(values, step):
    count = lax.axis_size("seq")
    return lax.ppermute(values, "seq", [((i + 2 * step) % count, i) for i in range(count)])


def from_shard(values, flip):
    return lax.ppermute(values, "shard", [(i, i ^ flip) for i in range(4)])


def both_cores(same):
    return [block for one in same for block in (one, swap_cores(one))]


def core_sum(near, other):
    return near.astype(F32) + swap_cores(other.astype(BF16)).astype(F32)


def after(token, values):
    return lax.optimization_barrier((values, token))[0]


def join(token, *values):
    return lax.optimization_barrier((token,) + values)[0]


def first_hops(block):
    return [from_shard(block, 1), from_shard(block, 2)]


def second_hops(first):
    rows = first[0].shape[0] // 2
    return [from_shard(first[0][:rows], 2), from_shard(first[1][rows:], 1)]


def scatter_shard_first(parts):
    rows = parts[3].shape[0] // 2
    low = parts[3].astype(BF16)
    return from_shard(low[:rows], 1), from_shard(low[rows:], 2)


def scatter_shard_last(parts, first):
    rows = parts[3].shape[0] // 2
    top, bottom = first
    one, two = parts[1].astype(F32), parts[2].astype(F32)
    one = jnp.concatenate([one[:rows], one[rows:] + bottom.astype(F32)])
    two = jnp.concatenate([two[:rows] + top.astype(F32), two[rows:]])
    return from_shard(one.astype(BF16), 1), from_shard(two.astype(BF16), 2)


def slot_block(slot, place, half):
    z, core = place // 2, place % 2
    return ((z + slot // 2) % half) * 2 + (core + slot) % 2


def rotate_rows(front, back, cos_t, sin_t):
    return jnp.concatenate([front * cos_t - back * sin_t, back * cos_t + front * sin_t], axis=-2)


def per_device(
    layer_input,
    doc_lengths,
    norm_gain,
    query_weight,
    key_weight,
    value_weight,
    output_weight,
    feed_gain,
    gate_weight,
    up_weight,
    down_weight,
    output_grad,
):
    tok, width = layer_input.shape
    seqs, shards = lax.axis_size("seq"), lax.axis_size("shard")
    shard, seq = lax.axis_index("shard"), lax.axis_index("seq")
    span = tok * seqs
    half_head = HEAD_DIM // 2
    place = jnp.reshape(seq, (1,)).astype(jnp.int32)

    positions = jnp.arange(shards * span, dtype=jnp.int32).reshape(shards, span)
    span_blocks = slot_block(jnp.arange(seqs, dtype=jnp.int32), seq.astype(jnp.int32), seqs // 2)
    bounds = doc_bounds(doc_lengths, positions)
    exponent = -2.0 * jnp.arange(half_head, dtype=jnp.float32) / HEAD_DIM
    inverse = jnp.power(jnp.float32(ROPE_BASE), exponent)
    angles = positions.astype(F32)[:, None, :] * inverse[None, :, None]
    cos_all, sin_all = jnp.cos(angles), jnp.sin(angles)
    cos_own = lax.dynamic_index_in_dim(cos_all, shard, 0, keepdims=False)
    sin_own = lax.dynamic_index_in_dim(sin_all, shard, 0, keepdims=False)

    steps = seqs // 2
    z, core = seq // 2, seq % 2
    shard_at = jnp.reshape(shard, (1,)).astype(jnp.int32)
    gain_row = norm_gain[None, :]
    heads_here = HEADS // seqs
    own_rows = query_weight.shape[0]
    attn_weights = (query_weight, key_weight, value_weight)
    slot = jnp.arange(HEADS, dtype=jnp.int32)

    packed = pack_columns(place, gain_row, attn_weights, seqs)
    point = join(jnp.zeros((), F32), packed)
    from_other = swap_cores(packed[1])
    gate_first = first_hops(after(point, gate_weight))
    col_blocks = []
    for step in range(steps):
        block = jnp.concatenate([packed[0, step], from_other[step]])
        col_blocks.append(from_chip(block, -step) if step else block)
    point = join(point, col_blocks)
    col_block = jnp.concatenate(after(point, col_blocks))
    col_first = first_hops(col_block)
    own_input = after(point, layer_input)
    input_one, input_three = from_chip(own_input, 1), from_chip(own_input, -1)
    point = join(point, col_first, input_one, input_three, gate_first)
    col_far = second_hops(after(point, col_first))
    input_two = from_chip(after(point, input_one), 1)
    input_slots = both_cores([own_input, after(point, input_one)])
    input_last = both_cores([after(point, input_three)])
    gate_far = second_hops(after(point, gate_first))
    point = join(point, col_far, input_two, input_slots, input_last)
    input_slots += both_cores([after(point, input_two)]) + input_last
    rel_blocks = (
        (shard ^ (slot // seqs)) * seqs
        + (z + steps - slot % seqs // 2) % steps * 2
        + (core ^ (slot % 2))
    ).astype(jnp.int32)
    columns = order_blocks([col_block] + col_first + after(point, col_far), rel_blocks, own_rows)
    unit_low = unit_tokens(span_blocks, input_slots)
    qkv = lax.dot_general(
        columns, unit_low, (((0,), (1,)), ((), ())), preferred_element_type=F32
    ).reshape(shards, 3, HEAD_DIM, span)
    turned = rotate_rows(
        qkv[:, :2, :half_head], qkv[:, :2, half_head:], cos_own[None, None], sin_own[None, None]
    )
    qkv_low = jnp.concatenate([turned, qkv[:, 2:]], axis=1).astype(BF16)
    qkv_low = qkv_low.reshape(shards, 3 * HEAD_DIM, span)
    output_own = after(point, output_weight)
    output_one, output_three = from_chip(output_own, 1), from_chip(output_own, -1)
    up_top, up_bottom = up_weight[: up_weight.shape[0] // 2], up_weight[up_weight.shape[0] // 2 :]
    up_first = [
        from_shard(after(point, half), flip) for half in (up_top, up_bottom) for flip in (1, 2)
    ]
    point = join(point, qkv_low, gate_far, output_one, output_three, up_first)

    head_qkv = lax.all_to_all(
        after(point, qkv_low), "shard", split_axis=0, concat_axis=0, tiled=True
    )
    output_two = from_chip(after(point, output_one), 1)
    own_grad = after(point, output_grad)
    grad_one = from_chip(own_grad, 1)
    point = join(point, head_qkv, output_two, grad_one)
    output_own = jnp.concatenate(after(point, [output_own, output_one, output_two, output_three]))
    output_first = first_hops(output_own)
    output_swapped = [swap_cores(output_own)]
    grad_two, grad_three = from_chip(after(point, grad_one), 1), from_chip(own_grad, -1)
    gain_rows = jnp.pad(feed_gain[None, :], ((0, EXTRA - 1), (0, tok - own_rows)))
    head_out, head_low, out_blocks, lse = attend(
        after(point, head_qkv), gain_rows, tok, shard_at, bounds
    )
    point = join(point, out_blocks, output_first, output_swapped, grad_two, grad_three)
    token_blocks = lax.all_to_all(
        after(point, out_blocks), ("shard", "seq"), split_axis=0, concat_axis=0, tiled=True
    )
    output_far = second_hops(after(point, output_first))
    output_swapped += [swap_cores(piece) for piece in after(point, output_first)]
    point = join(point, token_blocks, output_far, output_swapped)
    gain_two = token_blocks[:, HEAD_DIM, :own_rows].astype(F32).reshape(1, width)
    output_swapped += [swap_cores(piece) for piece in after(point, output_far)]
    up_far = [from_shard(after(point, up_first[0]), 2), from_shard(after(point, up_first[3]), 1)]
    output_pieces = [output_own] + output_first + output_far + output_swapped
    rel_heads = (
        (shard ^ (slot // steps % shards)) * seqs
        + (z + slot % steps) % steps * 2
        + (core ^ (slot // (HEADS // 2)))
    ).astype(jnp.int32)
    middle, normed_two, scale_two = project(
        rel_heads, after(point, token_blocks), layer_input, gain_two, output_pieces
    )
    point = join(point, normed_two)

    own_tokens = after(point, normed_two)
    tokens_one, tokens_three = from_chip(own_tokens, 1), from_chip(own_tokens, -1)
    down_first = first_hops(after(point, down_weight))
    grad_slots = both_cores(after(point, [output_grad, grad_one, grad_two, grad_three]))
    point = join(point, tokens_one, tokens_three, down_first, grad_slots, up_far)
    tokens_two = from_chip(after(point, tokens_one), 1)
    down_far = second_hops(after(point, down_first))
    feed_slots = both_cores([own_tokens, after(point, tokens_one)])
    first_two = load_weights(
        [
            after(point, [gate_weight, *gate_first, *gate_far]),
            [up_weight, up_first[0], up_first[2], up_first[1], up_first[3], *up_far],
        ]
    )
    output_here = load_weights([after(point, output_pieces)])
    feed_last = both_cores([after(point, tokens_three)])
    point = join(point, tokens_two, down_far, feed_slots, feed_last, first_two, output_here)
    feed_slots += both_cores([after(point, tokens_two)]) + feed_last
    down_here = load_weights([[down_weight, *down_first, *after(point, down_far)]])
    order = (2, 1, 3, 0)

    def feed(step, tokens, whole):
        here = slice(2 * step, 2 * step + 2)
        return feed_blocks(
            order.index(step), seqs, shard_at, tokens, grad_slots[here], first_two, down_here, whole
        )

    parts_two, whole = feed(2, feed_slots[4:6], None)
    sum_two = core_sum(*parts_two).astype(BF16)
    point = join(point, sum_two)
    arrived_two = from_chip(after(point, sum_two), -2)
    parts_one, whole = feed(1, after(point, feed_slots[2:4]), whole)
    parts_three, whole = feed(3, feed_slots[6:8], whole)
    parts_own, whole = feed(0, feed_slots[0:2], whole)
    head_slots = [head_low[0]] + [from_shard(after(point, head_low[k]), k) for k in range(1, 4)]
    point = join(point, arrived_two, parts_one, parts_three, parts_own, head_slots)
    sum_one = core_sum(*after(point, parts_one)).astype(BF16)
    sum_three = core_sum(*after(point, parts_three)).astype(BF16)
    point = join(point, sum_one, sum_three)
    arrived_one = from_chip(after(point, sum_one), -1)
    arrived_three = from_chip(after(point, sum_three), 1)
    sum_own = core_sum(*after(point, parts_own))
    feed_low, span_grad, hidden, gate_grad, up_grad, down_near, down_other = after(point, whole)
    feed_wparts = feed_wgrads(shards, gate_grad, up_grad, hidden, feed_low, span_grad)
    point = join(point, sum_own, feed_wparts, arrived_one, arrived_three)
    middle_grad, attend_grad, head_grad = token_grad(
        rel_heads,
        [sum_own, *after(point, [arrived_one, arrived_two, arrived_three])],
        middle,
        scale_two,
        gain_two,
        output_grad,
        output_here,
    )
    point = join(point, head_grad)

    out_grad_blocks = lax.all_to_all(
        after(point, head_grad), ("shard", "seq"), split_axis=0, concat_axis=0, tiled=True
    )
    feed_wsum = lax.psum_scatter(
        after(point, feed_wparts).reshape(-1, width), "shard", scatter_dimension=0, tiled=True
    ).reshape(3, -1, width)
    own_agrad = after(point, attend_grad)
    agrad_one = from_chip(own_agrad, 1)
    down_all = core_sum(after(point, down_near), down_other).astype(BF16)
    down_sums = [down_all[order.index(step)] for step in range(steps)]
    pair = jnp.concatenate([own_agrad, down_sums[2]])
    point = join(point, out_grad_blocks, agrad_one, pair, down_sums[3])
    both = from_chip(after(point, pair), -1)
    down_three = from_chip(after(point, down_sums[3]), 1)
    back = attend_back(
        head_qkv, lse, head_out, after(point, out_grad_blocks), cos_all, sin_all, tok, bounds
    )
    point = join(point, back, both, down_three)
    agrad_three, down_two = both[:tok], both[tok:]
    span_back = lax.all_to_all(
        after(point, back), "shard", split_axis=0, concat_axis=0, tiled=True
    ).reshape(heads_here * 3 * HEAD_DIM, span)
    agrad_two = from_chip(after(point, agrad_one), 1)
    down_one = from_chip(
        (down_sums[1].astype(F32) + after(point, down_two).astype(F32)).astype(BF16), -1
    )
    agrad_slots = both_cores([after(point, own_agrad), agrad_one, agrad_two, agrad_three])
    out_part = output_wgrad_parts(span_blocks, jnp.stack(head_slots), agrad_slots)
    out_parts = [out_part[k] for k in range(4)]
    out_first = scatter_shard_first(out_parts)
    point = join(point, span_back, down_one, out_first)

    span_back = after(point, span_back)
    cols_part = cols_parts_of(shard_at, span_back, unit_low, shards)
    point = join(point, cols_part)
    cols_parts = [after(point, cols_part)[k] for k in range(4)]
    cols_first = scatter_shard_first(cols_parts)
    unit_near, unit_other = unit_back(span_blocks, after(point, span_back), columns, tok)
    unit_swapped = swap_cores(unit_other)
    point = join(point, unit_near, unit_swapped)
    unit_sums = unit_near + after(point, unit_swapped).astype(F32)
    unit_two = from_chip(unit_sums[2].astype(BF16), -1)
    unit_three = from_chip(unit_sums[3].astype(BF16), 1)
    out_last = scatter_shard_last(out_parts, after(point, out_first))
    layer_output = (
        middle
        + down_sums[0].astype(F32)
        + after(point, down_one).astype(F32)
        + down_three.astype(F32)
    ).astype(BF16)
    gain_rows_back = out_grad_blocks[:, HEAD_DIM].astype(F32)
    gain_two_out = jnp.sum(
        gain_rows_back[:, :own_rows] + gain_rows_back[:, own_rows : 2 * own_rows], axis=0
    )
    point, layer_output, gain_two_out = lax.optimization_barrier(
        (join(point, unit_two, unit_three, cols_first, out_last), layer_output, gain_two_out)
    )
    unit_one = from_chip((unit_sums[1] + after(point, unit_two).astype(F32)).astype(BF16), -1)
    cols_last = scatter_shard_last(cols_parts, after(point, cols_first))
    point = join(point, unit_one, cols_last)
    cols_near, cols_other = spread_columns(
        place, cols_parts[0], *after(point, cols_last), steps
    )
    cols_blocks = pair_columns(cols_near, swap_cores(cols_other))
    point = join(point, cols_blocks)
    cols_same = list(after(point, cols_blocks))
    cols_same = cols_same[:1] + [from_chip(cols_same[step], -step) for step in range(1, steps)]
    out_one, out_two = after(point, out_last)
    output_wgrad = out_parts[0].astype(F32) + out_one.astype(F32) + out_two.astype(F32)
    unit_grad = unit_sums[0] + after(point, unit_one).astype(F32) + unit_three.astype(F32)
    inputs = layer_input.astype(F32)
    scale_one = lax.rsqrt(jnp.mean(inputs * inputs, axis=-1, keepdims=True) + NORM_EPS)
    unit_rows = inputs * scale_one
    input_grad = (
        middle_grad
        + scale_one * (unit_grad - unit_rows * jnp.mean(unit_grad * unit_rows, axis=-1, keepdims=True))
    ).astype(BF16)
    gate_wgrad, up_wgrad, down_wgrad = [
        after(point, feed_wsum)[m].astype(F32) for m in range(3)
    ]
    point, output_wgrad, input_grad, gate_wgrad, up_wgrad, down_wgrad, cols_same = (
        lax.optimization_barrier(
            (
                *(point, output_wgrad, input_grad, gate_wgrad, up_wgrad, down_wgrad),
                cols_same,
            )
        )
    )
    query_wgrad, key_wgrad, value_wgrad, gain_one_out = unpack_columns(
        place, gain_row, attn_weights, after(point, cols_same)
    )
    return (
        layer_output,
        input_grad,
        gain_one_out.reshape(-1),
        query_wgrad,
        key_wgrad,
        value_wgrad,
        output_wgrad,
        gain_two_out,
        gate_wgrad,
        up_wgrad,
        down_wgrad,
    )


def solution(mesh):
    shards, seqs = mesh.shape["shard"], mesh.shape["seq"]
    body = per_device if shards == 4 and shards * seqs == HEADS else per_device_any
    return jax.shard_map(
        body,
        mesh=mesh,
        in_specs=(
            P(("shard", "seq"), None),
            P(),
            P(("shard", "seq")),
            P(("shard", "seq"), None),
            P(("shard", "seq"), None),
            P(("shard", "seq"), None),
            P(("shard", "seq"), None),
            P(("shard", "seq")),
            P(("shard", "seq"), None),
            P(("shard", "seq"), None),
            P(("shard", "seq"), None),
            P(("shard", "seq"), None),
        ),
        out_specs=(
            P(("shard", "seq"), None),
            P(("shard", "seq"), None),
            P(("shard", "seq")),
            P(("shard", "seq"), None),
            P(("shard", "seq"), None),
            P(("shard", "seq"), None),
            P(("shard", "seq"), None),
            P(("shard", "seq")),
            P(("shard", "seq"), None),
            P(("shard", "seq"), None),
            P(("shard", "seq"), None),
        ),
        check_vma=False,
    )
```

```python
import functools
import math

import jax
import jax.numpy as jnp
from jax import lax
from jax.experimental import pallas as pl
from jax.experimental.pallas import tpu as pltpu
from jax.sharding import PartitionSpec as P

HEAD_DIM = 64


NORM_EPS = 1e-05
ROPE_BASE = 130000.0


def rope_tables(positions, width):
    half_width = width // 2
    exponent = -2.0 * jnp.arange(half_width, dtype=jnp.float32) / width
    inverse = jnp.power(jnp.float32(ROPE_BASE), exponent)
    angles = positions.astype(jnp.float32)[:, None] * inverse[None, :]
    return (jnp.cos(angles), jnp.sin(angles))


def rotate(values, cos_table, sin_table):
    half_width = values.shape[-1] // 2
    front = values[..., :half_width]
    back_half = values[..., half_width:]
    cos_wide = cos_table[:, None, :]
    sin_wide = sin_table[:, None, :]
    return jnp.concatenate(
        [front * cos_wide - back_half * sin_wide, back_half * cos_wide + front * sin_wide], axis=-1
    )


def unrotate(values, cos_table, sin_table):
    half_width = values.shape[-1] // 2
    front = values[..., :half_width]
    back_half = values[..., half_width:]
    cos_wide = cos_table[:, None, :]
    sin_wide = sin_table[:, None, :]
    return jnp.concatenate(
        [front * cos_wide + back_half * sin_wide, back_half * cos_wide - front * sin_wide], axis=-1
    )


def doc_numbers(doc_lengths, positions):
    doc_ends = jnp.cumsum(doc_lengths)
    return jnp.sum((doc_ends[:, None] <= positions[None, :]).astype(jnp.int32), axis=0)


def normalize(values, gain_vec):
    scale_row = lax.rsqrt(jnp.mean(values * values, axis=-1, keepdims=True) + NORM_EPS)
    return (values * scale_row * gain_vec, scale_row)


def norm_back(grad_in, values, scale_row, gain_vec):
    unit_rows = values * scale_row
    gain_grad = jnp.sum(grad_in * unit_rows, axis=0)
    unit_grad = grad_in * gain_vec
    value_grad = scale_row * (
        unit_grad - unit_rows * jnp.mean(unit_grad * unit_rows, axis=-1, keepdims=True)
    )
    return (value_grad, gain_grad)


def times_trans(lhs_mat, rhs_mat):
    return lax.dot_general(
        lhs_mat, rhs_mat, (((1,), (1,)), ((), ())), preferred_element_type=jnp.float32
    )


def trans_times(lhs_mat, rhs_mat):
    return lax.dot_general(
        lhs_mat, rhs_mat, (((0,), (0,)), ((), ())), preferred_element_type=jnp.float32
    )


def per_device_any(
    layer_input,
    doc_lengths,
    norm_gain,
    query_weight,
    key_weight,
    value_weight,
    output_weight,
    feed_gain,
    gate_weight,
    up_weight,
    down_weight,
    output_grad,
):
    tok_rows = layer_input.shape[0]
    width = layer_input.shape[1]
    seq_count = lax.axis_size("seq")
    shard_count = lax.axis_size("shard")
    span_len = tok_rows * seq_count
    stream_len = span_len * shard_count
    span_start = lax.axis_index("shard") * span_len
    own_positions = (
        span_start + lax.axis_index("seq") * tok_rows + jnp.arange(tok_rows, dtype=jnp.int32)
    )
    span_positions = span_start + jnp.arange(span_len, dtype=jnp.int32)
    all_positions = jnp.arange(stream_len, dtype=jnp.int32)
    key_docs = doc_numbers(doc_lengths, all_positions)
    query_docs = lax.dynamic_slice_in_dim(key_docs, span_start, span_len)
    score_scale = HEAD_DIM ** (-0.5)
    gathered = (
        lax.all_gather(query_weight, ("shard", "seq"), axis=0, tiled=True),
        lax.all_gather(key_weight, ("shard", "seq"), axis=0, tiled=True),
        lax.all_gather(value_weight, ("shard", "seq"), axis=0, tiled=True),
        lax.all_gather(output_weight, ("shard", "seq"), axis=0, tiled=True),
        lax.all_gather(norm_gain, ("shard", "seq"), axis=0, tiled=True),
        lax.all_gather(feed_gain, ("shard", "seq"), axis=0, tiled=True),
    )
    query_full, key_full, value_full, output_full = (
        gathered[0],
        gathered[1],
        gathered[2],
        gathered[3],
    )
    gain_one = gathered[4].astype(jnp.float32)
    gain_two = gathered[5].astype(jnp.float32)
    inputs = layer_input.astype(jnp.float32)
    normed, scale_one = normalize(inputs, gain_one)
    normed_low = normed.astype(jnp.bfloat16)
    own_cos, own_sin = rope_tables(own_positions, HEAD_DIM)
    query_proj = jnp.dot(normed_low, query_full, preferred_element_type=jnp.float32)
    key_proj = jnp.dot(normed_low, key_full, preferred_element_type=jnp.float32)
    value_proj = jnp.dot(normed_low, value_full, preferred_element_type=jnp.float32)
    query_rot = rotate(query_proj.reshape(tok_rows, -1, HEAD_DIM), own_cos, own_sin).reshape(
        tok_rows, width
    )
    key_rot = rotate(key_proj.reshape(tok_rows, -1, HEAD_DIM), own_cos, own_sin).reshape(
        tok_rows, width
    )
    stacked = jnp.stack(
        [
            query_rot.astype(jnp.bfloat16),
            key_rot.astype(jnp.bfloat16),
            value_proj.astype(jnp.bfloat16),
        ]
    )
    head_triple = lax.all_to_all(stacked, "seq", split_axis=2, concat_axis=1, tiled=True)
    head_width = head_triple.shape[2]
    heads_dev = head_width // HEAD_DIM
    head_query = head_triple[0].reshape(span_len, heads_dev, HEAD_DIM)
    key_value = lax.all_gather(head_triple[1:], "shard", axis=1, tiled=True)
    key_block = math.gcd(stream_len, max(512, stream_len // 16))
    block_count = stream_len // key_block
    key_blocks = key_value[0].reshape(block_count, key_block, heads_dev, HEAD_DIM)
    value_blocks = key_value[1].reshape(block_count, key_block, heads_dev, HEAD_DIM)
    pos_blocks = all_positions.reshape(block_count, key_block)
    doc_blocks = key_docs.reshape(block_count, key_block)

    def block_scores(key_blk, key_pos, key_doc):
        scores = (
            jnp.einsum("qhd,khd->hqk", head_query, key_blk, preferred_element_type=jnp.float32)
            * score_scale
        )
        allowed = (key_pos[None, :] <= span_positions[:, None]) & (
            key_doc[None, :] == query_docs[:, None]
        )
        return jnp.where(allowed[None], scores, -jnp.inf)

    def total_step(state_pair, pieces):
        run_max, run_sum = state_pair
        scores = block_scores(pieces[0], pieces[1], pieces[2])
        new_max = jnp.maximum(run_max, jnp.max(scores, axis=-1))
        new_sum = run_sum * jnp.exp(run_max - new_max) + jnp.sum(
            jnp.exp(scores - new_max[..., None]), axis=-1
        )
        return ((new_max, new_sum), None)

    start_max = jnp.full((heads_dev, span_len), -1e30, jnp.float32)
    start_sum = jnp.zeros((heads_dev, span_len), jnp.float32)
    totals, unused = lax.scan(
        total_step, (start_max, start_sum), (key_blocks, pos_blocks, doc_blocks)
    )
    log_total = totals[0] + jnp.log(totals[1])

    def output_step(accum, pieces):
        scores = block_scores(pieces[0], pieces[2], pieces[3])
        probs = jnp.exp(scores - log_total[..., None]).astype(jnp.bfloat16)
        return (
            accum
            + jnp.einsum("hqk,khd->qhd", probs, pieces[1], preferred_element_type=jnp.float32),
            None,
        )

    start_acc = jnp.zeros((span_len, heads_dev, HEAD_DIM), jnp.float32)
    head_out32, unused = lax.scan(
        output_step, start_acc, (key_blocks, value_blocks, pos_blocks, doc_blocks)
    )
    head_out = head_out32.reshape(span_len, head_width).astype(jnp.bfloat16)
    token_out = lax.all_to_all(head_out, "seq", split_axis=0, concat_axis=1, tiled=True)
    middle = inputs + jnp.dot(token_out, output_full, preferred_element_type=jnp.float32)
    normed_two, scale_two = normalize(middle, gain_two)
    feed_low = normed_two.astype(jnp.bfloat16)
    feed_mats = (
        lax.all_gather(gate_weight, ("shard", "seq"), axis=0, tiled=True),
        lax.all_gather(up_weight, ("shard", "seq"), axis=0, tiled=True),
        lax.all_gather(down_weight, ("shard", "seq"), axis=0, tiled=True),
    )
    gate_full, up_full, down_full = (feed_mats[0], feed_mats[1], feed_mats[2])
    gate_val = times_trans(feed_low, gate_full)
    up_val = times_trans(feed_low, up_full)
    hidden = (jax.nn.silu(gate_val) * up_val).astype(jnp.bfloat16)
    down_val = jnp.dot(hidden, down_full, preferred_element_type=jnp.float32)
    layer_output = (middle + down_val).astype(jnp.bfloat16)
    hidden_grad = times_trans(output_grad, down_full)
    sigmoid_val = jax.nn.sigmoid(gate_val)
    gate_grad = (
        hidden_grad * up_val * (sigmoid_val * (1.0 + gate_val * (1.0 - sigmoid_val)))
    ).astype(jnp.bfloat16)
    up_grad = (hidden_grad * jax.nn.silu(gate_val)).astype(jnp.bfloat16)
    feed_grad = jnp.dot(gate_grad, gate_full, preferred_element_type=jnp.float32) + jnp.dot(
        up_grad, up_full, preferred_element_type=jnp.float32
    )
    feed_sums = lax.psum_scatter(
        jnp.stack(
            [
                trans_times(gate_grad, feed_low),
                trans_times(up_grad, feed_low),
                trans_times(hidden, output_grad),
            ],
            axis=1,
        ),
        ("shard", "seq"),
        scatter_dimension=0,
        tiled=True,
    )
    middle_norm_grad, gain_two_grad = norm_back(feed_grad, middle, scale_two, gain_two)
    middle_grad = output_grad.astype(jnp.float32) + middle_norm_grad
    attend_grad = middle_grad.astype(jnp.bfloat16)
    output_term = trans_times(token_out, attend_grad)
    token_out_grad = times_trans(attend_grad, output_full).astype(jnp.bfloat16)
    head_out_grad = lax.all_to_all(
        token_out_grad, "seq", split_axis=1, concat_axis=0, tiled=True
    ).reshape(span_len, heads_dev, HEAD_DIM)
    row_dots = jnp.transpose(jnp.sum(head_out_grad.astype(jnp.float32) * head_out32, axis=-1))

    def grad_step(query_acc, pieces):
        key_blk, value_blk, key_pos, key_doc = pieces
        scores = block_scores(key_blk, key_pos, key_doc)
        probs = jnp.exp(scores - log_total[..., None])
        prob_grad = jnp.einsum(
            "qhd,khd->hqk", head_out_grad, value_blk, preferred_element_type=jnp.float32
        )
        score_grad = (probs * (prob_grad - row_dots[..., None])).astype(jnp.bfloat16)
        query_next = query_acc + score_scale * jnp.einsum(
            "hqk,khd->qhd", score_grad, key_blk, preferred_element_type=jnp.float32
        )
        key_part = score_scale * jnp.einsum(
            "hqk,qhd->khd", score_grad, head_query, preferred_element_type=jnp.float32
        )
        value_part = jnp.einsum(
            "hqk,qhd->khd",
            probs.astype(jnp.bfloat16),
            head_out_grad,
            preferred_element_type=jnp.float32,
        )
        return (query_next, (key_part, value_part))

    query_grad, block_grads = lax.scan(
        grad_step, start_acc, (key_blocks, value_blocks, pos_blocks, doc_blocks)
    )
    pair_grads = jnp.stack(
        [
            block_grads[0].reshape(stream_len, head_width),
            block_grads[1].reshape(stream_len, head_width),
        ]
    )
    own_pair = lax.psum_scatter(
        pair_grads.astype(jnp.bfloat16), "shard", scatter_dimension=1, tiled=True
    ).astype(jnp.float32)
    span_cos, span_sin = rope_tables(span_positions, HEAD_DIM)
    query_back = unrotate(query_grad, span_cos, span_sin).reshape(span_len, head_width)
    key_back = unrotate(
        own_pair[0].reshape(span_len, heads_dev, HEAD_DIM), span_cos, span_sin
    ).reshape(span_len, head_width)
    back_stack = jnp.stack([query_back, key_back, own_pair[1]]).astype(jnp.bfloat16)
    token_grads = lax.all_to_all(back_stack, "seq", split_axis=1, concat_axis=2, tiled=True)
    norm_grad = (
        times_trans(token_grads[0], query_full)
        + times_trans(token_grads[1], key_full)
        + times_trans(token_grads[2], value_full)
    )
    input_norm_grad, gain_one_grad = norm_back(norm_grad, inputs, scale_one, gain_one)
    input_grad = (middle_grad + input_norm_grad).astype(jnp.bfloat16)
    query_term = trans_times(normed_low, token_grads[0])
    key_term = trans_times(normed_low, token_grads[1])
    value_term = trans_times(normed_low, token_grads[2])
    summed = (
        lax.psum_scatter(query_term, ("shard", "seq"), scatter_dimension=0, tiled=True),
        lax.psum_scatter(key_term, ("shard", "seq"), scatter_dimension=0, tiled=True),
        lax.psum_scatter(value_term, ("shard", "seq"), scatter_dimension=0, tiled=True),
        lax.psum_scatter(output_term, ("shard", "seq"), scatter_dimension=0, tiled=True),
        lax.psum_scatter(gain_one_grad, ("shard", "seq"), scatter_dimension=0, tiled=True),
        lax.psum_scatter(gain_two_grad, ("shard", "seq"), scatter_dimension=0, tiled=True),
    )
    query_wgrad, key_wgrad, value_wgrad = (summed[0], summed[1], summed[2])
    output_wgrad, gain_one_out, gain_two_out = (summed[3], summed[4], summed[5])
    return (
        layer_output,
        input_grad,
        gain_one_out,
        query_wgrad,
        key_wgrad,
        value_wgrad,
        output_wgrad,
        gain_two_out,
        feed_sums[:, 0],
        feed_sums[:, 1],
        feed_sums[:, 2],
    )


HEADS = 32
EXTRA = 16
BF16 = jnp.bfloat16
F32 = jnp.float32


SHORT = pl.CostEstimate(flops=0, bytes_accessed=0, transcendentals=0)


def in_hbm(arrays):
    return [pltpu.with_memory_space_constraint(array, pltpu.HBM) for array in arrays]


def dot_nn(lhs_mat, rhs_mat):
    return lax.dot_general(
        lhs_mat, rhs_mat, (((1,), (0,)), ((), ())), preferred_element_type=jnp.float32
    )


def allowed_pairs(i, j, keys, cols, span, start_ref, same):
    shape = (keys.stop - keys.start, cols.stop - cols.start)
    k_pos = j * span + keys.start + lax.broadcasted_iota(jnp.int32, shape, 0)
    begun = k_pos >= start_ref[i][:, cols]
    if not same:
        return begun
    q_pos = i * span + cols.start + lax.broadcasted_iota(jnp.int32, shape, 1)
    return (k_pos <= q_pos) & begun


def own_span_parts(span):
    half = span // 2
    return (slice(0, half), slice(0, half)), (slice(0, span), slice(half, span))


def fwd_kernel(tok, shard_ref, lo_ref, full_ref, start_ref, qkv_ref, gain_ref, out_ref, low_ref, blocks_ref,
               lse_ref, k_nat, m_s, l_s, acc_s):
    i = pl.program_id(0)
    spans, rows, span = qkv_ref.shape
    slots = span // tok
    scale2 = HEAD_DIM ** -0.5 * math.log2(math.e)

    @pl.when(i == 0)
    def _():
        for s in range(spans):
            k_nat[pl.ds(s * span, span), :] = qkv_ref[s, HEAD_DIM : 2 * HEAD_DIM, :].T

    m_s[...] = jnp.full_like(m_s, -1e30)
    l_s[...] = jnp.zeros_like(l_s)
    acc_s[...] = jnp.zeros_like(acc_s)

    def step(j, masked, same=False, keys=slice(0, span), cols=slice(0, span)):
        k_rows = pl.ds(pl.multiple_of(j * span + keys.start, 128), keys.stop - keys.start)
        s_t = dot_nn(k_nat[k_rows, :], qkv_ref[i, :HEAD_DIM, cols]) * scale2
        if masked:
            s_t = jnp.where(allowed_pairs(i, j, keys, cols, span, start_ref, same), s_t, -jnp.inf)
        m_old = m_s[:, cols]
        m_new = jnp.maximum(m_old, jnp.max(s_t, axis=0, keepdims=True))
        alpha = jnp.exp2(m_old - m_new)
        p_t = jnp.exp2(s_t - m_new)
        l_s[:, cols] = l_s[:, cols] * alpha + jnp.sum(p_t, axis=0, keepdims=True)
        m_s[:, cols] = m_new
        acc_s[:, cols] = acc_s[:, cols] * alpha + dot_nn(
            qkv_ref[j, 2 * HEAD_DIM :, keys], p_t.astype(jnp.bfloat16)
        )

    def loop_body(masked):
        def body(j, carry):
            step(j, masked)
            return carry

        return body

    lax.fori_loop(lo_ref[i], full_ref[i], loop_body(True), 0)
    lax.fori_loop(full_ref[i], i, loop_body(False), 0)
    for keys, cols in own_span_parts(span):
        step(i, True, True, keys, cols)
    out = acc_s[...] / l_s[...]
    out_ref[0] = out
    low = out.astype(jnp.bfloat16)
    low_ref[i ^ shard_ref[0]] = low
    lse_ref[0] = m_s[...] + jnp.log2(l_s[...])
    for slot in range(slots):
        blocks_ref[slot, :HEAD_DIM] = low[:, slot * tok : (slot + 1) * tok]
        blocks_ref[slot, HEAD_DIM:] = gain_ref[...]


def bwd_kernel(tok, hi_ref, full_ref, start_ref, qkv_ref, lse_ref, out_hbm, dob_ref,
               cos_ref, sin_ref, back_ref, dq_s, dk_s, dv_s, do_s, di_s, out_ref, sem):
    j = pl.program_id(0)
    spans, rows, span = qkv_ref.shape
    slots = span // tok
    scale = HEAD_DIM ** -0.5
    scale2 = scale * math.log2(math.e)

    @pl.when(j == 0)
    def _():
        copy = pltpu.make_async_copy(out_hbm, out_ref, sem)
        copy.start()
        dq_s[...] = jnp.zeros_like(dq_s)
        for s in range(spans):
            for slot in range(slots):
                do_s[s, :, slot * tok : (slot + 1) * tok] = dob_ref[s * slots + slot, :HEAD_DIM]
        copy.wait()
        for s in range(spans):
            di_s[s] = jnp.sum(do_s[s].astype(jnp.float32) * out_ref[s], axis=0, keepdims=True)

    k_nat = qkv_ref[j, HEAD_DIM : 2 * HEAD_DIM, :].T
    v_nat = qkv_ref[j, 2 * HEAD_DIM :, :].T
    dk_s[...] = jnp.zeros_like(dk_s)
    dv_s[...] = jnp.zeros_like(dv_s)

    def step(i, masked, same=False, keys=slice(0, span), cols=slice(0, span)):
        q_t = qkv_ref[i, :HEAD_DIM, cols]
        p_t = jnp.exp2(dot_nn(k_nat[keys], q_t) * scale2 - lse_ref[i][:, cols])
        if masked:
            p_t = jnp.where(allowed_pairs(i, j, keys, cols, span, start_ref, same), p_t, 0.0)
        do_t = do_s[i, :, cols]
        dv_s[:, keys] += times_trans(do_t, p_t.astype(jnp.bfloat16))
        ds_t = (p_t * (dot_nn(v_nat[keys], do_t) - di_s[i][:, cols])).astype(jnp.bfloat16)
        dk_s[:, keys] += times_trans(q_t, ds_t)
        dq_s[i, :, cols] += dot_nn(qkv_ref[j, HEAD_DIM : 2 * HEAD_DIM, keys], ds_t)

    for keys, cols in own_span_parts(span):
        step(j, True, True, keys, cols)

    def body(i, carry):
        whole = full_ref[i] <= j

        @pl.when(whole)
        def _():
            step(i, False)

        @pl.when(jnp.logical_not(whole))
        def _():
            step(i, True)

        return carry

    lax.fori_loop(j + 1, hi_ref[j], body, 0)

    def turned_back(grad):
        front, back_half = grad[: HEAD_DIM // 2], grad[HEAD_DIM // 2 :]
        cos_t, sin_t = cos_ref[0], sin_ref[0]
        return jnp.concatenate(
            [front * cos_t + back_half * sin_t, back_half * cos_t - front * sin_t], axis=0
        ).astype(jnp.bfloat16)

    back_ref[0, :HEAD_DIM] = turned_back(dq_s[j] * scale)
    back_ref[0, HEAD_DIM : 2 * HEAD_DIM] = turned_back(dk_s[...] * scale)
    back_ref[0, 2 * HEAD_DIM :] = dv_s[...].astype(jnp.bfloat16)


def doc_bounds(doc_lengths, positions):
    spans, span = positions.shape
    ends = jnp.cumsum(doc_lengths)
    over = ends[:, None, None] <= positions[None]
    start = jnp.max(jnp.where(over, ends[:, None, None], 0), axis=0).astype(jnp.int32)
    stop = jnp.min(jnp.where(over, spans * span, ends[:, None, None]), axis=0).astype(jnp.int32)
    first = jnp.min(start, axis=1) // span
    whole = jnp.minimum(
        (jnp.max(start, axis=1) + span - 1) // span, jnp.arange(spans, dtype=jnp.int32)
    )
    last = (jnp.max(stop, axis=1) + span - 1) // span
    return start[:, None, :], first, whole, last


def attend(qkv, gain_rows, tok, shard, bounds):
    spans, rows, span = qkv.shape
    stream = spans * span
    slots = span // tok
    start, first, whole, last = bounds
    smem = pl.BlockSpec(memory_space=pltpu.SMEM)
    vmem = pl.BlockSpec(memory_space=pltpu.VMEM)

    def one(*block):
        return pl.BlockSpec((1,) + block, lambda i: (i, 0, 0))

    return pl.pallas_call(
        functools.partial(fwd_kernel, tok),
        grid=(spans,),
        in_specs=[smem, smem, smem, vmem, vmem, vmem],
        out_specs=[
            one(HEAD_DIM, span),
            pl.BlockSpec((spans, HEAD_DIM, span), lambda i: (0, 0, 0)),
            pl.BlockSpec((slots, HEAD_DIM + EXTRA, tok), lambda i: (i, 0, 0)),
            one(1, span),
        ],
        out_shape=[
            pltpu.HBM((spans, HEAD_DIM, span), jnp.float32),
            pltpu.HBM((spans, HEAD_DIM, span), jnp.bfloat16),
            pltpu.HBM((stream // tok, HEAD_DIM + EXTRA, tok), jnp.bfloat16),
            jax.ShapeDtypeStruct((spans, 1, span), jnp.float32),
        ],
        scratch_shapes=[
            pltpu.VMEM((stream, HEAD_DIM), jnp.bfloat16),
            pltpu.VMEM((1, span), jnp.float32),
            pltpu.VMEM((1, span), jnp.float32),
            pltpu.VMEM((HEAD_DIM, span), jnp.float32),
        ],
        compiler_params=pltpu.CompilerParams(vmem_limit_bytes=24 * 2**20),
        cost_estimate=pl.CostEstimate(
            flops=stream * stream * 256 * 5, bytes_accessed=stream * 1024, transcendentals=0
        ),
        name="attend",
    )(shard, first, whole, start, qkv, gain_rows)


def attend_back(qkv, lse, out, out_grad, cos_t, sin_t, tok, bounds):
    spans, rows, span = qkv.shape
    stream = spans * span
    start, first, whole, last = bounds
    smem = pl.BlockSpec(memory_space=pltpu.SMEM)
    vmem = pl.BlockSpec(memory_space=pltpu.VMEM)

    def one(*block):
        return pl.BlockSpec((1,) + block, lambda j: (j, 0, 0))

    return pl.pallas_call(
        functools.partial(bwd_kernel, tok),
        grid=(spans,),
        in_specs=[smem, smem, vmem, vmem, vmem, pl.BlockSpec(memory_space=pl.ANY), vmem]
        + [one(HEAD_DIM // 2, span)] * 2,
        out_specs=one(rows, span),
        out_shape=pltpu.HBM(qkv.shape, jnp.bfloat16),
        scratch_shapes=[
            pltpu.VMEM((spans, HEAD_DIM, span), jnp.float32),
            pltpu.VMEM((HEAD_DIM, span), jnp.float32),
            pltpu.VMEM((HEAD_DIM, span), jnp.float32),
            pltpu.VMEM((spans, HEAD_DIM, span), jnp.bfloat16),
            pltpu.VMEM((spans, 1, span), jnp.float32),
            pltpu.VMEM((spans, HEAD_DIM, span), jnp.float32),
            pltpu.SemaphoreType.DMA,
        ],
        compiler_params=pltpu.CompilerParams(vmem_limit_bytes=32 * 2**20),
        cost_estimate=pl.CostEstimate(
            flops=stream * stream * 256 * 7, bytes_accessed=stream * 1024, transcendentals=0
        ),
        name="attend_back",
    )(last, whole, start, qkv, lse, *in_hbm([out]), out_grad, *in_hbm([cos_t, sin_t]))


def as_column(row):
    shape = (row.shape[1], row.shape[1])
    same = lax.broadcasted_iota(jnp.int32, shape, 0) == lax.broadcasted_iota(jnp.int32, shape, 1)
    return jnp.sum(jnp.where(same, row.astype(jnp.float32), 0.0), axis=1, keepdims=True)


def pack_kernel(heads, place_ref, gain_ref, query_ref, key_ref, value_ref, out_ref):
    steps = out_ref.shape[1]
    seqs = 2 * steps
    z, core = place_ref[0] // 2, place_ref[0] % 2
    gain_col = as_column(gain_ref[...])
    for m, ref in enumerate((query_ref, key_ref, value_ref)):
        rows = (ref[...].astype(jnp.float32) * gain_col).astype(jnp.bfloat16)
        for head in range(heads):
            at = (head // seqs * 3 + m) * HEAD_DIM
            other = (core + head) % 2
            step = (head % seqs // 2 + steps - z) % steps
            out_ref[other, step, :, at : at + HEAD_DIM] = rows[
                :, head * HEAD_DIM : (head + 1) * HEAD_DIM
            ]


def pack_columns(place, gain_row, weights, seqs):
    rows, width = weights[0].shape
    heads = width // HEAD_DIM
    vmem = pl.BlockSpec(memory_space=pltpu.VMEM)
    return pl.pallas_call(
        functools.partial(pack_kernel, heads),
        in_specs=[pl.BlockSpec(memory_space=pltpu.SMEM)] + [vmem] * 4,
        out_specs=vmem,
        out_shape=jax.ShapeDtypeStruct(
            (2, seqs // 2, rows, heads // seqs * 3 * HEAD_DIM), jnp.bfloat16
        ),
        cost_estimate=SHORT,
        name="pack_columns",
    )(place, gain_row, *weights)


def order_kernel(index_ref, *refs):
    out_ref = refs[-1]
    rows = out_ref.shape[1]
    count = 0
    for ref in refs[:-1]:
        for i in range(ref.shape[0] // rows):
            out_ref[index_ref[count]] = ref[i * rows : (i + 1) * rows]
            count += 1


def order_blocks(pieces, index, rows):
    vmem = pl.BlockSpec(memory_space=pltpu.VMEM)
    blocks = sum(piece.shape[0] for piece in pieces) // rows
    width = pieces[0].shape[1]
    return pl.pallas_call(
        order_kernel,
        in_specs=[pl.BlockSpec(memory_space=pltpu.SMEM)] + [vmem] * len(pieces),
        out_specs=vmem,
        out_shape=jax.ShapeDtypeStruct((blocks, rows, width), pieces[0].dtype),
        compiler_params=pltpu.CompilerParams(vmem_limit_bytes=12 * 2**20),
        cost_estimate=SHORT,
        name="order_blocks",
    )(index, *pieces).reshape(blocks * rows, width)


def cols_kernel(shard_ref, back_ref, unit_hbm, out_ref, unit_s, sem):
    slots, _, width = out_ref.shape
    copies = [
        pltpu.make_async_copy(
            unit_hbm.at[:, pl.ds(pl.multiple_of((shard_ref[0] ^ k) * width, width), width)],
            unit_s.at[k],
            sem.at[k],
        )
        for k in range(slots)
    ]
    for copy in copies:
        copy.start()
    for k in range(slots):
        copies[k].wait()
        out_ref[k] = dot_nn(back_ref[...], unit_s[k]).astype(jnp.bfloat16)


def cols_parts_of(shard, back, unit_low, slots):
    rows = back.shape[0]
    tokens = unit_low.shape[0]
    width = unit_low.shape[1] // slots
    vmem = pl.BlockSpec(memory_space=pltpu.VMEM)
    return pl.pallas_call(
        cols_kernel,
        in_specs=[
            pl.BlockSpec(memory_space=pltpu.SMEM), vmem, pl.BlockSpec(memory_space=pl.ANY)
        ],
        out_specs=vmem,
        out_shape=jax.ShapeDtypeStruct((slots, rows, width), jnp.bfloat16),
        scratch_shapes=[
            pltpu.VMEM((slots, tokens, width), unit_low.dtype),
            pltpu.SemaphoreType.DMA((slots,)),
        ],
        compiler_params=pltpu.CompilerParams(vmem_limit_bytes=24 * 2**20),
        cost_estimate=SHORT,
        name="cols_parts",
    )(shard, back, *in_hbm([unit_low]))


def unit_back_kernel(index_ref, back_ref, columns_ref, near_ref, other_ref):
    steps, tok, _ = near_ref.shape
    for step in range(steps):
        lanes = [
            back_ref[:, pl.ds(pl.multiple_of(index_ref[2 * step + c] * tok, tok), tok)]
            for c in range(2)
        ]
        part = times_trans(jnp.concatenate(lanes, axis=1).T, columns_ref[...])
        near_ref[step] = part[:tok]
        other_ref[step] = part[tok:].astype(jnp.bfloat16)


def unit_back(index, back, columns, tok):
    steps = back.shape[1] // (2 * tok)
    width = columns.shape[0]
    vmem = pl.BlockSpec(memory_space=pltpu.VMEM)
    return pl.pallas_call(
        unit_back_kernel,
        in_specs=[pl.BlockSpec(memory_space=pltpu.SMEM)] + [vmem] * 2,
        out_specs=[vmem] * 2,
        out_shape=[
            jax.ShapeDtypeStruct((steps, tok, width), jnp.float32),
            jax.ShapeDtypeStruct((steps, tok, width), jnp.bfloat16),
        ],
        compiler_params=pltpu.CompilerParams(vmem_limit_bytes=24 * 2**20),
        cost_estimate=SHORT,
        name="unit_back",
    )(index, back, columns)


def spread_kernel(place_ref, own_ref, one_ref, two_ref, near_ref, other_ref, both_s):
    steps, rows, _ = near_ref.shape
    z, core = place_ref[0] // 2, place_ref[0] % 2
    total = own_ref[...].astype(jnp.float32)
    total += one_ref[...].astype(jnp.float32) + two_ref[...].astype(jnp.float32)
    total = total.T.astype(jnp.bfloat16)
    for q in range(2 * steps):
        both_s[(core + q) % 2, (q // 2 + steps - z) % steps] = total[q * rows : (q + 1) * rows]
    near_ref[...] = both_s[0]
    other_ref[...] = both_s[1]


def spread_columns(place, own, one, two, steps):
    columns, rows = own.shape
    vmem = pl.BlockSpec(memory_space=pltpu.VMEM)
    shape = (steps, rows // (2 * steps), columns)
    return pl.pallas_call(
        spread_kernel,
        in_specs=[pl.BlockSpec(memory_space=pltpu.SMEM)] + [vmem] * 3,
        out_specs=[vmem] * 2,
        out_shape=[jax.ShapeDtypeStruct(shape, jnp.bfloat16)] * 2,
        scratch_shapes=[pltpu.VMEM((2,) + shape, jnp.bfloat16)],
        cost_estimate=SHORT,
        name="spread_columns",
    )(place, own, one, two)


def pair_kernel(spread_ref, other_ref, *out_refs):
    for step, out_ref in enumerate(out_refs):
        out_ref[...] = jnp.concatenate([spread_ref[step], other_ref[step]])


def pair_columns(spread, other):
    steps, rows, columns = other.shape
    vmem = pl.BlockSpec(memory_space=pltpu.VMEM)
    return pl.pallas_call(
        pair_kernel,
        in_specs=[vmem] * 2,
        out_specs=[vmem] * steps,
        out_shape=[jax.ShapeDtypeStruct((2 * rows, columns), other.dtype)] * steps,
        cost_estimate=SHORT,
        name="pair_columns",
    )(spread, other)


def unpack_kernel(heads, place_ref, gain_ref, query_ref, key_ref, value_ref, *refs):
    out_refs, cols_s = refs[-5:-1], refs[-1]
    steps = len(refs) - 5
    rows = query_ref.shape[0]
    seqs = 2 * steps
    z, core = place_ref[0] // 2, place_ref[0] % 2
    for step in range(steps):
        cols_s[0, step] = refs[step][:rows]
        cols_s[1, step] = refs[step][rows:]
    gain_col = as_column(gain_ref[...])
    total = jnp.zeros((rows, 1), jnp.float32)
    for m, ref in enumerate((query_ref, key_ref, value_ref)):
        grads = jnp.concatenate(
            [
                cols_s[
                    (core + head) % 2,
                    (z + steps - head % seqs // 2) % steps,
                    :,
                    (head // seqs * 3 + m) * HEAD_DIM : (head // seqs * 3 + m + 1) * HEAD_DIM,
                ]
                for head in range(heads)
            ],
            axis=1,
        ).astype(jnp.float32)
        total += jnp.sum(grads * ref[...].astype(jnp.float32), axis=1, keepdims=True)
        out_refs[m][...] = grads * gain_col
    out_refs[3][...] = jnp.broadcast_to(total, (rows, 128)).T[:1]


def unpack_columns(place, gain_row, weights, cols):
    rows, width = weights[0].shape
    vmem = pl.BlockSpec(memory_space=pltpu.VMEM)
    return pl.pallas_call(
        functools.partial(unpack_kernel, width // HEAD_DIM),
        in_specs=[pl.BlockSpec(memory_space=pltpu.SMEM)] + [vmem] * (4 + len(cols)),
        out_specs=[vmem] * 4,
        out_shape=[jax.ShapeDtypeStruct((rows, width), jnp.float32)] * 3
        + [jax.ShapeDtypeStruct((1, rows), jnp.float32)],
        scratch_shapes=[pltpu.VMEM((2, len(cols), rows, cols[0].shape[1]), cols[0].dtype)],
        cost_estimate=SHORT,
        name="unpack_columns",
    )(place, gain_row, *weights, *cols)


def unit_kernel(index_ref, *refs):
    out_ref = refs[-1]
    tok = refs[0].shape[0]
    for slot, ref in enumerate(refs[:-1]):
        rows = ref[...].astype(jnp.float32)
        scale = lax.rsqrt(jnp.mean(rows * rows, axis=-1, keepdims=True) + NORM_EPS)
        at = pl.ds(pl.multiple_of(index_ref[slot] * tok, tok), tok)
        out_ref[at, :] = (rows * scale).astype(jnp.bfloat16)


def unit_tokens(index, slots):
    tok, width = slots[0].shape
    vmem = pl.BlockSpec(memory_space=pltpu.VMEM)
    return pl.pallas_call(
        unit_kernel,
        in_specs=[pl.BlockSpec(memory_space=pltpu.SMEM)] + [vmem] * len(slots),
        out_specs=vmem,
        out_shape=jax.ShapeDtypeStruct((len(slots) * tok, width), jnp.bfloat16),
        compiler_params=pltpu.CompilerParams(vmem_limit_bytes=16 * 2**20),
        cost_estimate=SHORT,
        name="unit_tokens",
    )(index, *slots)


def join_kernel(*refs):
    rows = refs[0].shape[0]
    for i, ref in enumerate(refs[:-1]):
        refs[-1][i * rows : (i + 1) * rows] = ref[...]


def join_rows(arrays):
    rows, width = arrays[0].shape
    vmem = pl.BlockSpec(memory_space=pltpu.VMEM)
    return pl.pallas_call(
        join_kernel,
        in_specs=[vmem] * len(arrays),
        out_specs=vmem,
        out_shape=jax.ShapeDtypeStruct((len(arrays) * rows, width), arrays[0].dtype),
        cost_estimate=SHORT,
        name="join_rows",
    )(*arrays)


def load_kernel(layout, *refs):
    pieces, out_ref, sem = refs[:-2], refs[-2], refs[-1]
    copies = [
        pltpu.make_async_copy(ref, out_ref.at[m, pl.ds(row, ref.shape[0])], sem.at[i])
        for i, (ref, (m, row)) in enumerate(zip(pieces, layout, strict=True))
    ]
    for copy in copies:
        copy.start()
    for copy in copies:
        copy.wait()


def load_weights(matrices):
    layout, pieces = [], []
    for m, matrix in enumerate(matrices):
        row = 0
        for piece in matrix:
            layout.append((m, row))
            pieces.append(piece)
            row += piece.shape[0]
    shape = (len(matrices), row, pieces[0].shape[1])
    return pl.pallas_call(
        functools.partial(load_kernel, tuple(layout)),
        in_specs=[pl.BlockSpec(memory_space=pl.ANY)] * len(pieces),
        out_specs=pl.BlockSpec(memory_space=pltpu.VMEM),
        out_shape=pltpu.VMEM(shape, pieces[0].dtype),
        scratch_shapes=[pltpu.SemaphoreType.DMA((len(pieces),))],
        cost_estimate=SHORT,
        compiler_params=pltpu.CompilerParams(vmem_limit_bytes=14 * 2**20),
        name="load_weights",
    )(*in_hbm(pieces))


def feed_kernel(call, aliased, *refs):
    shard_ref, tokens, grads, first_ref, down_ref = refs[0], refs[1:3], refs[3:5], refs[5], refs[6]
    refs = refs[7 + aliased :]
    part_near, part_other = refs[:2]
    all_refs = refs[2:9]
    tok_s, grad_s, hidden_s, gate_s, up_s, hidden_t, gate_t, up_t, down_s, sem = refs[9:]
    tok, width = tokens[0].shape
    shards, block = 4, down_ref.shape[1] // 4
    rows = pl.ds(2 * tok * call, 2 * tok)
    for c in range(2):
        tok_s[c * tok : (c + 1) * tok] = tokens[c][...]
        grad_s[c * tok : (c + 1) * tok] = grads[c][...]
    copies = [
        pltpu.make_async_copy(tok_s, all_refs[0].at[rows], sem.at[0]),
        pltpu.make_async_copy(grad_s, all_refs[1].at[rows], sem.at[1]),
    ]
    for copy in copies:
        copy.start()
    for b in range(shards):
        at = slice(b * block, (b + 1) * block)
        place = pl.ds(pl.multiple_of((shard_ref[0] ^ b) * block, block), block)
        gate_val = times_trans(tok_s[...], first_ref[0, at])
        up_val = times_trans(tok_s[...], first_ref[1, at])
        hidden_grad = times_trans(grad_s[...], down_ref[0, at])
        sigmoid_val = 1.0 / (1.0 + jnp.exp(-gate_val))
        silu_val = gate_val * sigmoid_val
        hidden = (silu_val * up_val).astype(jnp.bfloat16)
        gate_grad = (
            hidden_grad * up_val * (sigmoid_val + silu_val * (1.0 - sigmoid_val))
        ).astype(jnp.bfloat16)
        up_grad = (hidden_grad * silu_val).astype(jnp.bfloat16)
        for value, by_unit, by_token in (
            (hidden, hidden_t, hidden_s), (gate_grad, gate_t, gate_s), (up_grad, up_t, up_s)
        ):
            by_unit[place, :] = value.T
            by_token[:, at] = value
    late = [
        pltpu.make_async_copy(src, dst.at[:, rows], sem.at[2 + i])
        for i, (src, dst) in enumerate(zip((hidden_t, gate_t, up_t), all_refs[2:5], strict=True))
    ]
    for copy in late:
        copy.start()
    for c in range(4):
        at = slice(c * (width // 4), (c + 1) * (width // 4))
        down = dot_nn(hidden_s[...], down_ref[0, :, at]).astype(jnp.bfloat16)
        down_s[0, :, at] = down[:tok]
        down_s[1, :, at] = down[tok:]
    last = [
        pltpu.make_async_copy(down_s.at[c], all_refs[5 + c].at[call], sem.at[5 + c])
        for c in range(2)
    ]
    for copy in last:
        copy.start()
    for c in range(4):
        at = slice(c * (width // 4), (c + 1) * (width // 4))
        part = dot_nn(gate_s[...], first_ref[0, :, at]) + dot_nn(up_s[...], first_ref[1, :, at])
        part_near[:, at] = part[:tok]
        part_other[:, at] = part[tok:].astype(jnp.bfloat16)
    for copy in copies + late + last:
        copy.wait()


def feed_blocks(call, slots, shard, tokens, grads, first_two, down, whole):
    tok, width = tokens[0].shape
    units = down.shape[1]
    anywhere = pl.BlockSpec(memory_space=pl.ANY)
    vmem = pl.BlockSpec(memory_space=pltpu.VMEM)
    low, full = jnp.bfloat16, jnp.float32
    shapes = (
        [(slots * tok, width)] * 2
        + [(units, slots * tok)] * 3
        + [(slots // 2, tok, width)] * 2
    )
    whole = in_hbm(whole or [])
    out = pl.pallas_call(
        functools.partial(feed_kernel, call, len(whole)),
        in_specs=[pl.BlockSpec(memory_space=pltpu.SMEM)] + [vmem] * 6 + [anywhere] * len(whole),
        out_specs=[vmem] * 2 + [anywhere] * 7,
        out_shape=[jax.ShapeDtypeStruct((tok, width), full), jax.ShapeDtypeStruct((tok, width), low)]
        + [pltpu.HBM(shape, low) for shape in shapes],
        input_output_aliases={7 + i: 2 + i for i in range(len(whole))},
        scratch_shapes=[pltpu.VMEM((2 * tok, width), low)] * 2
        + [pltpu.VMEM((2 * tok, units), low)] * 3
        + [pltpu.VMEM((units, 2 * tok), low)] * 3
        + [pltpu.VMEM((2, tok, width), low), pltpu.SemaphoreType.DMA((7,))],
        compiler_params=pltpu.CompilerParams(vmem_limit_bytes=30 * 2**20),
        cost_estimate=SHORT,
        name="feed_blocks",
    )(
        shard,
        *tokens,
        *grads,
        *[pltpu.with_memory_space_constraint(weight, pltpu.VMEM) for weight in (first_two, down)],
        *whole,
    )
    return out[:2], out[2:]


def start_pieces(pieces, weight_s, sem):
    places, row = [], 0
    for i, ref in enumerate(pieces):
        at = pl.ds(row, ref.shape[0])
        copy = pltpu.make_async_copy(ref, weight_s.at[at], sem.at[i])
        copy.start()
        places.append((row, ref.shape[0], copy))
        row += ref.shape[0]
    return places


def project_kernel(index_ref, blocks_ref, input_ref, gain_ref, *refs):
    pieces, (middle_ref, normed_ref, scale_ref, weight_s, sem) = refs[:-5], refs[-5:]
    places = start_pieces(pieces, weight_s, sem)
    heads = blocks_ref.shape[0]
    rows = jnp.concatenate([blocks_ref[index_ref[i], :HEAD_DIM] for i in range(heads)]).T
    total = input_ref[...].astype(jnp.float32)
    for row, size, copy in places:
        copy.wait()
        total += dot_nn(rows[:, row : row + size], weight_s[row : row + size])
    scale = lax.rsqrt(jnp.mean(total * total, axis=-1, keepdims=True) + NORM_EPS)
    middle_ref[...] = total
    normed_ref[...] = (total * scale * gain_ref[...]).astype(jnp.bfloat16)
    scale_ref[...] = jnp.broadcast_to(scale, scale_ref.shape)


def project(index, blocks, inputs, gain, pieces):
    tok, width = inputs.shape
    vmem = pl.BlockSpec(memory_space=pltpu.VMEM)
    return pl.pallas_call(
        project_kernel,
        in_specs=[pl.BlockSpec(memory_space=pltpu.SMEM)]
        + [vmem] * 3
        + [pl.BlockSpec(memory_space=pl.ANY)] * len(pieces),
        out_specs=[vmem] * 3,
        out_shape=[
            jax.ShapeDtypeStruct((tok, width), jnp.float32),
            jax.ShapeDtypeStruct((tok, width), jnp.bfloat16),
            jax.ShapeDtypeStruct((tok, 128), jnp.float32),
        ],
        scratch_shapes=[
            pltpu.VMEM((HEADS * HEAD_DIM, width), jnp.bfloat16),
            pltpu.SemaphoreType.DMA((len(pieces),)),
        ],
        compiler_params=pltpu.CompilerParams(vmem_limit_bytes=18 * 2**20),
        cost_estimate=SHORT,
        name="project",
    )(index, blocks, inputs, gain, *in_hbm(pieces))


def token_grad_kernel(
    index_ref, own_ref, one_ref, two_ref, three_ref, middle_ref, scale_ref, gain_ref, grad_ref, *refs
):
    weight_ref, middle_grad_ref, low_ref, out_ref = refs
    normed_grad = own_ref[...]
    for ref in (one_ref, two_ref, three_ref):
        normed_grad += ref[...].astype(jnp.float32)
    tok = normed_grad.shape[0]
    scale = scale_ref[:, :1]
    unit = middle_ref[...] * scale
    gain_part = jnp.sum(normed_grad * unit, axis=0, keepdims=True)
    unit_grad = normed_grad * gain_ref[...]
    middle_grad = grad_ref[...].astype(jnp.float32) + scale * (
        unit_grad - unit * jnp.mean(unit_grad * unit, axis=-1, keepdims=True)
    )
    middle_grad_ref[...] = middle_grad
    low = middle_grad.astype(jnp.bfloat16)
    low_ref[...] = low
    grad_t = low.T
    size = weight_ref.shape[1] // 8
    for row in range(0, weight_ref.shape[1], size):
        out = dot_nn(weight_ref[0, row : row + size], grad_t).astype(jnp.bfloat16)
        for i in range(size // HEAD_DIM):
            out_ref[index_ref[row // HEAD_DIM + i], :HEAD_DIM] = out[
                i * HEAD_DIM : (i + 1) * HEAD_DIM
            ]
    coarse = gain_part.astype(jnp.bfloat16)
    fine = (gain_part - coarse.astype(jnp.float32)).astype(jnp.bfloat16)
    wide = gain_part.shape[1] // out_ref.shape[0]
    for head in range(out_ref.shape[0]):
        at = slice(head * wide, (head + 1) * wide)
        row = jnp.concatenate([coarse[:, at], fine[:, at]], axis=1)
        out_ref[head, HEAD_DIM:] = jnp.broadcast_to(row, (EXTRA, tok))


def token_grad(index, sums, middle, scale, gain, output_grad, weight):
    tok, width = middle.shape
    vmem = pl.BlockSpec(memory_space=pltpu.VMEM)
    return pl.pallas_call(
        token_grad_kernel,
        in_specs=[pl.BlockSpec(memory_space=pltpu.SMEM)]
        + [vmem] * 9,
        out_specs=[vmem] * 3,
        out_shape=[
            jax.ShapeDtypeStruct((tok, width), jnp.float32),
            jax.ShapeDtypeStruct((tok, width), jnp.bfloat16),
            pltpu.HBM((HEADS, HEAD_DIM + EXTRA, tok), jnp.bfloat16),
        ],
        compiler_params=pltpu.CompilerParams(vmem_limit_bytes=20 * 2**20),
        cost_estimate=SHORT,
        name="token_grad",
    )(
        index,
        *sums,
        middle,
        scale,
        gain,
        output_grad,
        pltpu.with_memory_space_constraint(weight, pltpu.VMEM),
    )


def feed_wgrad_kernel(gate_ref, up_ref, hidden_ref, tokens_ref, grads_ref, out_ref):
    tokens, grads = tokens_ref[...], grads_ref[...]
    out_ref[0, 0] = dot_nn(gate_ref[...], tokens).astype(jnp.bfloat16)
    out_ref[0, 1] = dot_nn(up_ref[...], tokens).astype(jnp.bfloat16)
    out_ref[0, 2] = dot_nn(hidden_ref[...], grads).astype(jnp.bfloat16)


def feed_wgrads(shards, gate_grad, up_grad, hidden, feed_low, span_grad):
    units, tokens = hidden.shape
    width = feed_low.shape[1]
    block = units // shards
    cuts = 2
    half = width // cuts
    rows = pl.BlockSpec((block, tokens), lambda c, i: (i, 0))
    every = pl.BlockSpec((tokens, half), lambda c, i: (0, c))
    return pl.pallas_call(
        feed_wgrad_kernel,
        grid=(cuts, shards),
        in_specs=[rows] * 3 + [every] * 2,
        out_specs=pl.BlockSpec((1, 3, block, half), lambda c, i: (i, 0, 0, c)),
        out_shape=pltpu.HBM((shards, 3, block, width), jnp.bfloat16),
        compiler_params=pltpu.CompilerParams(vmem_limit_bytes=24 * 2**20),
        cost_estimate=SHORT,
        name="feed_wgrads",
    )(*in_hbm([gate_grad, up_grad, hidden, feed_low, span_grad]))


def output_wgrad_kernel(index_ref, heads_ref, *refs):
    grads, (out_ref, grads_s) = refs[:-2], refs[-2:]
    tok = grads[0].shape[0]
    for slot, ref in enumerate(grads):
        grads_s[pl.ds(pl.multiple_of(index_ref[slot] * tok, tok), tok), :] = ref[...]
    for k in range(heads_ref.shape[0]):
        out_ref[k] = dot_nn(heads_ref[k], grads_s[...]).astype(jnp.bfloat16)


def output_wgrad_parts(index, heads, grads):
    tok, width = grads[0].shape
    vmem = pl.BlockSpec(memory_space=pltpu.VMEM)
    return pl.pallas_call(
        output_wgrad_kernel,
        in_specs=[pl.BlockSpec(memory_space=pltpu.SMEM)] + [vmem] * (1 + len(grads)),
        out_specs=vmem,
        out_shape=jax.ShapeDtypeStruct((heads.shape[0], HEAD_DIM, width), jnp.bfloat16),
        scratch_shapes=[pltpu.VMEM((len(grads) * tok, width), jnp.bfloat16)],
        compiler_params=pltpu.CompilerParams(vmem_limit_bytes=18 * 2**20),
        cost_estimate=SHORT,
        name="output_wgrad",
    )(index, heads, *grads)


def swap_cores(values):
    count = lax.axis_size("seq")
    return lax.ppermute(values, "seq", [(i, i ^ 1) for i in range(count)])


def from_chip(values, step):
    count = lax.axis_size("seq")
    return lax.ppermute(values, "seq", [((i + 2 * step) % count, i) for i in range(count)])


def from_shard(values, flip):
    return lax.ppermute(values, "shard", [(i, i ^ flip) for i in range(4)])


def both_cores(same):
    return [block for one in same for block in (one, swap_cores(one))]


def core_sum(near, other):
    return near.astype(F32) + swap_cores(other.astype(BF16)).astype(F32)


def after(token, values):
    return lax.optimization_barrier((values, token))[0]


def join(token, *values):
    return lax.optimization_barrier((token,) + values)[0]


def first_hops(block):
    return [from_shard(block, 1), from_shard(block, 2)]


def second_hops(first):
    rows = first[0].shape[0] // 2
    return [from_shard(first[0][:rows], 2), from_shard(first[1][rows:], 1)]


def scatter_shard_first(parts):
    rows = parts[3].shape[0] // 2
    low = parts[3].astype(BF16)
    return from_shard(low[:rows], 1), from_shard(low[rows:], 2)


def scatter_shard_last(parts, first):
    rows = parts[3].shape[0] // 2
    top, bottom = first
    one, two = parts[1].astype(F32), parts[2].astype(F32)
    one = jnp.concatenate([one[:rows], one[rows:] + bottom.astype(F32)])
    two = jnp.concatenate([two[:rows] + top.astype(F32), two[rows:]])
    return from_shard(one.astype(BF16), 1), from_shard(two.astype(BF16), 2)


def slot_block(slot, place, half):
    z, core = place // 2, place % 2
    return ((z + slot // 2) % half) * 2 + (core + slot) % 2


def rotate_rows(front, back, cos_t, sin_t):
    return jnp.concatenate([front * cos_t - back * sin_t, back * cos_t + front * sin_t], axis=-2)


def per_device(
    layer_input,
    doc_lengths,
    norm_gain,
    query_weight,
    key_weight,
    value_weight,
    output_weight,
    feed_gain,
    gate_weight,
    up_weight,
    down_weight,
    output_grad,
):
    tok, width = layer_input.shape
    seqs, shards = lax.axis_size("seq"), lax.axis_size("shard")
    shard, seq = lax.axis_index("shard"), lax.axis_index("seq")
    span = tok * seqs
    half_head = HEAD_DIM // 2
    place = jnp.reshape(seq, (1,)).astype(jnp.int32)

    positions = jnp.arange(shards * span, dtype=jnp.int32).reshape(shards, span)
    span_blocks = slot_block(jnp.arange(seqs, dtype=jnp.int32), seq.astype(jnp.int32), seqs // 2)
    bounds = doc_bounds(doc_lengths, positions)
    exponent = -2.0 * jnp.arange(half_head, dtype=jnp.float32) / HEAD_DIM
    inverse = jnp.power(jnp.float32(ROPE_BASE), exponent)
    angles = positions.astype(F32)[:, None, :] * inverse[None, :, None]
    cos_all, sin_all = jnp.cos(angles), jnp.sin(angles)
    cos_own = lax.dynamic_index_in_dim(cos_all, shard, 0, keepdims=False)
    sin_own = lax.dynamic_index_in_dim(sin_all, shard, 0, keepdims=False)

    steps = seqs // 2
    z, core = seq // 2, seq % 2
    shard_at = jnp.reshape(shard, (1,)).astype(jnp.int32)
    gain_row = norm_gain[None, :]
    heads_here = HEADS // seqs
    own_rows = query_weight.shape[0]
    attn_weights = (query_weight, key_weight, value_weight)
    slot = jnp.arange(HEADS, dtype=jnp.int32)

    packed = pack_columns(place, gain_row, attn_weights, seqs)
    point = join(jnp.zeros((), F32), packed)
    from_other = swap_cores(packed[1])
    gate_first = first_hops(after(point, gate_weight))
    col_blocks = []
    for step in range(steps):
        block = jnp.concatenate([packed[0, step], from_other[step]])
        col_blocks.append(from_chip(block, -step) if step else block)
    point = join(point, col_blocks)
    col_block = jnp.concatenate(after(point, col_blocks))
    col_first = first_hops(col_block)
    own_input = after(point, layer_input)
    input_one, input_three = from_chip(own_input, 1), from_chip(own_input, -1)
    point = join(point, col_first, input_one, input_three, gate_first)
    col_far = second_hops(after(point, col_first))
    input_two = from_chip(after(point, input_one), 1)
    input_slots = both_cores([own_input, after(point, input_one)])
    input_last = both_cores([after(point, input_three)])
    gate_far = second_hops(after(point, gate_first))
    point = join(point, col_far, input_two, input_slots, input_last)
    input_slots += both_cores([after(point, input_two)]) + input_last
    rel_blocks = (
        (shard ^ (slot // seqs)) * seqs
        + (z + steps - slot % seqs // 2) % steps * 2
        + (core ^ (slot % 2))
    ).astype(jnp.int32)
    columns = order_blocks([col_block] + col_first + after(point, col_far), rel_blocks, own_rows)
    unit_low = unit_tokens(span_blocks, input_slots)
    qkv = lax.dot_general(
        columns, unit_low, (((0,), (1,)), ((), ())), preferred_element_type=F32
    ).reshape(shards, 3, HEAD_DIM, span)
    turned = rotate_rows(
        qkv[:, :2, :half_head], qkv[:, :2, half_head:], cos_own[None, None], sin_own[None, None]
    )
    qkv_low = jnp.concatenate([turned, qkv[:, 2:]], axis=1).astype(BF16)
    qkv_low = qkv_low.reshape(shards, 3 * HEAD_DIM, span)
    output_own = after(point, output_weight)
    output_one, output_three = from_chip(output_own, 1), from_chip(output_own, -1)
    up_top, up_bottom = up_weight[: up_weight.shape[0] // 2], up_weight[up_weight.shape[0] // 2 :]
    up_first = [
        from_shard(after(point, half), flip) for half in (up_top, up_bottom) for flip in (1, 2)
    ]
    point = join(point, qkv_low, gate_far, output_one, output_three, up_first)

    head_qkv = lax.all_to_all(
        after(point, qkv_low), "shard", split_axis=0, concat_axis=0, tiled=True
    )
    output_two = from_chip(after(point, output_one), 1)
    point = join(point, head_qkv, output_two)
    output_own = jnp.concatenate(after(point, [output_own, output_one, output_two, output_three]))
    output_first = first_hops(output_own)
    output_swapped = [swap_cores(output_own)]
    own_grad = after(point, output_grad)
    grad_one, grad_three = from_chip(own_grad, 1), from_chip(own_grad, -1)
    gain_rows = jnp.pad(feed_gain[None, :], ((0, EXTRA - 1), (0, tok - own_rows)))
    head_out, head_low, out_blocks, lse = attend(
        after(point, head_qkv), gain_rows, tok, shard_at, bounds
    )
    point = join(point, out_blocks, output_first, output_swapped, grad_one, grad_three)
    token_blocks = lax.all_to_all(
        after(point, out_blocks), ("shard", "seq"), split_axis=0, concat_axis=0, tiled=True
    )
    output_far = second_hops(after(point, output_first))
    output_swapped += [swap_cores(piece) for piece in after(point, output_first)]
    grad_two = from_chip(after(point, grad_one), 1)
    point = join(point, token_blocks, output_far, output_swapped, grad_two)
    gain_two = token_blocks[:, HEAD_DIM, :own_rows].astype(F32).reshape(1, width)
    output_swapped += [swap_cores(piece) for piece in after(point, output_far)]
    up_far = [from_shard(after(point, up_first[0]), 2), from_shard(after(point, up_first[3]), 1)]
    output_pieces = [output_own] + output_first + output_far + output_swapped
    rel_heads = (
        (shard ^ (slot // steps % shards)) * seqs
        + (z + slot % steps) % steps * 2
        + (core ^ (slot // (HEADS // 2)))
    ).astype(jnp.int32)
    middle, normed_two, scale_two = project(
        rel_heads, after(point, token_blocks), layer_input, gain_two, output_pieces
    )
    point = join(point, normed_two)

    own_tokens = after(point, normed_two)
    tokens_one, tokens_three = from_chip(own_tokens, 1), from_chip(own_tokens, -1)
    down_first = first_hops(after(point, down_weight))
    grad_slots = both_cores(after(point, [output_grad, grad_one, grad_two, grad_three]))
    point = join(point, tokens_one, tokens_three, down_first, grad_slots, up_far)
    tokens_two = from_chip(after(point, tokens_one), 1)
    down_far = second_hops(after(point, down_first))
    feed_slots = both_cores([own_tokens, after(point, tokens_one)])
    first_two = load_weights(
        [
            after(point, [gate_weight, *gate_first, *gate_far]),
            [up_weight, up_first[0], up_first[2], up_first[1], up_first[3], *up_far],
        ]
    )
    output_here = load_weights([after(point, output_pieces)])
    feed_last = both_cores([after(point, tokens_three)])
    point = join(point, tokens_two, down_far, feed_slots, feed_last, first_two, output_here)
    feed_slots += both_cores([after(point, tokens_two)]) + feed_last
    down_here = load_weights([[down_weight, *down_first, *after(point, down_far)]])
    order = (2, 1, 3, 0)

    def feed(step, tokens, whole):
        here = slice(2 * step, 2 * step + 2)
        return feed_blocks(
            order.index(step), seqs, shard_at, tokens, grad_slots[here], first_two, down_here, whole
        )

    parts_two, whole = feed(2, feed_slots[4:6], None)
    sum_two = core_sum(*parts_two).astype(BF16)
    point = join(point, sum_two)
    arrived_two = from_chip(after(point, sum_two), -2)
    parts_one, whole = feed(1, after(point, feed_slots[2:4]), whole)
    parts_three, whole = feed(3, feed_slots[6:8], whole)
    parts_own, whole = feed(0, feed_slots[0:2], whole)
    head_slots = [head_low[0]] + [from_shard(after(point, head_low[k]), k) for k in range(1, 4)]
    point = join(point, arrived_two, parts_one, parts_three, parts_own, head_slots)
    sum_one = core_sum(*after(point, parts_one)).astype(BF16)
    sum_three = core_sum(*after(point, parts_three)).astype(BF16)
    point = join(point, sum_one, sum_three)
    arrived_one = from_chip(after(point, sum_one), -1)
    arrived_three = from_chip(after(point, sum_three), 1)
    sum_own = core_sum(*after(point, parts_own))
    feed_low, span_grad, hidden, gate_grad, up_grad, down_near, down_other = after(point, whole)
    feed_wparts = feed_wgrads(shards, gate_grad, up_grad, hidden, feed_low, span_grad)
    point = join(point, sum_own, feed_wparts, arrived_one, arrived_three)
    middle_grad, attend_grad, head_grad = token_grad(
        rel_heads,
        [sum_own, *after(point, [arrived_one, arrived_two, arrived_three])],
        middle,
        scale_two,
        gain_two,
        output_grad,
        output_here,
    )
    point = join(point, head_grad)

    out_grad_blocks = lax.all_to_all(
        after(point, head_grad), ("shard", "seq"), split_axis=0, concat_axis=0, tiled=True
    )
    feed_wsum = lax.psum_scatter(
        after(point, feed_wparts).reshape(-1, width), "shard", scatter_dimension=0, tiled=True
    ).reshape(3, -1, width)
    own_agrad = after(point, attend_grad)
    agrad_one = from_chip(own_agrad, 1)
    down_all = core_sum(after(point, down_near), down_other).astype(BF16)
    down_sums = [down_all[order.index(step)] for step in range(steps)]
    pair = jnp.concatenate([own_agrad, down_sums[2]])
    point = join(point, out_grad_blocks, agrad_one, pair, down_sums[3])
    both = from_chip(after(point, pair), -1)
    down_three = from_chip(after(point, down_sums[3]), 1)
    back = attend_back(
        head_qkv, lse, head_out, after(point, out_grad_blocks), cos_all, sin_all, tok, bounds
    )
    point = join(point, back, both, down_three)
    agrad_three, down_two = both[:tok], both[tok:]
    span_back = lax.all_to_all(
        after(point, back), "shard", split_axis=0, concat_axis=0, tiled=True
    ).reshape(heads_here * 3 * HEAD_DIM, span)
    agrad_two = from_chip(after(point, agrad_one), 1)
    down_one = from_chip(
        (down_sums[1].astype(F32) + after(point, down_two).astype(F32)).astype(BF16), -1
    )
    agrad_slots = both_cores([after(point, own_agrad), agrad_one, agrad_two, agrad_three])
    out_part = output_wgrad_parts(span_blocks, jnp.stack(head_slots), agrad_slots)
    out_parts = [out_part[k] for k in range(4)]
    out_first = scatter_shard_first(out_parts)
    point = join(point, span_back, down_one, out_first)

    span_back = after(point, span_back)
    cols_part = cols_parts_of(shard_at, span_back, unit_low, shards)
    point = join(point, cols_part)
    cols_parts = [after(point, cols_part)[k] for k in range(4)]
    cols_first = scatter_shard_first(cols_parts)
    unit_near, unit_other = unit_back(span_blocks, after(point, span_back), columns, tok)
    unit_swapped = swap_cores(unit_other)
    point = join(point, unit_near, unit_swapped)
    unit_sums = unit_near + after(point, unit_swapped).astype(F32)
    unit_two = from_chip(unit_sums[2].astype(BF16), -1)
    unit_three = from_chip(unit_sums[3].astype(BF16), 1)
    out_last = scatter_shard_last(out_parts, after(point, out_first))
    layer_output = (
        middle
        + down_sums[0].astype(F32)
        + after(point, down_one).astype(F32)
        + down_three.astype(F32)
    ).astype(BF16)
    gain_rows_back = out_grad_blocks[:, HEAD_DIM].astype(F32)
    gain_two_out = jnp.sum(
        gain_rows_back[:, :own_rows] + gain_rows_back[:, own_rows : 2 * own_rows], axis=0
    )
    point, layer_output, gain_two_out = lax.optimization_barrier(
        (join(point, unit_two, unit_three, cols_first, out_last), layer_output, gain_two_out)
    )
    unit_one = from_chip((unit_sums[1] + after(point, unit_two).astype(F32)).astype(BF16), -1)
    cols_last = scatter_shard_last(cols_parts, after(point, cols_first))
    point = join(point, unit_one, cols_last)
    cols_near, cols_other = spread_columns(
        place, cols_parts[0], *after(point, cols_last), steps
    )
    cols_blocks = pair_columns(cols_near, swap_cores(cols_other))
    point = join(point, cols_blocks)
    cols_same = list(after(point, cols_blocks))
    cols_same = cols_same[:1] + [from_chip(cols_same[step], -step) for step in range(1, steps)]
    out_one, out_two = after(point, out_last)
    output_wgrad = out_parts[0].astype(F32) + out_one.astype(F32) + out_two.astype(F32)
    unit_grad = unit_sums[0] + after(point, unit_one).astype(F32) + unit_three.astype(F32)
    inputs = layer_input.astype(F32)
    scale_one = lax.rsqrt(jnp.mean(inputs * inputs, axis=-1, keepdims=True) + NORM_EPS)
    unit_rows = inputs * scale_one
    input_grad = (
        middle_grad
        + scale_one * (unit_grad - unit_rows * jnp.mean(unit_grad * unit_rows, axis=-1, keepdims=True))
    ).astype(BF16)
    gate_wgrad, up_wgrad, down_wgrad = [
        after(point, feed_wsum)[m].astype(F32) for m in range(3)
    ]
    point, output_wgrad, input_grad, gate_wgrad, up_wgrad, down_wgrad, cols_same = (
        lax.optimization_barrier(
            (
                *(point, output_wgrad, input_grad, gate_wgrad, up_wgrad, down_wgrad),
                cols_same,
            )
        )
    )
    query_wgrad, key_wgrad, value_wgrad, gain_one_out = unpack_columns(
        place, gain_row, attn_weights, after(point, cols_same)
    )
    return (
        layer_output,
        input_grad,
        gain_one_out.reshape(-1),
        query_wgrad,
        key_wgrad,
        value_wgrad,
        output_wgrad,
        gain_two_out,
        gate_wgrad,
        up_wgrad,
        down_wgrad,
    )


def solution(mesh):
    shards, seqs = mesh.shape["shard"], mesh.shape["seq"]
    body = per_device if shards == 4 and shards * seqs == HEADS else per_device_any
    return jax.shard_map(
        body,
        mesh=mesh,
        in_specs=(
            P(("shard", "seq"), None),
            P(),
            P(("shard", "seq")),
            P(("shard", "seq"), None),
            P(("shard", "seq"), None),
            P(("shard", "seq"), None),
            P(("shard", "seq"), None),
            P(("shard", "seq")),
            P(("shard", "seq"), None),
            P(("shard", "seq"), None),
            P(("shard", "seq"), None),
            P(("shard", "seq"), None),
        ),
        out_specs=(
            P(("shard", "seq"), None),
            P(("shard", "seq"), None),
            P(("shard", "seq")),
            P(("shard", "seq"), None),
            P(("shard", "seq"), None),
            P(("shard", "seq"), None),
            P(("shard", "seq"), None),
            P(("shard", "seq")),
            P(("shard", "seq"), None),
            P(("shard", "seq"), None),
            P(("shard", "seq"), None),
        ),
        check_vma=False,
    )
```

```python
import functools
import math

import jax
import jax.numpy as jnp
from jax import lax
from jax.experimental import pallas as pl
from jax.experimental.pallas import tpu as pltpu
from jax.sharding import PartitionSpec as P

HEAD_DIM = 64


NORM_EPS = 1e-05
ROPE_BASE = 130000.0


def rope_tables(positions, width):
    half_width = width // 2
    exponent = -2.0 * jnp.arange(half_width, dtype=jnp.float32) / width
    inverse = jnp.power(jnp.float32(ROPE_BASE), exponent)
    angles = positions.astype(jnp.float32)[:, None] * inverse[None, :]
    return (jnp.cos(angles), jnp.sin(angles))


def rotate(values, cos_table, sin_table):
    half_width = values.shape[-1] // 2
    front = values[..., :half_width]
    back_half = values[..., half_width:]
    cos_wide = cos_table[:, None, :]
    sin_wide = sin_table[:, None, :]
    return jnp.concatenate(
        [front * cos_wide - back_half * sin_wide, back_half * cos_wide + front * sin_wide], axis=-1
    )


def unrotate(values, cos_table, sin_table):
    half_width = values.shape[-1] // 2
    front = values[..., :half_width]
    back_half = values[..., half_width:]
    cos_wide = cos_table[:, None, :]
    sin_wide = sin_table[:, None, :]
    return jnp.concatenate(
        [front * cos_wide + back_half * sin_wide, back_half * cos_wide - front * sin_wide], axis=-1
    )


def doc_numbers(doc_lengths, positions):
    doc_ends = jnp.cumsum(doc_lengths)
    return jnp.sum((doc_ends[:, None] <= positions[None, :]).astype(jnp.int32), axis=0)


def normalize(values, gain_vec):
    scale_row = lax.rsqrt(jnp.mean(values * values, axis=-1, keepdims=True) + NORM_EPS)
    return (values * scale_row * gain_vec, scale_row)


def norm_back(grad_in, values, scale_row, gain_vec):
    unit_rows = values * scale_row
    gain_grad = jnp.sum(grad_in * unit_rows, axis=0)
    unit_grad = grad_in * gain_vec
    value_grad = scale_row * (
        unit_grad - unit_rows * jnp.mean(unit_grad * unit_rows, axis=-1, keepdims=True)
    )
    return (value_grad, gain_grad)


def times_trans(lhs_mat, rhs_mat):
    return lax.dot_general(
        lhs_mat, rhs_mat, (((1,), (1,)), ((), ())), preferred_element_type=jnp.float32
    )


def trans_times(lhs_mat, rhs_mat):
    return lax.dot_general(
        lhs_mat, rhs_mat, (((0,), (0,)), ((), ())), preferred_element_type=jnp.float32
    )


def per_device_any(
    layer_input,
    doc_lengths,
    norm_gain,
    query_weight,
    key_weight,
    value_weight,
    output_weight,
    feed_gain,
    gate_weight,
    up_weight,
    down_weight,
    output_grad,
):
    tok_rows = layer_input.shape[0]
    width = layer_input.shape[1]
    seq_count = lax.axis_size("seq")
    shard_count = lax.axis_size("shard")
    span_len = tok_rows * seq_count
    stream_len = span_len * shard_count
    span_start = lax.axis_index("shard") * span_len
    own_positions = (
        span_start + lax.axis_index("seq") * tok_rows + jnp.arange(tok_rows, dtype=jnp.int32)
    )
    span_positions = span_start + jnp.arange(span_len, dtype=jnp.int32)
    all_positions = jnp.arange(stream_len, dtype=jnp.int32)
    key_docs = doc_numbers(doc_lengths, all_positions)
    query_docs = lax.dynamic_slice_in_dim(key_docs, span_start, span_len)
    score_scale = HEAD_DIM ** (-0.5)
    gathered = (
        lax.all_gather(query_weight, ("shard", "seq"), axis=0, tiled=True),
        lax.all_gather(key_weight, ("shard", "seq"), axis=0, tiled=True),
        lax.all_gather(value_weight, ("shard", "seq"), axis=0, tiled=True),
        lax.all_gather(output_weight, ("shard", "seq"), axis=0, tiled=True),
        lax.all_gather(norm_gain, ("shard", "seq"), axis=0, tiled=True),
        lax.all_gather(feed_gain, ("shard", "seq"), axis=0, tiled=True),
    )
    query_full, key_full, value_full, output_full = (
        gathered[0],
        gathered[1],
        gathered[2],
        gathered[3],
    )
    gain_one = gathered[4].astype(jnp.float32)
    gain_two = gathered[5].astype(jnp.float32)
    inputs = layer_input.astype(jnp.float32)
    normed, scale_one = normalize(inputs, gain_one)
    normed_low = normed.astype(jnp.bfloat16)
    own_cos, own_sin = rope_tables(own_positions, HEAD_DIM)
    query_proj = jnp.dot(normed_low, query_full, preferred_element_type=jnp.float32)
    key_proj = jnp.dot(normed_low, key_full, preferred_element_type=jnp.float32)
    value_proj = jnp.dot(normed_low, value_full, preferred_element_type=jnp.float32)
    query_rot = rotate(query_proj.reshape(tok_rows, -1, HEAD_DIM), own_cos, own_sin).reshape(
        tok_rows, width
    )
    key_rot = rotate(key_proj.reshape(tok_rows, -1, HEAD_DIM), own_cos, own_sin).reshape(
        tok_rows, width
    )
    stacked = jnp.stack(
        [
            query_rot.astype(jnp.bfloat16),
            key_rot.astype(jnp.bfloat16),
            value_proj.astype(jnp.bfloat16),
        ]
    )
    head_triple = lax.all_to_all(stacked, "seq", split_axis=2, concat_axis=1, tiled=True)
    head_width = head_triple.shape[2]
    heads_dev = head_width // HEAD_DIM
    head_query = head_triple[0].reshape(span_len, heads_dev, HEAD_DIM)
    key_value = lax.all_gather(head_triple[1:], "shard", axis=1, tiled=True)
    key_block = math.gcd(stream_len, max(512, stream_len // 16))
    block_count = stream_len // key_block
    key_blocks = key_value[0].reshape(block_count, key_block, heads_dev, HEAD_DIM)
    value_blocks = key_value[1].reshape(block_count, key_block, heads_dev, HEAD_DIM)
    pos_blocks = all_positions.reshape(block_count, key_block)
    doc_blocks = key_docs.reshape(block_count, key_block)

    def block_scores(key_blk, key_pos, key_doc):
        scores = (
            jnp.einsum("qhd,khd->hqk", head_query, key_blk, preferred_element_type=jnp.float32)
            * score_scale
        )
        allowed = (key_pos[None, :] <= span_positions[:, None]) & (
            key_doc[None, :] == query_docs[:, None]
        )
        return jnp.where(allowed[None], scores, -jnp.inf)

    def total_step(state_pair, pieces):
        run_max, run_sum = state_pair
        scores = block_scores(pieces[0], pieces[1], pieces[2])
        new_max = jnp.maximum(run_max, jnp.max(scores, axis=-1))
        new_sum = run_sum * jnp.exp(run_max - new_max) + jnp.sum(
            jnp.exp(scores - new_max[..., None]), axis=-1
        )
        return ((new_max, new_sum), None)

    start_max = jnp.full((heads_dev, span_len), -1e30, jnp.float32)
    start_sum = jnp.zeros((heads_dev, span_len), jnp.float32)
    totals, unused = lax.scan(
        total_step, (start_max, start_sum), (key_blocks, pos_blocks, doc_blocks)
    )
    log_total = totals[0] + jnp.log(totals[1])

    def output_step(accum, pieces):
        scores = block_scores(pieces[0], pieces[2], pieces[3])
        probs = jnp.exp(scores - log_total[..., None]).astype(jnp.bfloat16)
        return (
            accum
            + jnp.einsum("hqk,khd->qhd", probs, pieces[1], preferred_element_type=jnp.float32),
            None,
        )

    start_acc = jnp.zeros((span_len, heads_dev, HEAD_DIM), jnp.float32)
    head_out32, unused = lax.scan(
        output_step, start_acc, (key_blocks, value_blocks, pos_blocks, doc_blocks)
    )
    head_out = head_out32.reshape(span_len, head_width).astype(jnp.bfloat16)
    token_out = lax.all_to_all(head_out, "seq", split_axis=0, concat_axis=1, tiled=True)
    middle = inputs + jnp.dot(token_out, output_full, preferred_element_type=jnp.float32)
    normed_two, scale_two = normalize(middle, gain_two)
    feed_low = normed_two.astype(jnp.bfloat16)
    feed_mats = (
        lax.all_gather(gate_weight, ("shard", "seq"), axis=0, tiled=True),
        lax.all_gather(up_weight, ("shard", "seq"), axis=0, tiled=True),
        lax.all_gather(down_weight, ("shard", "seq"), axis=0, tiled=True),
    )
    gate_full, up_full, down_full = (feed_mats[0], feed_mats[1], feed_mats[2])
    gate_val = times_trans(feed_low, gate_full)
    up_val = times_trans(feed_low, up_full)
    hidden = (jax.nn.silu(gate_val) * up_val).astype(jnp.bfloat16)
    down_val = jnp.dot(hidden, down_full, preferred_element_type=jnp.float32)
    layer_output = (middle + down_val).astype(jnp.bfloat16)
    hidden_grad = times_trans(output_grad, down_full)
    sigmoid_val = jax.nn.sigmoid(gate_val)
    gate_grad = (
        hidden_grad * up_val * (sigmoid_val * (1.0 + gate_val * (1.0 - sigmoid_val)))
    ).astype(jnp.bfloat16)
    up_grad = (hidden_grad * jax.nn.silu(gate_val)).astype(jnp.bfloat16)
    feed_grad = jnp.dot(gate_grad, gate_full, preferred_element_type=jnp.float32) + jnp.dot(
        up_grad, up_full, preferred_element_type=jnp.float32
    )
    feed_sums = lax.psum_scatter(
        jnp.stack(
            [
                trans_times(gate_grad, feed_low),
                trans_times(up_grad, feed_low),
                trans_times(hidden, output_grad),
            ],
            axis=1,
        ),
        ("shard", "seq"),
        scatter_dimension=0,
        tiled=True,
    )
    middle_norm_grad, gain_two_grad = norm_back(feed_grad, middle, scale_two, gain_two)
    middle_grad = output_grad.astype(jnp.float32) + middle_norm_grad
    attend_grad = middle_grad.astype(jnp.bfloat16)
    output_term = trans_times(token_out, attend_grad)
    token_out_grad = times_trans(attend_grad, output_full).astype(jnp.bfloat16)
    head_out_grad = lax.all_to_all(
        token_out_grad, "seq", split_axis=1, concat_axis=0, tiled=True
    ).reshape(span_len, heads_dev, HEAD_DIM)
    row_dots = jnp.transpose(jnp.sum(head_out_grad.astype(jnp.float32) * head_out32, axis=-1))

    def grad_step(query_acc, pieces):
        key_blk, value_blk, key_pos, key_doc = pieces
        scores = block_scores(key_blk, key_pos, key_doc)
        probs = jnp.exp(scores - log_total[..., None])
        prob_grad = jnp.einsum(
            "qhd,khd->hqk", head_out_grad, value_blk, preferred_element_type=jnp.float32
        )
        score_grad = (probs * (prob_grad - row_dots[..., None])).astype(jnp.bfloat16)
        query_next = query_acc + score_scale * jnp.einsum(
            "hqk,khd->qhd", score_grad, key_blk, preferred_element_type=jnp.float32
        )
        key_part = score_scale * jnp.einsum(
            "hqk,qhd->khd", score_grad, head_query, preferred_element_type=jnp.float32
        )
        value_part = jnp.einsum(
            "hqk,qhd->khd",
            probs.astype(jnp.bfloat16),
            head_out_grad,
            preferred_element_type=jnp.float32,
        )
        return (query_next, (key_part, value_part))

    query_grad, block_grads = lax.scan(
        grad_step, start_acc, (key_blocks, value_blocks, pos_blocks, doc_blocks)
    )
    pair_grads = jnp.stack(
        [
            block_grads[0].reshape(stream_len, head_width),
            block_grads[1].reshape(stream_len, head_width),
        ]
    )
    own_pair = lax.psum_scatter(
        pair_grads.astype(jnp.bfloat16), "shard", scatter_dimension=1, tiled=True
    ).astype(jnp.float32)
    span_cos, span_sin = rope_tables(span_positions, HEAD_DIM)
    query_back = unrotate(query_grad, span_cos, span_sin).reshape(span_len, head_width)
    key_back = unrotate(
        own_pair[0].reshape(span_len, heads_dev, HEAD_DIM), span_cos, span_sin
    ).reshape(span_len, head_width)
    back_stack = jnp.stack([query_back, key_back, own_pair[1]]).astype(jnp.bfloat16)
    token_grads = lax.all_to_all(back_stack, "seq", split_axis=1, concat_axis=2, tiled=True)
    norm_grad = (
        times_trans(token_grads[0], query_full)
        + times_trans(token_grads[1], key_full)
        + times_trans(token_grads[2], value_full)
    )
    input_norm_grad, gain_one_grad = norm_back(norm_grad, inputs, scale_one, gain_one)
    input_grad = (middle_grad + input_norm_grad).astype(jnp.bfloat16)
    query_term = trans_times(normed_low, token_grads[0])
    key_term = trans_times(normed_low, token_grads[1])
    value_term = trans_times(normed_low, token_grads[2])
    summed = (
        lax.psum_scatter(query_term, ("shard", "seq"), scatter_dimension=0, tiled=True),
        lax.psum_scatter(key_term, ("shard", "seq"), scatter_dimension=0, tiled=True),
        lax.psum_scatter(value_term, ("shard", "seq"), scatter_dimension=0, tiled=True),
        lax.psum_scatter(output_term, ("shard", "seq"), scatter_dimension=0, tiled=True),
        lax.psum_scatter(gain_one_grad, ("shard", "seq"), scatter_dimension=0, tiled=True),
        lax.psum_scatter(gain_two_grad, ("shard", "seq"), scatter_dimension=0, tiled=True),
    )
    query_wgrad, key_wgrad, value_wgrad = (summed[0], summed[1], summed[2])
    output_wgrad, gain_one_out, gain_two_out = (summed[3], summed[4], summed[5])
    return (
        layer_output,
        input_grad,
        gain_one_out,
        query_wgrad,
        key_wgrad,
        value_wgrad,
        output_wgrad,
        gain_two_out,
        feed_sums[:, 0],
        feed_sums[:, 1],
        feed_sums[:, 2],
    )


HEADS = 32
EXTRA = 16
BF16 = jnp.bfloat16
F32 = jnp.float32


SHORT = pl.CostEstimate(flops=0, bytes_accessed=0, transcendentals=0)


def in_hbm(arrays):
    return [pltpu.with_memory_space_constraint(array, pltpu.HBM) for array in arrays]


def dot_nn(lhs_mat, rhs_mat):
    return lax.dot_general(
        lhs_mat, rhs_mat, (((1,), (0,)), ((), ())), preferred_element_type=jnp.float32
    )


def allowed_pairs(i, j, keys, cols, span, start_ref, same):
    shape = (keys.stop - keys.start, cols.stop - cols.start)
    k_pos = j * span + keys.start + lax.broadcasted_iota(jnp.int32, shape, 0)
    begun = k_pos >= start_ref[i][:, cols]
    if not same:
        return begun
    q_pos = i * span + cols.start + lax.broadcasted_iota(jnp.int32, shape, 1)
    return (k_pos <= q_pos) & begun


def own_span_parts(span):
    half = span // 2
    return (slice(0, half), slice(0, half)), (slice(0, span), slice(half, span))


def fwd_kernel(tok, shard_ref, lo_ref, full_ref, start_ref, qkv_ref, gain_ref, out_ref, low_ref, blocks_ref,
               lse_ref, k_nat, m_s, l_s, acc_s):
    i = pl.program_id(0)
    spans, rows, span = qkv_ref.shape
    slots = span // tok
    scale2 = HEAD_DIM ** -0.5 * math.log2(math.e)

    @pl.when(i == 0)
    def _():
        for s in range(spans):
            k_nat[pl.ds(s * span, span), :] = qkv_ref[s, HEAD_DIM : 2 * HEAD_DIM, :].T

    m_s[...] = jnp.full_like(m_s, -1e30)
    l_s[...] = jnp.zeros_like(l_s)
    acc_s[...] = jnp.zeros_like(acc_s)

    def step(j, masked, same=False, keys=slice(0, span), cols=slice(0, span)):
        k_rows = pl.ds(pl.multiple_of(j * span + keys.start, 128), keys.stop - keys.start)
        s_t = dot_nn(k_nat[k_rows, :], qkv_ref[i, :HEAD_DIM, cols]) * scale2
        if masked:
            s_t = jnp.where(allowed_pairs(i, j, keys, cols, span, start_ref, same), s_t, -jnp.inf)
        m_old = m_s[:, cols]
        m_new = jnp.maximum(m_old, jnp.max(s_t, axis=0, keepdims=True))
        alpha = jnp.exp2(m_old - m_new)
        p_t = jnp.exp2(s_t - m_new)
        l_s[:, cols] = l_s[:, cols] * alpha + jnp.sum(p_t, axis=0, keepdims=True)
        m_s[:, cols] = m_new
        acc_s[:, cols] = acc_s[:, cols] * alpha + dot_nn(
            qkv_ref[j, 2 * HEAD_DIM :, keys], p_t.astype(jnp.bfloat16)
        )

    def loop_body(masked):
        def body(j, carry):
            step(j, masked)
            return carry

        return body

    lax.fori_loop(lo_ref[i], full_ref[i], loop_body(True), 0)
    lax.fori_loop(full_ref[i], i, loop_body(False), 0)
    for keys, cols in own_span_parts(span):
        step(i, True, True, keys, cols)
    out = acc_s[...] / l_s[...]
    out_ref[0] = out
    low = out.astype(jnp.bfloat16)
    low_ref[i ^ shard_ref[0]] = low
    lse_ref[0] = m_s[...] + jnp.log2(l_s[...])
    for slot in range(slots):
        blocks_ref[slot, :HEAD_DIM] = low[:, slot * tok : (slot + 1) * tok]
        blocks_ref[slot, HEAD_DIM:] = gain_ref[...]


def bwd_kernel(tok, hi_ref, full_ref, start_ref, qkv_ref, lse_ref, out_hbm, dob_ref,
               cos_ref, sin_ref, back_ref, dq_s, dk_s, dv_s, do_s, di_s, out_ref, sem):
    j = pl.program_id(0)
    spans, rows, span = qkv_ref.shape
    slots = span // tok
    scale = HEAD_DIM ** -0.5
    scale2 = scale * math.log2(math.e)

    @pl.when(j == 0)
    def _():
        copy = pltpu.make_async_copy(out_hbm, out_ref, sem)
        copy.start()
        dq_s[...] = jnp.zeros_like(dq_s)
        for s in range(spans):
            for slot in range(slots):
                do_s[s, :, slot * tok : (slot + 1) * tok] = dob_ref[s * slots + slot, :HEAD_DIM]
        copy.wait()
        for s in range(spans):
            di_s[s] = jnp.sum(do_s[s].astype(jnp.float32) * out_ref[s], axis=0, keepdims=True)

    k_nat = qkv_ref[j, HEAD_DIM : 2 * HEAD_DIM, :].T
    v_nat = qkv_ref[j, 2 * HEAD_DIM :, :].T
    dk_s[...] = jnp.zeros_like(dk_s)
    dv_s[...] = jnp.zeros_like(dv_s)

    def step(i, masked, same=False, keys=slice(0, span), cols=slice(0, span)):
        q_t = qkv_ref[i, :HEAD_DIM, cols]
        p_t = jnp.exp2(dot_nn(k_nat[keys], q_t) * scale2 - lse_ref[i][:, cols])
        if masked:
            p_t = jnp.where(allowed_pairs(i, j, keys, cols, span, start_ref, same), p_t, 0.0)
        do_t = do_s[i, :, cols]
        dv_s[:, keys] += times_trans(do_t, p_t.astype(jnp.bfloat16))
        ds_t = (p_t * (dot_nn(v_nat[keys], do_t) - di_s[i][:, cols])).astype(jnp.bfloat16)
        dk_s[:, keys] += times_trans(q_t, ds_t)
        dq_s[i, :, cols] += dot_nn(qkv_ref[j, HEAD_DIM : 2 * HEAD_DIM, keys], ds_t)

    for keys, cols in own_span_parts(span):
        step(j, True, True, keys, cols)

    def body(i, carry):
        whole = full_ref[i] <= j

        @pl.when(whole)
        def _():
            step(i, False)

        @pl.when(jnp.logical_not(whole))
        def _():
            step(i, True)

        return carry

    lax.fori_loop(j + 1, hi_ref[j], body, 0)

    def turned_back(grad):
        front, back_half = grad[: HEAD_DIM // 2], grad[HEAD_DIM // 2 :]
        cos_t, sin_t = cos_ref[0], sin_ref[0]
        return jnp.concatenate(
            [front * cos_t + back_half * sin_t, back_half * cos_t - front * sin_t], axis=0
        ).astype(jnp.bfloat16)

    back_ref[0, :HEAD_DIM] = turned_back(dq_s[j] * scale)
    back_ref[0, HEAD_DIM : 2 * HEAD_DIM] = turned_back(dk_s[...] * scale)
    back_ref[0, 2 * HEAD_DIM :] = dv_s[...].astype(jnp.bfloat16)


def doc_bounds(doc_lengths, positions):
    spans, span = positions.shape
    ends = jnp.cumsum(doc_lengths)
    over = ends[:, None, None] <= positions[None]
    start = jnp.max(jnp.where(over, ends[:, None, None], 0), axis=0).astype(jnp.int32)
    stop = jnp.min(jnp.where(over, spans * span, ends[:, None, None]), axis=0).astype(jnp.int32)
    first = jnp.min(start, axis=1) // span
    whole = jnp.minimum(
        (jnp.max(start, axis=1) + span - 1) // span, jnp.arange(spans, dtype=jnp.int32)
    )
    last = (jnp.max(stop, axis=1) + span - 1) // span
    return start[:, None, :], first, whole, last


def attend(qkv, gain_rows, tok, shard, bounds):
    spans, rows, span = qkv.shape
    stream = spans * span
    slots = span // tok
    start, first, whole, last = bounds
    smem = pl.BlockSpec(memory_space=pltpu.SMEM)
    vmem = pl.BlockSpec(memory_space=pltpu.VMEM)

    def one(*block):
        return pl.BlockSpec((1,) + block, lambda i: (i, 0, 0))

    return pl.pallas_call(
        functools.partial(fwd_kernel, tok),
        grid=(spans,),
        in_specs=[smem, smem, smem, vmem, vmem, vmem],
        out_specs=[
            one(HEAD_DIM, span),
            pl.BlockSpec((spans, HEAD_DIM, span), lambda i: (0, 0, 0)),
            pl.BlockSpec((slots, HEAD_DIM + EXTRA, tok), lambda i: (i, 0, 0)),
            one(1, span),
        ],
        out_shape=[
            pltpu.HBM((spans, HEAD_DIM, span), jnp.float32),
            pltpu.HBM((spans, HEAD_DIM, span), jnp.bfloat16),
            pltpu.HBM((stream // tok, HEAD_DIM + EXTRA, tok), jnp.bfloat16),
            jax.ShapeDtypeStruct((spans, 1, span), jnp.float32),
        ],
        scratch_shapes=[
            pltpu.VMEM((stream, HEAD_DIM), jnp.bfloat16),
            pltpu.VMEM((1, span), jnp.float32),
            pltpu.VMEM((1, span), jnp.float32),
            pltpu.VMEM((HEAD_DIM, span), jnp.float32),
        ],
        compiler_params=pltpu.CompilerParams(vmem_limit_bytes=24 * 2**20),
        cost_estimate=pl.CostEstimate(
            flops=stream * stream * 256 * 5, bytes_accessed=stream * 1024, transcendentals=0
        ),
        name="attend",
    )(shard, first, whole, start, qkv, gain_rows)


def attend_back(qkv, lse, out, out_grad, cos_t, sin_t, tok, bounds):
    spans, rows, span = qkv.shape
    stream = spans * span
    start, first, whole, last = bounds
    smem = pl.BlockSpec(memory_space=pltpu.SMEM)
    vmem = pl.BlockSpec(memory_space=pltpu.VMEM)

    def one(*block):
        return pl.BlockSpec((1,) + block, lambda j: (j, 0, 0))

    return pl.pallas_call(
        functools.partial(bwd_kernel, tok),
        grid=(spans,),
        in_specs=[smem, smem, vmem, vmem, vmem, pl.BlockSpec(memory_space=pl.ANY), vmem]
        + [one(HEAD_DIM // 2, span)] * 2,
        out_specs=one(rows, span),
        out_shape=pltpu.HBM(qkv.shape, jnp.bfloat16),
        scratch_shapes=[
            pltpu.VMEM((spans, HEAD_DIM, span), jnp.float32),
            pltpu.VMEM((HEAD_DIM, span), jnp.float32),
            pltpu.VMEM((HEAD_DIM, span), jnp.float32),
            pltpu.VMEM((spans, HEAD_DIM, span), jnp.bfloat16),
            pltpu.VMEM((spans, 1, span), jnp.float32),
            pltpu.VMEM((spans, HEAD_DIM, span), jnp.float32),
            pltpu.SemaphoreType.DMA,
        ],
        compiler_params=pltpu.CompilerParams(vmem_limit_bytes=32 * 2**20),
        cost_estimate=pl.CostEstimate(
            flops=stream * stream * 256 * 7, bytes_accessed=stream * 1024, transcendentals=0
        ),
        name="attend_back",
    )(last, whole, start, qkv, lse, *in_hbm([out]), out_grad, *in_hbm([cos_t, sin_t]))


def as_column(row):
    shape = (row.shape[1], row.shape[1])
    same = lax.broadcasted_iota(jnp.int32, shape, 0) == lax.broadcasted_iota(jnp.int32, shape, 1)
    return jnp.sum(jnp.where(same, row.astype(jnp.float32), 0.0), axis=1, keepdims=True)


def pack_kernel(heads, place_ref, gain_ref, query_ref, key_ref, value_ref, out_ref):
    steps = out_ref.shape[1]
    seqs = 2 * steps
    z, core = place_ref[0] // 2, place_ref[0] % 2
    gain_col = as_column(gain_ref[...])
    for m, ref in enumerate((query_ref, key_ref, value_ref)):
        rows = (ref[...].astype(jnp.float32) * gain_col).astype(jnp.bfloat16)
        for head in range(heads):
            at = (head // seqs * 3 + m) * HEAD_DIM
            other = (core + head) % 2
            step = (head % seqs // 2 + steps - z) % steps
            out_ref[other, step, :, at : at + HEAD_DIM] = rows[
                :, head * HEAD_DIM : (head + 1) * HEAD_DIM
            ]


def pack_columns(place, gain_row, weights, seqs):
    rows, width = weights[0].shape
    heads = width // HEAD_DIM
    vmem = pl.BlockSpec(memory_space=pltpu.VMEM)
    return pl.pallas_call(
        functools.partial(pack_kernel, heads),
        in_specs=[pl.BlockSpec(memory_space=pltpu.SMEM)] + [vmem] * 4,
        out_specs=vmem,
        out_shape=jax.ShapeDtypeStruct(
            (2, seqs // 2, rows, heads // seqs * 3 * HEAD_DIM), jnp.bfloat16
        ),
        cost_estimate=SHORT,
        name="pack_columns",
    )(place, gain_row, *weights)


def order_kernel(index_ref, *refs):
    out_ref = refs[-1]
    rows = out_ref.shape[1]
    count = 0
    for ref in refs[:-1]:
        for i in range(ref.shape[0] // rows):
            out_ref[index_ref[count]] = ref[i * rows : (i + 1) * rows]
            count += 1


def order_blocks(pieces, index, rows):
    vmem = pl.BlockSpec(memory_space=pltpu.VMEM)
    blocks = sum(piece.shape[0] for piece in pieces) // rows
    width = pieces[0].shape[1]
    return pl.pallas_call(
        order_kernel,
        in_specs=[pl.BlockSpec(memory_space=pltpu.SMEM)] + [vmem] * len(pieces),
        out_specs=vmem,
        out_shape=jax.ShapeDtypeStruct((blocks, rows, width), pieces[0].dtype),
        compiler_params=pltpu.CompilerParams(vmem_limit_bytes=12 * 2**20),
        cost_estimate=SHORT,
        name="order_blocks",
    )(index, *pieces).reshape(blocks * rows, width)


def cols_kernel(shard_ref, back_ref, unit_hbm, out_ref, unit_s, sem):
    slots, _, width = out_ref.shape
    copies = [
        pltpu.make_async_copy(
            unit_hbm.at[:, pl.ds(pl.multiple_of((shard_ref[0] ^ k) * width, width), width)],
            unit_s.at[k],
            sem.at[k],
        )
        for k in range(slots)
    ]
    for copy in copies:
        copy.start()
    for k in range(slots):
        copies[k].wait()
        out_ref[k] = dot_nn(back_ref[...], unit_s[k]).astype(jnp.bfloat16)


def cols_parts_of(shard, back, unit_low, slots):
    rows = back.shape[0]
    tokens = unit_low.shape[0]
    width = unit_low.shape[1] // slots
    vmem = pl.BlockSpec(memory_space=pltpu.VMEM)
    return pl.pallas_call(
        cols_kernel,
        in_specs=[
            pl.BlockSpec(memory_space=pltpu.SMEM), vmem, pl.BlockSpec(memory_space=pl.ANY)
        ],
        out_specs=vmem,
        out_shape=jax.ShapeDtypeStruct((slots, rows, width), jnp.bfloat16),
        scratch_shapes=[
            pltpu.VMEM((slots, tokens, width), unit_low.dtype),
            pltpu.SemaphoreType.DMA((slots,)),
        ],
        compiler_params=pltpu.CompilerParams(vmem_limit_bytes=24 * 2**20),
        cost_estimate=SHORT,
        name="cols_parts",
    )(shard, back, *in_hbm([unit_low]))


def unit_back_kernel(index_ref, back_ref, columns_ref, near_ref, other_ref):
    steps, tok, _ = near_ref.shape
    for step in range(steps):
        lanes = [
            back_ref[:, pl.ds(pl.multiple_of(index_ref[2 * step + c] * tok, tok), tok)]
            for c in range(2)
        ]
        part = times_trans(jnp.concatenate(lanes, axis=1).T, columns_ref[...])
        near_ref[step] = part[:tok]
        other_ref[step] = part[tok:].astype(jnp.bfloat16)


def unit_back(index, back, columns, tok):
    steps = back.shape[1] // (2 * tok)
    width = columns.shape[0]
    vmem = pl.BlockSpec(memory_space=pltpu.VMEM)
    return pl.pallas_call(
        unit_back_kernel,
        in_specs=[pl.BlockSpec(memory_space=pltpu.SMEM)] + [vmem] * 2,
        out_specs=[vmem] * 2,
        out_shape=[
            jax.ShapeDtypeStruct((steps, tok, width), jnp.float32),
            jax.ShapeDtypeStruct((steps, tok, width), jnp.bfloat16),
        ],
        compiler_params=pltpu.CompilerParams(vmem_limit_bytes=24 * 2**20),
        cost_estimate=SHORT,
        name="unit_back",
    )(index, back, columns)


def spread_kernel(place_ref, own_ref, one_ref, two_ref, near_ref, other_ref, both_s):
    steps, rows, _ = near_ref.shape
    z, core = place_ref[0] // 2, place_ref[0] % 2
    total = own_ref[...].astype(jnp.float32)
    total += one_ref[...].astype(jnp.float32) + two_ref[...].astype(jnp.float32)
    total = total.T.astype(jnp.bfloat16)
    for q in range(2 * steps):
        both_s[(core + q) % 2, (q // 2 + steps - z) % steps] = total[q * rows : (q + 1) * rows]
    near_ref[...] = both_s[0]
    other_ref[...] = both_s[1]


def spread_columns(place, own, one, two, steps):
    columns, rows = own.shape
    vmem = pl.BlockSpec(memory_space=pltpu.VMEM)
    shape = (steps, rows // (2 * steps), columns)
    return pl.pallas_call(
        spread_kernel,
        in_specs=[pl.BlockSpec(memory_space=pltpu.SMEM)] + [vmem] * 3,
        out_specs=[vmem] * 2,
        out_shape=[jax.ShapeDtypeStruct(shape, jnp.bfloat16)] * 2,
        scratch_shapes=[pltpu.VMEM((2,) + shape, jnp.bfloat16)],
        cost_estimate=SHORT,
        name="spread_columns",
    )(place, own, one, two)


def pair_kernel(spread_ref, other_ref, *out_refs):
    for step, out_ref in enumerate(out_refs):
        out_ref[...] = jnp.concatenate([spread_ref[step], other_ref[step]])


def pair_columns(spread, other):
    steps, rows, columns = other.shape
    vmem = pl.BlockSpec(memory_space=pltpu.VMEM)
    return pl.pallas_call(
        pair_kernel,
        in_specs=[vmem] * 2,
        out_specs=[vmem] * steps,
        out_shape=[jax.ShapeDtypeStruct((2 * rows, columns), other.dtype)] * steps,
        cost_estimate=SHORT,
        name="pair_columns",
    )(spread, other)


def unpack_kernel(heads, place_ref, gain_ref, query_ref, key_ref, value_ref, *refs):
    out_refs, cols_s = refs[-5:-1], refs[-1]
    steps = len(refs) - 5
    rows = query_ref.shape[0]
    seqs = 2 * steps
    z, core = place_ref[0] // 2, place_ref[0] % 2
    for step in range(steps):
        cols_s[0, step] = refs[step][:rows]
        cols_s[1, step] = refs[step][rows:]
    gain_col = as_column(gain_ref[...])
    total = jnp.zeros((rows, 1), jnp.float32)
    for m, ref in enumerate((query_ref, key_ref, value_ref)):
        grads = jnp.concatenate(
            [
                cols_s[
                    (core + head) % 2,
                    (z + steps - head % seqs // 2) % steps,
                    :,
                    (head // seqs * 3 + m) * HEAD_DIM : (head // seqs * 3 + m + 1) * HEAD_DIM,
                ]
                for head in range(heads)
            ],
            axis=1,
        ).astype(jnp.float32)
        total += jnp.sum(grads * ref[...].astype(jnp.float32), axis=1, keepdims=True)
        out_refs[m][...] = grads * gain_col
    out_refs[3][...] = jnp.broadcast_to(total, (rows, 128)).T[:1]


def unpack_columns(place, gain_row, weights, cols):
    rows, width = weights[0].shape
    vmem = pl.BlockSpec(memory_space=pltpu.VMEM)
    return pl.pallas_call(
        functools.partial(unpack_kernel, width // HEAD_DIM),
        in_specs=[pl.BlockSpec(memory_space=pltpu.SMEM)] + [vmem] * (4 + len(cols)),
        out_specs=[vmem] * 4,
        out_shape=[jax.ShapeDtypeStruct((rows, width), jnp.float32)] * 3
        + [jax.ShapeDtypeStruct((1, rows), jnp.float32)],
        scratch_shapes=[pltpu.VMEM((2, len(cols), rows, cols[0].shape[1]), cols[0].dtype)],
        cost_estimate=SHORT,
        name="unpack_columns",
    )(place, gain_row, *weights, *cols)


def unit_kernel(index_ref, *refs):
    out_ref = refs[-1]
    tok = refs[0].shape[0]
    for slot, ref in enumerate(refs[:-1]):
        rows = ref[...].astype(jnp.float32)
        scale = lax.rsqrt(jnp.mean(rows * rows, axis=-1, keepdims=True) + NORM_EPS)
        at = pl.ds(pl.multiple_of(index_ref[slot] * tok, tok), tok)
        out_ref[at, :] = (rows * scale).astype(jnp.bfloat16)


def unit_tokens(index, slots):
    tok, width = slots[0].shape
    vmem = pl.BlockSpec(memory_space=pltpu.VMEM)
    return pl.pallas_call(
        unit_kernel,
        in_specs=[pl.BlockSpec(memory_space=pltpu.SMEM)] + [vmem] * len(slots),
        out_specs=vmem,
        out_shape=jax.ShapeDtypeStruct((len(slots) * tok, width), jnp.bfloat16),
        compiler_params=pltpu.CompilerParams(vmem_limit_bytes=16 * 2**20),
        cost_estimate=SHORT,
        name="unit_tokens",
    )(index, *slots)


def join_kernel(*refs):
    rows = refs[0].shape[0]
    for i, ref in enumerate(refs[:-1]):
        refs[-1][i * rows : (i + 1) * rows] = ref[...]


def join_rows(arrays):
    rows, width = arrays[0].shape
    vmem = pl.BlockSpec(memory_space=pltpu.VMEM)
    return pl.pallas_call(
        join_kernel,
        in_specs=[vmem] * len(arrays),
        out_specs=vmem,
        out_shape=jax.ShapeDtypeStruct((len(arrays) * rows, width), arrays[0].dtype),
        cost_estimate=SHORT,
        name="join_rows",
    )(*arrays)


def load_kernel(layout, *refs):
    pieces, out_ref, sem = refs[:-2], refs[-2], refs[-1]
    copies = [
        pltpu.make_async_copy(ref, out_ref.at[m, pl.ds(row, ref.shape[0])], sem.at[i])
        for i, (ref, (m, row)) in enumerate(zip(pieces, layout, strict=True))
    ]
    for copy in copies:
        copy.start()
    for copy in copies:
        copy.wait()


def load_weights(matrices):
    layout, pieces = [], []
    for m, matrix in enumerate(matrices):
        row = 0
        for piece in matrix:
            layout.append((m, row))
            pieces.append(piece)
            row += piece.shape[0]
    shape = (len(matrices), row, pieces[0].shape[1])
    return pl.pallas_call(
        functools.partial(load_kernel, tuple(layout)),
        in_specs=[pl.BlockSpec(memory_space=pl.ANY)] * len(pieces),
        out_specs=pl.BlockSpec(memory_space=pltpu.VMEM),
        out_shape=pltpu.VMEM(shape, pieces[0].dtype),
        scratch_shapes=[pltpu.SemaphoreType.DMA((len(pieces),))],
        cost_estimate=SHORT,
        compiler_params=pltpu.CompilerParams(vmem_limit_bytes=14 * 2**20),
        name="load_weights",
    )(*in_hbm(pieces))


def feed_kernel(call, aliased, *refs):
    shard_ref, tokens, grads, first_ref, down_ref = refs[0], refs[1:3], refs[3:5], refs[5], refs[6]
    refs = refs[7 + aliased :]
    part_near, part_other = refs[:2]
    all_refs = refs[2:9]
    tok_s, grad_s, hidden_s, gate_s, up_s, hidden_t, gate_t, up_t, down_s, sem = refs[9:]
    tok, width = tokens[0].shape
    shards, block = 4, down_ref.shape[1] // 4
    rows = pl.ds(2 * tok * call, 2 * tok)
    for c in range(2):
        tok_s[c * tok : (c + 1) * tok] = tokens[c][...]
        grad_s[c * tok : (c + 1) * tok] = grads[c][...]
    copies = [
        pltpu.make_async_copy(tok_s, all_refs[0].at[rows], sem.at[0]),
        pltpu.make_async_copy(grad_s, all_refs[1].at[rows], sem.at[1]),
    ]
    for copy in copies:
        copy.start()
    for b in range(shards):
        at = slice(b * block, (b + 1) * block)
        place = pl.ds(pl.multiple_of((shard_ref[0] ^ b) * block, block), block)
        gate_val = times_trans(tok_s[...], first_ref[0, at])
        up_val = times_trans(tok_s[...], first_ref[1, at])
        hidden_grad = times_trans(grad_s[...], down_ref[0, at])
        sigmoid_val = 1.0 / (1.0 + jnp.exp(-gate_val))
        silu_val = gate_val * sigmoid_val
        hidden = (silu_val * up_val).astype(jnp.bfloat16)
        gate_grad = (
            hidden_grad * up_val * (sigmoid_val + silu_val * (1.0 - sigmoid_val))
        ).astype(jnp.bfloat16)
        up_grad = (hidden_grad * silu_val).astype(jnp.bfloat16)
        for value, by_unit, by_token in (
            (hidden, hidden_t, hidden_s), (gate_grad, gate_t, gate_s), (up_grad, up_t, up_s)
        ):
            by_unit[place, :] = value.T
            by_token[:, at] = value
    late = [
        pltpu.make_async_copy(src, dst.at[:, rows], sem.at[2 + i])
        for i, (src, dst) in enumerate(zip((hidden_t, gate_t, up_t), all_refs[2:5], strict=True))
    ]
    for copy in late:
        copy.start()
    for c in range(4):
        at = slice(c * (width // 4), (c + 1) * (width // 4))
        down = dot_nn(hidden_s[...], down_ref[0, :, at]).astype(jnp.bfloat16)
        down_s[0, :, at] = down[:tok]
        down_s[1, :, at] = down[tok:]
    last = [
        pltpu.make_async_copy(down_s.at[c], all_refs[5 + c].at[call], sem.at[5 + c])
        for c in range(2)
    ]
    for copy in last:
        copy.start()
    for c in range(4):
        at = slice(c * (width // 4), (c + 1) * (width // 4))
        part = dot_nn(gate_s[...], first_ref[0, :, at]) + dot_nn(up_s[...], first_ref[1, :, at])
        part_near[:, at] = part[:tok]
        part_other[:, at] = part[tok:].astype(jnp.bfloat16)
    for copy in copies + late + last:
        copy.wait()


def feed_blocks(call, slots, shard, tokens, grads, first_two, down, whole):
    tok, width = tokens[0].shape
    units = down.shape[1]
    anywhere = pl.BlockSpec(memory_space=pl.ANY)
    vmem = pl.BlockSpec(memory_space=pltpu.VMEM)
    low, full = jnp.bfloat16, jnp.float32
    shapes = (
        [(slots * tok, width)] * 2
        + [(units, slots * tok)] * 3
        + [(slots // 2, tok, width)] * 2
    )
    whole = in_hbm(whole or [])
    out = pl.pallas_call(
        functools.partial(feed_kernel, call, len(whole)),
        in_specs=[pl.BlockSpec(memory_space=pltpu.SMEM)] + [vmem] * 6 + [anywhere] * len(whole),
        out_specs=[vmem] * 2 + [anywhere] * 7,
        out_shape=[jax.ShapeDtypeStruct((tok, width), full), jax.ShapeDtypeStruct((tok, width), low)]
        + [pltpu.HBM(shape, low) for shape in shapes],
        input_output_aliases={7 + i: 2 + i for i in range(len(whole))},
        scratch_shapes=[pltpu.VMEM((2 * tok, width), low)] * 2
        + [pltpu.VMEM((2 * tok, units), low)] * 3
        + [pltpu.VMEM((units, 2 * tok), low)] * 3
        + [pltpu.VMEM((2, tok, width), low), pltpu.SemaphoreType.DMA((7,))],
        compiler_params=pltpu.CompilerParams(vmem_limit_bytes=30 * 2**20),
        cost_estimate=SHORT,
        name="feed_blocks",
    )(
        shard,
        *tokens,
        *grads,
        *[pltpu.with_memory_space_constraint(weight, pltpu.VMEM) for weight in (first_two, down)],
        *whole,
    )
    return out[:2], out[2:]


def start_pieces(pieces, weight_s, sem):
    places, row = [], 0
    for i, ref in enumerate(pieces):
        at = pl.ds(row, ref.shape[0])
        copy = pltpu.make_async_copy(ref, weight_s.at[at], sem.at[i])
        copy.start()
        places.append((row, ref.shape[0], copy))
        row += ref.shape[0]
    return places


def project_kernel(index_ref, blocks_ref, input_ref, gain_ref, *refs):
    pieces, (middle_ref, normed_ref, scale_ref, weight_s, sem) = refs[:-5], refs[-5:]
    places = start_pieces(pieces, weight_s, sem)
    heads = blocks_ref.shape[0]
    rows = jnp.concatenate([blocks_ref[index_ref[i], :HEAD_DIM] for i in range(heads)]).T
    total = input_ref[...].astype(jnp.float32)
    for row, size, copy in places:
        copy.wait()
        total += dot_nn(rows[:, row : row + size], weight_s[row : row + size])
    scale = lax.rsqrt(jnp.mean(total * total, axis=-1, keepdims=True) + NORM_EPS)
    middle_ref[...] = total
    normed_ref[...] = (total * scale * gain_ref[...]).astype(jnp.bfloat16)
    scale_ref[...] = jnp.broadcast_to(scale, scale_ref.shape)


def project(index, blocks, inputs, gain, pieces):
    tok, width = inputs.shape
    vmem = pl.BlockSpec(memory_space=pltpu.VMEM)
    return pl.pallas_call(
        project_kernel,
        in_specs=[pl.BlockSpec(memory_space=pltpu.SMEM)]
        + [vmem] * 3
        + [pl.BlockSpec(memory_space=pl.ANY)] * len(pieces),
        out_specs=[vmem] * 3,
        out_shape=[
            jax.ShapeDtypeStruct((tok, width), jnp.float32),
            jax.ShapeDtypeStruct((tok, width), jnp.bfloat16),
            jax.ShapeDtypeStruct((tok, 128), jnp.float32),
        ],
        scratch_shapes=[
            pltpu.VMEM((HEADS * HEAD_DIM, width), jnp.bfloat16),
            pltpu.SemaphoreType.DMA((len(pieces),)),
        ],
        compiler_params=pltpu.CompilerParams(vmem_limit_bytes=18 * 2**20),
        cost_estimate=SHORT,
        name="project",
    )(index, blocks, inputs, gain, *in_hbm(pieces))


def token_grad_kernel(
    index_ref, own_ref, one_ref, two_ref, three_ref, middle_ref, scale_ref, gain_ref, grad_ref, *refs
):
    weight_ref, middle_grad_ref, low_ref, out_ref = refs
    normed_grad = own_ref[...]
    for ref in (one_ref, two_ref, three_ref):
        normed_grad += ref[...].astype(jnp.float32)
    tok = normed_grad.shape[0]
    scale = scale_ref[:, :1]
    unit = middle_ref[...] * scale
    gain_part = jnp.sum(normed_grad * unit, axis=0, keepdims=True)
    unit_grad = normed_grad * gain_ref[...]
    middle_grad = grad_ref[...].astype(jnp.float32) + scale * (
        unit_grad - unit * jnp.mean(unit_grad * unit, axis=-1, keepdims=True)
    )
    middle_grad_ref[...] = middle_grad
    low = middle_grad.astype(jnp.bfloat16)
    low_ref[...] = low
    grad_t = low.T
    size = weight_ref.shape[1] // 8
    for row in range(0, weight_ref.shape[1], size):
        out = dot_nn(weight_ref[0, row : row + size], grad_t).astype(jnp.bfloat16)
        for i in range(size // HEAD_DIM):
            out_ref[index_ref[row // HEAD_DIM + i], :HEAD_DIM] = out[
                i * HEAD_DIM : (i + 1) * HEAD_DIM
            ]
    coarse = gain_part.astype(jnp.bfloat16)
    fine = (gain_part - coarse.astype(jnp.float32)).astype(jnp.bfloat16)
    wide = gain_part.shape[1] // out_ref.shape[0]
    for head in range(out_ref.shape[0]):
        at = slice(head * wide, (head + 1) * wide)
        row = jnp.concatenate([coarse[:, at], fine[:, at]], axis=1)
        out_ref[head, HEAD_DIM:] = jnp.broadcast_to(row, (EXTRA, tok))


def token_grad(index, sums, middle, scale, gain, output_grad, weight):
    tok, width = middle.shape
    vmem = pl.BlockSpec(memory_space=pltpu.VMEM)
    return pl.pallas_call(
        token_grad_kernel,
        in_specs=[pl.BlockSpec(memory_space=pltpu.SMEM)]
        + [vmem] * 9,
        out_specs=[vmem] * 3,
        out_shape=[
            jax.ShapeDtypeStruct((tok, width), jnp.float32),
            jax.ShapeDtypeStruct((tok, width), jnp.bfloat16),
            pltpu.HBM((HEADS, HEAD_DIM + EXTRA, tok), jnp.bfloat16),
        ],
        compiler_params=pltpu.CompilerParams(vmem_limit_bytes=20 * 2**20),
        cost_estimate=SHORT,
        name="token_grad",
    )(
        index,
        *sums,
        middle,
        scale,
        gain,
        output_grad,
        pltpu.with_memory_space_constraint(weight, pltpu.VMEM),
    )


def feed_wgrad_kernel(gate_ref, up_ref, hidden_ref, tokens_ref, grads_ref, out_ref):
    tokens, grads = tokens_ref[...], grads_ref[...]
    out_ref[0, 0] = dot_nn(gate_ref[...], tokens).astype(jnp.bfloat16)
    out_ref[0, 1] = dot_nn(up_ref[...], tokens).astype(jnp.bfloat16)
    out_ref[0, 2] = dot_nn(hidden_ref[...], grads).astype(jnp.bfloat16)


def feed_wgrads(shards, gate_grad, up_grad, hidden, feed_low, span_grad):
    units, tokens = hidden.shape
    width = feed_low.shape[1]
    block = units // shards
    cuts = 2
    half = width // cuts
    rows = pl.BlockSpec((block, tokens), lambda c, i: (i, 0))
    every = pl.BlockSpec((tokens, half), lambda c, i: (0, c))
    return pl.pallas_call(
        feed_wgrad_kernel,
        grid=(cuts, shards),
        in_specs=[rows] * 3 + [every] * 2,
        out_specs=pl.BlockSpec((1, 3, block, half), lambda c, i: (i, 0, 0, c)),
        out_shape=pltpu.HBM((shards, 3, block, width), jnp.bfloat16),
        compiler_params=pltpu.CompilerParams(vmem_limit_bytes=24 * 2**20),
        cost_estimate=SHORT,
        name="feed_wgrads",
    )(*in_hbm([gate_grad, up_grad, hidden, feed_low, span_grad]))


def output_wgrad_kernel(index_ref, heads_ref, *refs):
    grads, (out_ref, grads_s) = refs[:-2], refs[-2:]
    tok = grads[0].shape[0]
    for slot, ref in enumerate(grads):
        grads_s[pl.ds(pl.multiple_of(index_ref[slot] * tok, tok), tok), :] = ref[...]
    for k in range(heads_ref.shape[0]):
        out_ref[k] = dot_nn(heads_ref[k], grads_s[...]).astype(jnp.bfloat16)


def output_wgrad_parts(index, heads, grads):
    tok, width = grads[0].shape
    vmem = pl.BlockSpec(memory_space=pltpu.VMEM)
    return pl.pallas_call(
        output_wgrad_kernel,
        in_specs=[pl.BlockSpec(memory_space=pltpu.SMEM)] + [vmem] * (1 + len(grads)),
        out_specs=vmem,
        out_shape=jax.ShapeDtypeStruct((heads.shape[0], HEAD_DIM, width), jnp.bfloat16),
        scratch_shapes=[pltpu.VMEM((len(grads) * tok, width), jnp.bfloat16)],
        compiler_params=pltpu.CompilerParams(vmem_limit_bytes=18 * 2**20),
        cost_estimate=SHORT,
        name="output_wgrad",
    )(index, heads, *grads)


def swap_cores(values):
    count = lax.axis_size("seq")
    return lax.ppermute(values, "seq", [(i, i ^ 1) for i in range(count)])


def from_chip(values, step):
    count = lax.axis_size("seq")
    return lax.ppermute(values, "seq", [((i + 2 * step) % count, i) for i in range(count)])


def from_shard(values, flip):
    return lax.ppermute(values, "shard", [(i, i ^ flip) for i in range(4)])


def both_cores(same):
    return [block for one in same for block in (one, swap_cores(one))]


def core_sum(near, other):
    return near.astype(F32) + swap_cores(other.astype(BF16)).astype(F32)


def after(token, values):
    return lax.optimization_barrier((values, token))[0]


def join(token, *values):
    return lax.optimization_barrier((token,) + values)[0]


def first_hops(block):
    return [from_shard(block, 1), from_shard(block, 2)]


def second_hops(first):
    rows = first[0].shape[0] // 2
    return [from_shard(first[0][:rows], 2), from_shard(first[1][rows:], 1)]


def scatter_shard_first(parts):
    rows = parts[3].shape[0] // 2
    low = parts[3].astype(BF16)
    return from_shard(low[:rows], 1), from_shard(low[rows:], 2)


def scatter_shard_last(parts, first):
    rows = parts[3].shape[0] // 2
    top, bottom = first
    one, two = parts[1].astype(F32), parts[2].astype(F32)
    one = jnp.concatenate([one[:rows], one[rows:] + bottom.astype(F32)])
    two = jnp.concatenate([two[:rows] + top.astype(F32), two[rows:]])
    return from_shard(one.astype(BF16), 1), from_shard(two.astype(BF16), 2)


def slot_block(slot, place, half):
    z, core = place // 2, place % 2
    return ((z + slot // 2) % half) * 2 + (core + slot) % 2


def rotate_rows(front, back, cos_t, sin_t):
    return jnp.concatenate([front * cos_t - back * sin_t, back * cos_t + front * sin_t], axis=-2)


def per_device(
    layer_input,
    doc_lengths,
    norm_gain,
    query_weight,
    key_weight,
    value_weight,
    output_weight,
    feed_gain,
    gate_weight,
    up_weight,
    down_weight,
    output_grad,
):
    tok, width = layer_input.shape
    seqs, shards = lax.axis_size("seq"), lax.axis_size("shard")
    shard, seq = lax.axis_index("shard"), lax.axis_index("seq")
    span = tok * seqs
    half_head = HEAD_DIM // 2
    place = jnp.reshape(seq, (1,)).astype(jnp.int32)

    positions = jnp.arange(shards * span, dtype=jnp.int32).reshape(shards, span)
    span_blocks = slot_block(jnp.arange(seqs, dtype=jnp.int32), seq.astype(jnp.int32), seqs // 2)
    bounds = doc_bounds(doc_lengths, positions)
    exponent = -2.0 * jnp.arange(half_head, dtype=jnp.float32) / HEAD_DIM
    inverse = jnp.power(jnp.float32(ROPE_BASE), exponent)
    angles = positions.astype(F32)[:, None, :] * inverse[None, :, None]
    cos_all, sin_all = jnp.cos(angles), jnp.sin(angles)
    cos_own = lax.dynamic_index_in_dim(cos_all, shard, 0, keepdims=False)
    sin_own = lax.dynamic_index_in_dim(sin_all, shard, 0, keepdims=False)

    steps = seqs // 2
    z, core = seq // 2, seq % 2
    shard_at = jnp.reshape(shard, (1,)).astype(jnp.int32)
    gain_row = norm_gain[None, :]
    heads_here = HEADS // seqs
    own_rows = query_weight.shape[0]
    attn_weights = (query_weight, key_weight, value_weight)
    slot = jnp.arange(HEADS, dtype=jnp.int32)

    packed = pack_columns(place, gain_row, attn_weights, seqs)
    point = join(jnp.zeros((), F32), packed)
    from_other = swap_cores(packed[1])
    gate_first = first_hops(after(point, gate_weight))
    col_blocks = []
    for step in range(steps):
        block = jnp.concatenate([packed[0, step], from_other[step]])
        col_blocks.append(from_chip(block, -step) if step else block)
    point = join(point, col_blocks)
    col_block = jnp.concatenate(after(point, col_blocks))
    col_first = first_hops(col_block)
    own_input = after(point, layer_input)
    input_one, input_three = from_chip(own_input, 1), from_chip(own_input, -1)
    point = join(point, col_first, input_one, input_three, gate_first)
    col_far = second_hops(after(point, col_first))
    input_two = from_chip(after(point, input_one), 1)
    input_slots = both_cores([own_input, after(point, input_one)])
    input_last = both_cores([after(point, input_three)])
    gate_far = second_hops(after(point, gate_first))
    point = join(point, col_far, input_two, input_slots, input_last)
    input_slots += both_cores([after(point, input_two)]) + input_last
    rel_blocks = (
        (shard ^ (slot // seqs)) * seqs
        + (z + steps - slot % seqs // 2) % steps * 2
        + (core ^ (slot % 2))
    ).astype(jnp.int32)
    columns = order_blocks([col_block] + col_first + after(point, col_far), rel_blocks, own_rows)
    unit_low = unit_tokens(span_blocks, input_slots)
    qkv = lax.dot_general(
        columns, unit_low, (((0,), (1,)), ((), ())), preferred_element_type=F32
    ).reshape(shards, 3, HEAD_DIM, span)
    turned = rotate_rows(
        qkv[:, :2, :half_head], qkv[:, :2, half_head:], cos_own[None, None], sin_own[None, None]
    )
    qkv_low = jnp.concatenate([turned, qkv[:, 2:]], axis=1).astype(BF16)
    qkv_low = qkv_low.reshape(shards, 3 * HEAD_DIM, span)
    output_own = after(point, output_weight)
    output_one, output_three = from_chip(output_own, 1), from_chip(output_own, -1)
    up_top, up_bottom = up_weight[: up_weight.shape[0] // 2], up_weight[up_weight.shape[0] // 2 :]
    up_first = [
        from_shard(after(point, half), flip) for half in (up_top, up_bottom) for flip in (1, 2)
    ]
    point = join(point, qkv_low, gate_far, output_one, output_three, up_first)

    head_qkv = lax.all_to_all(
        after(point, qkv_low), "shard", split_axis=0, concat_axis=0, tiled=True
    )
    output_two = from_chip(after(point, output_one), 1)
    point = join(point, head_qkv, output_two)
    output_own = jnp.concatenate(after(point, [output_own, output_one, output_two, output_three]))
    output_first = first_hops(output_own)
    output_swapped = [swap_cores(output_own)]
    own_grad = after(point, output_grad)
    grad_one, grad_three = from_chip(own_grad, 1), from_chip(own_grad, -1)
    gain_rows = jnp.pad(feed_gain[None, :], ((0, EXTRA - 1), (0, tok - own_rows)))
    head_out, head_low, out_blocks, lse = attend(
        after(point, head_qkv), gain_rows, tok, shard_at, bounds
    )
    point = join(point, out_blocks, output_first, output_swapped, grad_one, grad_three)
    token_blocks = lax.all_to_all(
        out_blocks, ("shard", "seq"), split_axis=0, concat_axis=0, tiled=True
    )
    output_far = second_hops(after(point, output_first))
    output_swapped += [swap_cores(piece) for piece in after(point, output_first)]
    grad_two = from_chip(after(point, grad_one), 1)
    point = join(point, token_blocks, output_far, output_swapped, grad_two)
    gain_two = token_blocks[:, HEAD_DIM, :own_rows].astype(F32).reshape(1, width)
    output_swapped += [swap_cores(piece) for piece in after(point, output_far)]
    up_far = [from_shard(after(point, up_first[0]), 2), from_shard(after(point, up_first[3]), 1)]
    output_pieces = [output_own] + output_first + output_far + output_swapped
    rel_heads = (
        (shard ^ (slot // steps % shards)) * seqs
        + (z + slot % steps) % steps * 2
        + (core ^ (slot // (HEADS // 2)))
    ).astype(jnp.int32)
    middle, normed_two, scale_two = project(
        rel_heads, after(point, token_blocks), layer_input, gain_two, output_pieces
    )
    point = join(point, normed_two)

    own_tokens = after(point, normed_two)
    tokens_one, tokens_three = from_chip(own_tokens, 1), from_chip(own_tokens, -1)
    down_first = first_hops(after(point, down_weight))
    grad_slots = both_cores(after(point, [output_grad, grad_one, grad_two, grad_three]))
    point = join(point, tokens_one, tokens_three, down_first, grad_slots, up_far)
    tokens_two = from_chip(after(point, tokens_one), 1)
    down_far = second_hops(after(point, down_first))
    feed_slots = both_cores([own_tokens, after(point, tokens_one)])
    first_two = load_weights(
        [
            after(point, [gate_weight, *gate_first, *gate_far]),
            [up_weight, up_first[0], up_first[2], up_first[1], up_first[3], *up_far],
        ]
    )
    output_here = load_weights([after(point, output_pieces)])
    feed_last = both_cores([after(point, tokens_three)])
    point = join(point, tokens_two, down_far, feed_slots, feed_last, first_two, output_here)
    feed_slots += both_cores([after(point, tokens_two)]) + feed_last
    down_here = load_weights([[down_weight, *down_first, *after(point, down_far)]])
    order = (2, 1, 3, 0)

    def feed(step, tokens, whole):
        here = slice(2 * step, 2 * step + 2)
        return feed_blocks(
            order.index(step), seqs, shard_at, tokens, grad_slots[here], first_two, down_here, whole
        )

    parts_two, whole = feed(2, feed_slots[4:6], None)
    sum_two = core_sum(*parts_two).astype(BF16)
    point = join(point, sum_two)
    arrived_two = from_chip(after(point, sum_two), -2)
    parts_one, whole = feed(1, after(point, feed_slots[2:4]), whole)
    parts_three, whole = feed(3, feed_slots[6:8], whole)
    parts_own, whole = feed(0, feed_slots[0:2], whole)
    head_slots = [head_low[0]] + [from_shard(after(point, head_low[k]), k) for k in range(1, 4)]
    point = join(point, arrived_two, parts_one, parts_three, parts_own, head_slots)
    sum_one = core_sum(*after(point, parts_one)).astype(BF16)
    sum_three = core_sum(*after(point, parts_three)).astype(BF16)
    point = join(point, sum_one, sum_three)
    arrived_one = from_chip(after(point, sum_one), -1)
    arrived_three = from_chip(after(point, sum_three), 1)
    sum_own = core_sum(*after(point, parts_own))
    feed_low, span_grad, hidden, gate_grad, up_grad, down_near, down_other = after(point, whole)
    feed_wparts = feed_wgrads(shards, gate_grad, up_grad, hidden, feed_low, span_grad)
    point = join(point, sum_own, feed_wparts, arrived_one, arrived_three)
    middle_grad, attend_grad, head_grad = token_grad(
        rel_heads,
        [sum_own, *after(point, [arrived_one, arrived_two, arrived_three])],
        middle,
        scale_two,
        gain_two,
        output_grad,
        output_here,
    )
    point = join(point, head_grad)

    out_grad_blocks = lax.all_to_all(
        after(point, head_grad), ("shard", "seq"), split_axis=0, concat_axis=0, tiled=True
    )
    feed_wsum = lax.psum_scatter(
        after(point, feed_wparts).reshape(-1, width), "shard", scatter_dimension=0, tiled=True
    ).reshape(3, -1, width)
    own_agrad = after(point, attend_grad)
    agrad_one = from_chip(own_agrad, 1)
    down_all = core_sum(after(point, down_near), down_other).astype(BF16)
    down_sums = [down_all[order.index(step)] for step in range(steps)]
    pair = jnp.concatenate([own_agrad, down_sums[2]])
    point = join(point, out_grad_blocks, agrad_one, pair, down_sums[3])
    both = from_chip(after(point, pair), -1)
    down_three = from_chip(after(point, down_sums[3]), 1)
    back = attend_back(
        head_qkv, lse, head_out, after(point, out_grad_blocks), cos_all, sin_all, tok, bounds
    )
    point = join(point, back, both, down_three)
    agrad_three, down_two = both[:tok], both[tok:]
    span_back = lax.all_to_all(
        after(point, back), "shard", split_axis=0, concat_axis=0, tiled=True
    ).reshape(heads_here * 3 * HEAD_DIM, span)
    agrad_two = from_chip(after(point, agrad_one), 1)
    down_one = from_chip(
        (down_sums[1].astype(F32) + after(point, down_two).astype(F32)).astype(BF16), -1
    )
    agrad_slots = both_cores([after(point, own_agrad), agrad_one, agrad_two, agrad_three])
    out_part = output_wgrad_parts(span_blocks, jnp.stack(head_slots), agrad_slots)
    out_parts = [out_part[k] for k in range(4)]
    out_first = scatter_shard_first(out_parts)
    point = join(point, span_back, down_one, out_first)

    span_back = after(point, span_back)
    cols_part = cols_parts_of(shard_at, span_back, unit_low, shards)
    point = join(point, cols_part)
    cols_parts = [after(point, cols_part)[k] for k in range(4)]
    cols_first = scatter_shard_first(cols_parts)
    unit_near, unit_other = unit_back(span_blocks, after(point, span_back), columns, tok)
    unit_swapped = swap_cores(unit_other)
    point = join(point, unit_near, unit_swapped)
    unit_sums = unit_near + after(point, unit_swapped).astype(F32)
    unit_two = from_chip(unit_sums[2].astype(BF16), -1)
    unit_three = from_chip(unit_sums[3].astype(BF16), 1)
    out_last = scatter_shard_last(out_parts, after(point, out_first))
    layer_output = (
        middle
        + down_sums[0].astype(F32)
        + after(point, down_one).astype(F32)
        + down_three.astype(F32)
    ).astype(BF16)
    gain_rows_back = out_grad_blocks[:, HEAD_DIM].astype(F32)
    gain_two_out = jnp.sum(
        gain_rows_back[:, :own_rows] + gain_rows_back[:, own_rows : 2 * own_rows], axis=0
    )
    point, layer_output, gain_two_out = lax.optimization_barrier(
        (join(point, unit_two, unit_three, cols_first, out_last), layer_output, gain_two_out)
    )
    unit_one = from_chip((unit_sums[1] + after(point, unit_two).astype(F32)).astype(BF16), -1)
    cols_last = scatter_shard_last(cols_parts, after(point, cols_first))
    point = join(point, unit_one, cols_last)
    cols_near, cols_other = spread_columns(
        place, cols_parts[0], *after(point, cols_last), steps
    )
    cols_blocks = pair_columns(cols_near, swap_cores(cols_other))
    point = join(point, cols_blocks)
    cols_same = list(after(point, cols_blocks))
    cols_same = cols_same[:1] + [from_chip(cols_same[step], -step) for step in range(1, steps)]
    out_one, out_two = after(point, out_last)
    output_wgrad = out_parts[0].astype(F32) + out_one.astype(F32) + out_two.astype(F32)
    unit_grad = unit_sums[0] + after(point, unit_one).astype(F32) + unit_three.astype(F32)
    inputs = layer_input.astype(F32)
    scale_one = lax.rsqrt(jnp.mean(inputs * inputs, axis=-1, keepdims=True) + NORM_EPS)
    unit_rows = inputs * scale_one
    input_grad = (
        middle_grad
        + scale_one * (unit_grad - unit_rows * jnp.mean(unit_grad * unit_rows, axis=-1, keepdims=True))
    ).astype(BF16)
    gate_wgrad, up_wgrad, down_wgrad = [
        after(point, feed_wsum)[m].astype(F32) for m in range(3)
    ]
    point, output_wgrad, input_grad, gate_wgrad, up_wgrad, down_wgrad, cols_same = (
        lax.optimization_barrier(
            (
                *(point, output_wgrad, input_grad, gate_wgrad, up_wgrad, down_wgrad),
                cols_same,
            )
        )
    )
    query_wgrad, key_wgrad, value_wgrad, gain_one_out = unpack_columns(
        place, gain_row, attn_weights, after(point, cols_same)
    )
    return (
        layer_output,
        input_grad,
        gain_one_out.reshape(-1),
        query_wgrad,
        key_wgrad,
        value_wgrad,
        output_wgrad,
        gain_two_out,
        gate_wgrad,
        up_wgrad,
        down_wgrad,
    )


def solution(mesh):
    shards, seqs = mesh.shape["shard"], mesh.shape["seq"]
    body = per_device if shards == 4 and shards * seqs == HEADS else per_device_any
    return jax.shard_map(
        body,
        mesh=mesh,
        in_specs=(
            P(("shard", "seq"), None),
            P(),
            P(("shard", "seq")),
            P(("shard", "seq"), None),
            P(("shard", "seq"), None),
            P(("shard", "seq"), None),
            P(("shard", "seq"), None),
            P(("shard", "seq")),
            P(("shard", "seq"), None),
            P(("shard", "seq"), None),
            P(("shard", "seq"), None),
            P(("shard", "seq"), None),
        ),
        out_specs=(
            P(("shard", "seq"), None),
            P(("shard", "seq"), None),
            P(("shard", "seq")),
            P(("shard", "seq"), None),
            P(("shard", "seq"), None),
            P(("shard", "seq"), None),
            P(("shard", "seq"), None),
            P(("shard", "seq")),
            P(("shard", "seq"), None),
            P(("shard", "seq"), None),
            P(("shard", "seq"), None),
        ),
        check_vma=False,
    )
```
